32 devices in a mesh: dp: 4 (over x, core), fsdp: 8 (over z, y).
Axes of the slice: x: 2, y: 2, z: 4, core: 2. Of those that a mesh axis runs over, the one named last changes fastest.
Arguments:
- tokens: bfloat16 [30720, 512], P(('dp', 'fsdp')), may hold values from -6 to 6
- frames: int32 [6144], P(('dp', 'fsdp')), may hold values from 2 to 5, as said below
- norm1_gain: float32 [512], P(('dp', 'fsdp')), may hold values from 0.1 to 1.9
- norm1_bias: float32 [512], P(('dp', 'fsdp')), may hold values from -1.75 to 1.75
- qkv_weight: float32 [786432], P(('dp', 'fsdp')), may hold values from -0.25 to 0.25
- qv_bias: float32 [1024], P(('dp', 'fsdp')), may hold values from -1.75 to 1.75
- out_weight: float32 [262144], P(('dp', 'fsdp')), may hold values from -0.375 to 0.375
- out_bias: float32 [512], P(('dp', 'fsdp')), may hold values from -1.75 to 1.75
- norm2_gain: float32 [512], P(('dp', 'fsdp')), may hold values from 0.1 to 1.9
- norm2_bias: float32 [512], P(('dp', 'fsdp')), may hold values from -1.75 to 1.75
- up_weight: float32 [1048576], P(('dp', 'fsdp')), may hold values from -0.25 to 0.25
- up_bias: float32 [2048], P(('dp', 'fsdp')), may hold values from -1.75 to 1.75
- down_weight: float32 [1048576], P(('dp', 'fsdp')), may hold values from -0.125 to 0.125
- down_bias: float32 [512], P(('dp', 'fsdp')), may hold values from -1.75 to 1.75
- cotangent: bfloat16 [30720, 512], P(('dp', 'fsdp')), may hold values from -6 to 6
Outputs:
- mixed: bfloat16 [30720, 512], P(('dp', 'fsdp'))
- tokens_grad: bfloat16 [30720, 512], P(('dp', 'fsdp'))
- grad_norm1_gain: float32 [512], P(('dp', 'fsdp'))
- grad_norm1_bias: float32 [512], P(('dp', 'fsdp'))
- grad_qkv_weight: float32 [786432], P(('dp', 'fsdp'))
- grad_qv_bias: float32 [1024], P(('dp', 'fsdp'))
- grad_out_weight: float32 [262144], P(('dp', 'fsdp'))
- grad_out_bias: float32 [512], P(('dp', 'fsdp'))
- grad_norm2_gain: float32 [512], P(('dp', 'fsdp'))
- grad_norm2_bias: float32 [512], P(('dp', 'fsdp'))
- grad_up_weight: float32 [1048576], P(('dp', 'fsdp'))
- grad_up_bias: float32 [2048], P(('dp', 'fsdp'))
- grad_down_weight: float32 [1048576], P(('dp', 'fsdp'))
- grad_down_bias: float32 [512], P(('dp', 'fsdp'))
The draws below stay inside these ranges and needn't reach their ends.
Inputs may be any that keep to these rules, and one draw needn't show every extreme that they name: Each sequence has 2, 3 or 5 valid frames; both ends occur.
All inputs are finite; a program needn't handle non-finite values.
Results may differ from the reference program's by a relative error of at most 0.011.
Values may be sent and summed in bfloat16 or wider, within the bound.
A program may use at most 128 MiB of HBM per device.

```python
import math
import jax
import jax.numpy as jnp
from jax import lax

D = 512
HEADS = 8
HEAD_DIM = 64
FF = 2048
FRAMES = 5
SEQ_DEV = 192
SEQS = 6144
TOKENS = 30720


def draw_frames(key, part):
    key = jax.random.fold_in(key, 11)
    chosen = jax.random.randint(key, (SEQS,), 0, 3)
    levels = jnp.array([2, 3, 5], dtype=jnp.int32)
    lengths = levels[chosen]
    places = jnp.arange(SEQS, dtype=jnp.int32)
    lengths = jnp.where(places % 7 == 0, 5, lengths)
    return jnp.where(places % 7 == 3, 2, lengths).astype(jnp.int32)


def block_levels(rng, shape, cuts, least, top_value):
    factor_of, own = 1.0, jax.random.fold_in(rng, 6)
    for axis_at, blocks in cuts:
        steps = jnp.exp(jax.random.uniform(jax.random.fold_in(own, axis_at), (blocks,), jnp.float32, least / len(cuts), top_value / len(cuts)))
        factor_of = factor_of * jnp.repeat(steps, shape[axis_at] // blocks).reshape([-1 if axis == axis_at else 1 for axis in range(len(shape))])
    return factor_of


def gaussian(stream_key, shape, scale, most, shards=(), held_as=jnp.bfloat16):
    level = block_levels(stream_key, shape, shards, -0.22, 0.18) if shards else 1.0
    values = jax.random.normal(stream_key, shape, jnp.float32) * scale * level
    return jnp.minimum(jnp.maximum(values, -most), most).astype(held_as)


def setup_inputs(seed: int = 0) -> dict:
    keys = jax.random.split(jax.random.key(seed), 16)
    return {
        "tokens": gaussian(keys[0], (TOKENS, D), 1.0, 6.0, ((0, 32),)),
        "frames": draw_frames(jax.random.fold_in(keys[15], 71), 0),
        "norm1_gain": jnp.clip(1.0 + 0.18 * jax.random.normal(keys[2], (D,), jnp.float32), 0.1, 1.9),
        "norm1_bias": gaussian(keys[3], (D,), 0.3, 1.75, ((0, 32),), jnp.float32),
        "qkv_weight": gaussian(keys[4], (3 * D * D,), D ** -0.5, 0.25, ((0, 32),), jnp.float32),
        "qv_bias": gaussian(keys[5], (2 * D,), 0.3, 1.75, ((0, 32),), jnp.float32),
        "out_weight": gaussian(keys[6], (D * D,), (D // 2) ** -0.5, 0.375, ((0, 32),), jnp.float32),
        "out_bias": gaussian(keys[7], (D,), 0.3, 1.75, ((0, 32),), jnp.float32),
        "norm2_gain": jnp.clip(1.0 + 0.18 * jax.random.normal(keys[8], (D,), jnp.float32), 0.1, 1.9),
        "norm2_bias": gaussian(keys[9], (D,), 0.3, 1.75, ((0, 32),), jnp.float32),
        "up_weight": gaussian(keys[10], (D * FF,), D ** -0.5, 0.25, ((0, 32),), jnp.float32),
        "up_bias": gaussian(keys[11], (FF,), 0.3, 1.75, ((0, 32),), jnp.float32),
        "down_weight": gaussian(keys[12], (FF * D,), FF ** -0.5, 0.125, ((0, 32),), jnp.float32),
        "down_bias": gaussian(keys[13], (D,), 0.3, 1.75, ((0, 32),), jnp.float32),
        "cotangent": gaussian(keys[14], (TOKENS, D), 1.0, 6.0, ((0, 32),)),
    }


@jax.custom_vjp
def low(v):
    return lax.optimization_barrier(v.astype(jnp.bfloat16)).astype(jnp.float32)

@jax.custom_vjp
def low_back(v):
    return v

def low_keep(v):
    return (low(v), None)

def low_pass(kept, grad):
    return (grad,)

def back_keep(v):
    return (v, None)

def back_low(kept, grad):
    return (low(grad),)
low.defvjp(low_keep, low_pass)
low_back.defvjp(back_keep, back_low)
EPSILON = 1e-05
PRECISE = lax.Precision.HIGHEST

def normalize(values, gain, shift):
    centered = values - lax.optimization_barrier(jnp.mean(values, axis=-1, keepdims=True))
    variance = lax.optimization_barrier(jnp.mean(centered * centered, axis=-1, keepdims=True))
    return centered * lax.rsqrt(variance + EPSILON) * gain + shift

def attend(queries, keys_in, values_in, frames):
    span = queries.shape[1]
    scale = 1.0 / math.sqrt(queries.shape[3])
    scores = jnp.einsum('sthe,suhe->shtu', queries, keys_in, precision=PRECISE) * scale
    slots = jnp.arange(span, dtype=jnp.int32)
    causal = slots[None, :] <= slots[:, None]
    living = slots[None, :] < frames[:, None]
    allowed = causal[None, None, :, :] & living[:, None, None, :]
    scores = jnp.where(allowed, scores, -1e+30)
    highest = lax.optimization_barrier(jnp.max(scores, axis=-1, keepdims=True))
    weights = jnp.exp(scores - highest)
    weights = weights / lax.optimization_barrier(jnp.sum(weights, axis=-1, keepdims=True))
    return jnp.einsum('shtu,suhe->sthe', weights, values_in, precision=PRECISE)

def layer(states, frames, params):
    norm1_gain, norm1_bias, qkv_weight, qv_bias, out_weight, out_bias, norm2_gain, norm2_bias, up_weight, up_bias, down_weight, down_bias = params
    count = states.shape[0]
    seqs_here = count // FRAMES
    first = low(normalize(states, low(norm1_gain), low(norm1_bias)))
    pair_bias = low(qv_bias)
    bias_full = jnp.concatenate([pair_bias[:D], jnp.zeros((D,), jnp.float32), pair_bias[D:]])
    mixed_in = jnp.dot(first, low(qkv_weight).reshape(D, 3 * D), precision=PRECISE) + bias_full
    packed = low(low_back(mixed_in)).reshape(seqs_here, FRAMES, 3, HEADS, HEAD_DIM)
    context = attend(packed[:, :, 0], packed[:, :, 1], packed[:, :, 2], frames).reshape(count, D)
    branch = low_back(jnp.dot(low(context), low(out_weight).reshape(D, D), precision=PRECISE) + low(out_bias))
    middle = states + branch
    second = low(normalize(middle, low(norm2_gain), low(norm2_bias)))
    lifted = low_back(jnp.dot(second, low(up_weight).reshape(D, FF), precision=PRECISE) + low(up_bias))
    activated = low(jax.nn.gelu(lifted))
    return middle + low_back(jnp.dot(activated, low(down_weight).reshape(FF, D), precision=PRECISE) + low(down_bias))

def reference(tokens, frames, norm1_gain, norm1_bias, qkv_weight, qv_bias, out_weight, out_bias, norm2_gain, norm2_bias, up_weight, up_bias, down_weight, down_bias, cotangent):
    params = (norm1_gain, norm1_bias, qkv_weight, qv_bias, out_weight, out_bias, norm2_gain, norm2_bias, up_weight, up_bias, down_weight, down_bias)
    block_rows = SEQ_DEV * FRAMES
    blocks = tokens.shape[0] // block_rows
    states_all = tokens.astype(jnp.float32).reshape(blocks, block_rows, D)
    frames_all = frames.reshape(blocks, SEQ_DEV)
    cotan_all = cotangent.astype(jnp.float32).reshape(blocks, block_rows, D)

    def advance(totals, item):
        states_blk, frames_blk, cotan_blk = item
        result, pullback = jax.vjp(lambda states, weights: layer(states, frames_blk, weights), states_blk, params)
        states_grad, param_grads = pullback(cotan_blk)
        totals = jax.tree.map(lambda left, right: left + right, totals, param_grads)
        return (totals, (result.astype(jnp.bfloat16), states_grad.astype(jnp.bfloat16)))
    starting = jax.tree.map(jnp.zeros_like, params)
    grads, (results, input_grads) = lax.scan(advance, starting, (states_all, frames_all, cotan_all))
    return (results.reshape(TOKENS, D), input_grads.reshape(TOKENS, D), grads[0], grads[1], grads[2], grads[3], grads[4], grads[5], grads[6], grads[7], grads[8], grads[9], grads[10], grads[11])
```

```python
import math

import jax
import jax.numpy as jnp
from jax import lax
from jax.experimental import pallas as pl
from jax.experimental.pallas import tpu as pltpu
from jax.sharding import PartitionSpec as P

D = 512
HEADS = 8
HEAD_DIM = 64
FF = 2048
FRAMES = 5
EPSILON = 1e-05
PAIRS = [(t, u) for t in range(FRAMES) for u in range(t + 1)]

F32 = jnp.float32
BF16 = jnp.bfloat16
MESH = pl.DeviceIdType.MESH

SM, QKV, OUT, UP, DOWN = range(5)
ROWS = (8, 16, 16, 16, 64)
COLS = (128, 3 * D, D, FF, D)
KEPT = (F32, BF16, BF16, BF16, BF16)
SMALL = (16, 16, 32, 16, 16, 16, 64, 16)
GAIN1, BIAS1, QVB, OUTB, GAIN2, BIAS2, UPB, DOWNB = range(8)

TILE = 64
CHUNK = 32


def dot(left, right):
    return lax.dot_general(left, right, (((1,), (0,)), ((), ())), preferred_element_type=F32)


def dot_nt(left, right):
    return lax.dot_general(left, right, (((1,), (1,)), ((), ())), preferred_element_type=F32)


def dot_tn(left, right):
    return lax.dot_general(left, right, (((0,), (0,)), ((), ())), preferred_element_type=F32)


def iota(shape, dim):
    return lax.broadcasted_iota(jnp.int32, shape, dim)


def fold(values):
    rows, cols = values.shape
    return jnp.sum(values.reshape(rows // 8, 8, cols), axis=0)


def split_two(values):
    high = values.astype(BF16)
    return high, (values - high.astype(F32)).astype(BF16)


def layer_kernel(split, count, *refs):
    refs = list(refs)

    def take(n):
        head = refs[:n]
        del refs[:n]
        return head

    tok_hbm, cot_hbm, frames_ref = take(3)
    small_in = take(8)
    shard_in = [None] + take(4)
    mixed_hbm, tgrad_hbm = take(2)
    small_out = take(8)
    shard_out = [None] + take(4)
    whole = take(5)
    acc = take(5)
    sib_out, sib_in = take(5), take(5)
    two_out, two_in = take(5), take(5)
    one_out, one_in = take(5), take(5)
    zed_out, zed_in = take(5), take(5)
    (tokb, cotb, stage, xt, dm, xh1, xh2, rs1, rs2, a1, a2, qkv, prob, ctx, x1, act, slope, wide, dao, dpre) = take(20)
    (vec16, vecqv, vecup, biasq, living, pick, pick_t, gs16, gsqv, gsup, sums) = take(11)
    (gsend, grecv, rsend, rrecv, io_sem) = take(5)

    seqs = count // FRAMES
    dp = lax.axis_index("dp")
    fs = lax.axis_index("fsdp")
    x, c = dp // 2, dp % 2
    group, rest = fs // split, fs % split
    z, y = group // 2, group % 2

    def device(x_, c_, z_, y_):
        return (x_ * 2 + c_, (z_ * 2 + y_) * split + rest)

    first = x + c * (y - x)
    second = y + c * (x - y)

    def to_xy(f_, s_):
        return f_ + c * (s_ - f_), s_ + c * (f_ - s_)

    def peer(f_, s_):
        x_, y_ = to_xy(f_, s_)
        return device(x_, c, z, y_)

    sibling = device(x, 1 - c, z, y)
    first_dev = peer(1 - first, second)
    second_dev = peer(first, 1 - second)
    zeds = (z + 1 - 2 * (z % 2), (z + 2) % 4, 3 - z)
    zed_dev = [device(x, c, zk, y) for zk in zeds]

    tok_copy = pltpu.make_async_copy(tok_hbm, tokb, io_sem.at[0])
    cot_copy = pltpu.make_async_copy(cot_hbm, cotb, io_sem.at[1])
    tok_copy.start()
    cot_copy.start()
    barrier = pltpu.get_barrier_semaphore()
    for dev in [sibling, first_dev, second_dev] + zed_dev:
        pl.semaphore_signal(barrier, inc=1, device_id=dev, device_id_type=MESH)

    def shard(w, f_, s_, z_):
        x_, y_ = to_xy(f_, s_)
        return whole[w].at[x_, c, z_, y_]

    def line(w, f_, s_):
        x_, y_ = to_xy(f_, s_)
        return whole[w].at[x_, c, :, y_]

    def gcopy(w, k, ref, dev):
        return pltpu.make_async_remote_copy(
            src_ref=ref, dst_ref=ref, send_sem=gsend.at[w, k], recv_sem=grecv.at[w, k], device_id=dev, device_id_type=MESH
        )

    def own_shard(w):
        if w == SM:
            whole[w][x, c, z, y] = jnp.zeros((8, 128), F32)
            for p, n in enumerate(SMALL):
                whole[w][x, c, z, y, p : p + 1, 0:n] = small_in[p][...].astype(BF16).astype(F32)
        else:
            step = COLS[w] // 128
            for k in range(step):
                part = shard_in[w][pl.ds(k, ROWS[w], stride=step), :]
                whole[w][x, c, z, y, :, k * 128 : (k + 1) * 128] = part.astype(BF16)

    def g_start(w):
        ref = shard(w, first, second, z)
        for k in range(3):
            gcopy(w, k, ref, zed_dev[k]).start()
        gcopy(w, 3 + z, ref, first_dev).start()
        gcopy(w, 7 + z, ref, second_dev).start()

    def g_z(w):
        for k in range(3):
            ref = shard(w, first, second, zeds[k])
            gcopy(w, k, ref, zed_dev[k]).wait_recv()
            gcopy(w, 3 + zeds[k], ref, first_dev).start()
            gcopy(w, 7 + zeds[k], ref, second_dev).start()
        gcopy(w, 15, line(w, first, second), sibling).start()

    def g_f(w):
        for k in range(4):
            ref = shard(w, 1 - first, second, k)
            gcopy(w, 3 + k, ref, first_dev).wait_recv()
            gcopy(w, 11 + k, ref, second_dev).start()
        gcopy(w, 16, line(w, 1 - first, second), sibling).start()

    def g_s(w):
        for k in range(4):
            gcopy(w, 7 + k, shard(w, first, 1 - second, k), second_dev).wait_recv()
        gcopy(w, 17, line(w, first, 1 - second), sibling).start()
        for k in range(4):
            gcopy(w, 11 + k, shard(w, 1 - first, 1 - second, k), second_dev).wait_recv()
        gcopy(w, 18, line(w, 1 - first, 1 - second), sibling).start()

    def g_sib(w):
        for k, (flip_f, flip_s) in enumerate(((0, 0), (0, 1), (1, 0), (1, 1))):
            x_, y_ = to_xy(first + flip_f * (1 - 2 * first), second + flip_s * (1 - 2 * second))
            gcopy(w, 15 + k, whole[w].at[x_, 1 - c, :, y_], sibling).wait_recv()

    def g_end(w):
        own = shard(w, first, second, z)
        for k in range(15):
            gcopy(w, k, own, sibling).wait_send()
        for k in range(15, 19):
            gcopy(w, k, line(w, first, second), sibling).wait_send()

    def place(f_, s_, z_):
        x_, y_ = to_xy(f_, s_)
        return x_ * 8 + z_ * 2 + y_

    def rcopy(w, k, src, dst, dev):
        return pltpu.make_async_remote_copy(
            src_ref=src, dst_ref=dst, send_sem=rsend.at[w, k], recv_sem=rrecv.at[w, k], device_id=dev, device_id_type=MESH
        )

    def sib_copy(w, h):
        return rcopy(w, h, sib_out[w].at[pl.ds(8 * h, 8)], sib_in[w].at[pl.ds(8 * h, 8)], sibling)

    def two_copy(w, k):
        return rcopy(w, 2 + k, two_out[w].at[k], two_in[w].at[k], second_dev)

    def one_copy(w, k):
        return rcopy(w, 10 + k, one_out[w].at[k], one_in[w].at[k], first_dev)

    def zed_copy(w, k):
        return rcopy(w, 14 + k, zed_out[w].at[k], zed_in[w].at[k], zed_dev[k])

    def r_1(w):
        for h in range(2):
            sib_copy(w, h).wait_recv()

        def step(k, carry):
            j = place(k // 4, 1 - second, k % 4)
            two_out[w][k] = (acc[w][j] + sib_in[w][j].astype(F32)).astype(KEPT[w])
            two_copy(w, k).start()
            return carry

        lax.fori_loop(0, 8, step, 0)

    def r_2(w):
        def step(k, carry):
            j = place(1 - first, second, k)
            slot = (1 - first) * 4 + k
            two_copy(w, slot).wait_recv()
            total = acc[w][j] + sib_in[w][j].astype(F32) + two_in[w][slot].astype(F32)
            one_out[w][k] = total.astype(KEPT[w])
            one_copy(w, k).start()
            return carry

        lax.fori_loop(0, 4, step, 0)

    def r_3(w):
        for k in range(3):
            j = place(first, second, zeds[k])
            slot = first * 4 + zeds[k]
            two_copy(w, slot).wait_recv()
            one_copy(w, zeds[k]).wait_recv()
            total = acc[w][j] + sib_in[w][j].astype(F32) + two_in[w][slot].astype(F32) + one_in[w][zeds[k]].astype(F32)
            zed_out[w][k] = total.astype(KEPT[w])
            zed_copy(w, k).start()

    def r_4(w):
        j = place(first, second, z)
        slot = first * 4 + z
        two_copy(w, slot).wait_recv()
        one_copy(w, z).wait_recv()
        total = acc[w][j] + sib_in[w][j].astype(F32) + two_in[w][slot].astype(F32) + one_in[w][z].astype(F32)
        for k in range(3):
            zed_copy(w, k).wait_recv()
            total = total + zed_in[w][k].astype(F32)
        if w == SM:
            for p, n in enumerate(SMALL):
                small_out[p][...] = total[p : p + 1, 0:n]
        else:
            step = COLS[w] // 128
            for k in range(step):
                shard_out[w][pl.ds(k, ROWS[w], stride=step), :] = total[:, k * 128 : (k + 1) * 128]

    def r_end(w):
        for h in range(2):
            sib_copy(w, h).wait_send()
        for k in range(8):
            two_copy(w, k).wait_send()
        for k in range(4):
            one_copy(w, k).wait_send()
        for k in range(3):
            zed_copy(w, k).wait_send()

    tiles = count // TILE
    per_frame = seqs // TILE

    def tile_rows(i):
        return pl.ds(pl.multiple_of(i * TILE, TILE), TILE)

    def strided(i):
        return pl.ds(i // per_frame + FRAMES * TILE * (i % per_frame), TILE, stride=FRAMES)

    def loop(n, body):
        def step(i, carry):
            body(i)
            return carry

        lax.fori_loop(0, n, step, 0)

    def widen(src):
        def body(i):
            for h in range(4):
                stage[h, tile_rows(i), :] = src[tile_rows(i), h * 128 : (h + 1) * 128].astype(F32)

        loop(tiles, body)

    def narrow(dst):
        def body(i):
            for h in range(4):
                dst[tile_rows(i), h * 128 : (h + 1) * 128] = stage[h, tile_rows(i), :].astype(BF16)

        loop(tiles, body)

    def center(values):
        mean = jnp.mean(values, axis=-1, keepdims=True)
        centered = values - mean
        root = lax.rsqrt(jnp.mean(centered * centered, axis=-1, keepdims=True) + EPSILON)
        return centered * root, root

    def constants():
        lane, row = iota((D, 128), 1), iota((D, 128), 0)
        pick[...] = jnp.where((row // HEAD_DIM == lane % HEADS) & (lane < 2 * HEADS), 1.0, 0.0).astype(BF16)
        lane, row = iota((128, D), 1), iota((128, D), 0)
        pick_t[...] = jnp.where((lane // HEAD_DIM == row % HEADS) & (row < 2 * HEADS), 1.0, 0.0).astype(BF16)
        same = iota((seqs, seqs), 0) == iota((seqs, seqs), 1)
        wide_frames = jnp.broadcast_to(frames_ref[...].astype(F32), (seqs, seqs))
        spread = jnp.where(same, wide_frames, 0.0).astype(BF16)
        living[...] = dot(spread, jnp.ones((seqs, 128), BF16))
        gs16[...] = jnp.zeros_like(gs16)
        gsqv[...] = jnp.zeros_like(gsqv)
        gsup[...] = jnp.zeros_like(gsup)

    def first_norm():
        widen(tokb)

        def body(i):
            values = jnp.concatenate([stage[h, strided(i), :] for h in range(4)], axis=1)
            xt[tile_rows(i), :] = values.astype(BF16)
            hat, root = center(values)
            xh1[tile_rows(i), :] = hat
            rs1[tile_rows(i), :] = jnp.broadcast_to(root, (TILE, 128))

        loop(tiles, body)

    def cotangent_in():
        widen(cotb)

        def body(i):
            values = jnp.concatenate([stage[h, strided(i), :] for h in range(4)], axis=1)
            dm[tile_rows(i), :] = values.astype(BF16)
            gs16[DOWNB : DOWNB + 1, :] += jnp.sum(fold(values), axis=0, keepdims=True)

        loop(tiles, body)

    def small_vectors():
        raw = whole[SM][...].reshape(256, 128).astype(BF16)
        for n, dst in ((16, vec16), (32, vecqv), (64, vecup)):
            width = 32 * n
            for at in range(0, width, 512):
                near = iota((128, 512), 0) == (iota((128, 512), 1) + at) % n
                spread = dot(raw, jnp.where(near, 1.0, 0.0).astype(BF16))
                mine = iota((256, 512), 0) // 8 == (iota((256, 512), 1) + at) // n
                dst[:, at : at + 512] = jnp.sum(jnp.where(mine, spread, 0.0).reshape(32, 8, 512), axis=0)
        biasq[:, 0:D] = vecqv[QVB : QVB + 1, 0:D]
        biasq[:, D : 2 * D] = jnp.zeros((1, D), F32)
        biasq[:, 2 * D : 3 * D] = vecqv[QVB : QVB + 1, D : 2 * D]

    def small_grads():
        for n, src in ((16, gs16), (32, gsqv), (64, gsup)):
            width = 32 * n
            for at in range(0, width, 512):
                mine = iota((256, 512), 0) // 8 == (iota((256, 512), 1) + at) // n
                values = jnp.broadcast_to(src[:, at : at + 512][None], (32, 8, 512)).reshape(256, 512)
                high, low = split_two(jnp.where(mine, values, 0.0))
                near = jnp.where(iota((128, 512), 0) == (iota((128, 512), 1) + at) % n, 1.0, 0.0).astype(BF16)
                part = dot_nt(high, near) + dot_nt(low, near)
                total = part if n == 16 and at == 0 else total + part
        sums[...] = total.reshape(2, 2, 8, 8, 128)
        for h in range(2):
            acc[SM][8 * h : 8 * h + 8] = sums[h, c]
            sib_out[SM][8 * h : 8 * h + 8] = sums[h, 1 - c]
            sib_copy(SM, h).start()

    def first_affine():
        gain, bias = vec16[GAIN1 : GAIN1 + 1, :], vec16[BIAS1 : BIAS1 + 1, :]

        def body(i):
            a1[tile_rows(i), :] = (xh1[tile_rows(i), :] * gain + bias).astype(BF16)

        loop(tiles, body)

    def cols(n, width):
        return pl.ds(pl.multiple_of(n * width, width), width)

    def matrix_cols(w, n, width):
        part = whole[w][:, :, :, :, :, cols(n, width)]
        return part.reshape(32 * ROWS[w], width)

    def matrix(w):
        return whole[w][...].reshape(32 * ROWS[w], COLS[w])

    def project_in():
        def body(n):
            r = dot(a1[...], matrix_cols(QKV, n, 256)) + biasq[:, cols(n, 256)]
            qkv[:, cols(n, 256)] = r.astype(BF16)

        loop(6, body)

    def frame_rows(t, i):
        return pl.ds(pl.multiple_of(t * seqs + i * CHUNK, CHUNK), CHUNK)

    def heads_of(i, part):
        return [qkv[frame_rows(t, i), part * D : (part + 1) * D].astype(F32) for t in range(FRAMES)]

    def spread_heads(parts):
        lanes = iota((CHUNK, 128), 1)
        mixed_parts = []
        for part in parts:
            high, low = split_two(part)
            mixed_parts.append(jnp.where(lanes < HEADS, high.astype(F32), low.astype(F32)).astype(BF16))
        return dot(jnp.concatenate(mixed_parts, axis=0), pick_t[...])

    def rows_of(values, k):
        return values[k * CHUNK : (k + 1) * CHUNK]

    def attention(i):
        q, k_, v = heads_of(i, 0), heads_of(i, 1), heads_of(i, 2)
        halves = [split_two(q[t] * k_[u]) for t, u in PAIRS]
        high = jnp.concatenate([h for h, _ in halves], axis=0)
        low = jnp.concatenate([l for _, l in halves], axis=0)
        scores = (dot(high, pick[...]) + dot(low, pick[...])) * (1.0 / math.sqrt(HEAD_DIM))
        live = living[pl.ds(pl.multiple_of(i * CHUNK, CHUNK), CHUNK), :]
        weights = []
        for t in range(FRAMES):
            row = [rows_of(scores, PAIRS.index((t, u))) for u in range(t + 1)]
            row = [jnp.where(u < live, part, -1e30) for u, part in enumerate(row)]
            top = row[0]
            for part in row[1:]:
                top = jnp.maximum(top, part)
            row = [jnp.exp(part - top) for part in row]
            total = row[0]
            for part in row[1:]:
                total = total + part
            weights += [part / total for part in row]
        for k, part in enumerate(weights):
            prob[k, pl.ds(pl.multiple_of(i * CHUNK, CHUNK), CHUNK), :] = part
        spread = spread_heads(weights)
        for t in range(FRAMES):
            total = rows_of(spread, PAIRS.index((t, 0))) * v[0]
            for u in range(1, t + 1):
                total = total + rows_of(spread, PAIRS.index((t, u))) * v[u]
            ctx[frame_rows(t, i), :] = total.astype(BF16)

    def attention_back(i):
        v = heads_of(i, 2)
        g = [wide[frame_rows(t, i), :] for t in range(FRAMES)]
        products = jnp.concatenate([(g[t] * v[u]).astype(BF16) for t, u in PAIRS], axis=0)
        slopes = dot(products, pick[...])
        weights = [prob[k, pl.ds(pl.multiple_of(i * CHUNK, CHUNK), CHUNK), :] for k in range(len(PAIRS))]
        scaled = []
        for t in range(FRAMES):
            ks = [PAIRS.index((t, u)) for u in range(t + 1)]
            mean = weights[ks[0]] * rows_of(slopes, ks[0])
            for k in ks[1:]:
                mean = mean + weights[k] * rows_of(slopes, k)
            scaled += [weights[k] * (rows_of(slopes, k) - mean) * (1.0 / math.sqrt(HEAD_DIM)) for k in ks]
        spread_p = spread_heads(weights)
        for u in range(FRAMES):
            total = None
            for t in range(u, FRAMES):
                part = rows_of(spread_p, PAIRS.index((t, u))) * g[t]
                total = part if total is None else total + part
            low = total.astype(BF16)
            dpre[frame_rows(u, i), 2 * D :] = low
            gsqv[QVB : QVB + 1, D:] += jnp.sum(fold(low.astype(F32)), axis=0, keepdims=True)
        q, k_ = heads_of(i, 0), heads_of(i, 1)
        spread_s = spread_heads(scaled)
        for t in range(FRAMES):
            total = None
            for u in range(t + 1):
                part = rows_of(spread_s, PAIRS.index((t, u))) * k_[u]
                total = part if total is None else total + part
            low = total.astype(BF16)
            dpre[frame_rows(t, i), :D] = low
            gsqv[QVB : QVB + 1, :D] += jnp.sum(fold(low.astype(F32)), axis=0, keepdims=True)
        for u in range(FRAMES):
            total = None
            for t in range(u, FRAMES):
                part = rows_of(spread_s, PAIRS.index((t, u))) * q[t]
                total = part if total is None else total + part
            dpre[frame_rows(u, i), D : 2 * D] = total.astype(BF16)

    def project_out():
        bias = vec16[OUTB : OUTB + 1, :]
        for n in range(2):
            at = slice(n * 256, (n + 1) * 256)
            r = dot(ctx[...], whole[OUT][:, :, :, :, :, at].reshape(D, 256))
            x1[:, at] = xt[:, at].astype(F32) + r + bias[:, at]

    def second_norm():
        gain, bias = vec16[GAIN2 : GAIN2 + 1, :], vec16[BIAS2 : BIAS2 + 1, :]

        def body(i):
            hat, root = center(x1[tile_rows(i), :])
            xh2[tile_rows(i), :] = hat
            rs2[tile_rows(i), :] = jnp.broadcast_to(root, (TILE, 128))
            a2[tile_rows(i), :] = (hat * gain + bias).astype(BF16)

        loop(tiles, body)

    def feed_up():
        k0 = math.sqrt(2.0 / math.pi)
        k1 = k0 * 0.044715

        def body(n):
            f = dot(a2[...], matrix_cols(UP, n, 256)) + vecup[UPB : UPB + 1, cols(n, 256)]
            square = f * f
            half = 0.5 + 0.5 * jnp.tanh(f * (k0 + k1 * square))
            act[:, cols(n, 256)] = (f * half).astype(BF16)
            grow = half + (f * (half - half * half)) * (2.0 * k0 + 6.0 * k1 * square)
            slope[:, cols(n, 256)] = grow.astype(BF16)

        loop(8, body)

    def feed_down():
        bias = vec16[DOWNB : DOWNB + 1, :]
        for n in range(2):
            at = slice(n * 256, (n + 1) * 256)
            r = dot(act[...], whole[DOWN][:, :, :, :, :, at].reshape(FF, 256))
            r = r + x1[:, at] + bias[:, at]
            for t in range(FRAMES):
                stage_rows = pl.ds(t, seqs, stride=FRAMES)
                for h in range(2):
                    stage[2 * n + h, stage_rows, :] = r[t * seqs : (t + 1) * seqs, h * 128 : (h + 1) * 128]
        narrow(tokb)

    def weight_grad(w, left, right, h_rows, width):
        def lhs(core):
            parts = [left[:, pl.ds(pl.multiple_of(h * 2 * h_rows + core * h_rows, 128), h_rows)] for h in range(2)]
            return jnp.concatenate(parts, axis=1)

        def theirs(n):
            r = dot_tn(lhs(1 - c), right[:, cols(n, width)])
            sib_out[w][:, :, cols(n, width)] = r.reshape(16, ROWS[w], width).astype(BF16)

        def ours(n):
            r = dot_tn(lhs(c), right[:, cols(n, width)])
            acc[w][:, :, cols(n, width)] = r.reshape(16, ROWS[w], width)

        loop(COLS[w] // width, theirs)
        for h in range(2):
            sib_copy(w, h).start()
        loop(COLS[w] // width, ours)

    def down_grad():
        def theirs(h):
            left = act[:, pl.ds(pl.multiple_of(h * 1024 + (1 - c) * 512, 512), 512)]
            r = dot_tn(left, dm[...])
            sib_out[DOWN][pl.ds(8 * h, 8)] = r.reshape(8, 64, D).astype(BF16)
            sib_copy(DOWN, h).start()

        def ours(h):
            left = act[:, pl.ds(pl.multiple_of(h * 1024 + c * 512, 512), 512)]
            r = dot_tn(left, dm[...])
            acc[DOWN][pl.ds(8 * h, 8)] = r.reshape(8, 64, D)

        loop(2, theirs)
        loop(2, ours)

    def feed_back():
        def body(n):
            part = whole[DOWN][n // 4, (n // 2) % 2, pl.ds(2 * (n % 2), 2)].reshape(256, D)
            low = (dot_nt(dm[...], part) * slope[:, cols(n, 256)].astype(F32)).astype(BF16)
            slope[:, cols(n, 256)] = low
            gsup[UPB : UPB + 1, cols(n, 256)] = jnp.sum(fold(low.astype(F32)), axis=0, keepdims=True)

        loop(8, body)

    def back_to(left, w):
        for h in range(2):
            part = whole[w][h].reshape(256, COLS[w])
            wide[:, h * 256 : (h + 1) * 256] = dot_nt(left[...], part)

    def norm_back(grads, hat, root, gain, gain_at, bias_at):
        gs16[gain_at : gain_at + 1, :] += jnp.sum(fold(grads * hat), axis=0, keepdims=True)
        gs16[bias_at : bias_at + 1, :] += jnp.sum(fold(grads), axis=0, keepdims=True)
        scaled = grads * gain
        mean = jnp.mean(scaled, axis=-1, keepdims=True)
        along = jnp.mean(scaled * hat, axis=-1, keepdims=True)
        return (scaled - mean - hat * along) * root

    def second_back():
        gain = vec16[GAIN2 : GAIN2 + 1, :]

        def body(i):
            at = tile_rows(i)
            part = norm_back(wide[at, :], xh2[at, :], rs2[at, 0:1], gain, GAIN2, BIAS2)
            total = dm[at, :].astype(F32) + part
            x1[at, :] = total
            low = total.astype(BF16)
            dao[at, :] = low
            gs16[OUTB : OUTB + 1, :] += jnp.sum(fold(low.astype(F32)), axis=0, keepdims=True)

        loop(tiles, body)

    def first_back():
        gain = vec16[GAIN1 : GAIN1 + 1, :]

        def body(i):
            at = tile_rows(i)
            part = norm_back(wide[at, :], xh1[at, :], rs1[at, 0:1], gain, GAIN1, BIAS1)
            stage_part = x1[at, :] + part
            for h in range(4):
                stage[h, strided(i), :] = stage_part[:, h * 128 : (h + 1) * 128]

        loop(tiles, body)
        narrow(cotb)

    for w in (SM, QKV, OUT, UP, DOWN):
        own_shard(w)
    pl.semaphore_wait(barrier, 6)
    for w in (SM, QKV, OUT, UP, DOWN):
        g_start(w)
    constants()
    tok_copy.wait()
    first_norm()
    cot_copy.wait()
    cotangent_in()
    for w in (SM, QKV, OUT, UP, DOWN):
        g_z(w)
    for w in (SM, QKV):
        g_f(w)
    for w in (SM, QKV):
        g_s(w)
    g_f(OUT)
    g_f(UP)
    g_sib(SM)
    small_vectors()
    first_affine()
    g_sib(QKV)
    project_in()
    g_s(OUT)
    g_f(DOWN)
    loop(seqs // CHUNK, attention)
    g_s(UP)
    g_sib(OUT)
    project_out()
    second_norm()
    g_sib(UP)
    feed_up()
    g_s(DOWN)
    down_grad()
    g_sib(DOWN)
    feed_down()
    mixed_copy = pltpu.make_async_copy(tokb, mixed_hbm, io_sem.at[2])
    mixed_copy.start()
    r_1(DOWN)
    feed_back()
    r_2(DOWN)
    weight_grad(UP, a2, slope, 128, 512)
    r_3(DOWN)
    back_to(slope, UP)
    r_1(UP)
    second_back()
    r_4(DOWN)
    r_2(UP)
    weight_grad(OUT, ctx, dao, 128, 512)
    back_to(dao, OUT)
    r_1(OUT)
    r_3(UP)
    loop(seqs // CHUNK, attention_back)
    r_2(OUT)
    r_4(UP)
    weight_grad(QKV, a1, dpre, 128, 512)
    r_3(OUT)
    back_to(dpre, QKV)
    r_1(QKV)
    first_back()
    tgrad_copy = pltpu.make_async_copy(cotb, tgrad_hbm, io_sem.at[3])
    tgrad_copy.start()
    small_grads()
    r_4(OUT)
    r_2(QKV)
    r_1(SM)
    r_2(SM)
    r_3(QKV)
    r_3(SM)
    r_4(QKV)
    r_4(SM)
    for w in (SM, QKV, OUT, UP, DOWN):
        g_end(w)
        r_end(w)
    mixed_copy.wait()
    tgrad_copy.wait()


def call_layer(split, tokens, frames, small, shards, cotangent):
    count = tokens.shape[0]
    any_spec = pl.BlockSpec(memory_space=pl.ANY)
    vmem = pl.BlockSpec(memory_space=pltpu.VMEM)

    def kept(n, dtype=None):
        return [pltpu.VMEM((n, r, k), dtype or t) for r, k, t in zip(ROWS, COLS, KEPT)]

    scratch = [pltpu.VMEM((2, 2, 4, 2, r, k), t) for r, k, t in zip(ROWS, COLS, KEPT)]
    scratch += kept(16, F32)
    for n in (16, 8, 4, 3):
        scratch += kept(n) + kept(n)
    rows_bf = lambda k: pltpu.VMEM((count, k), BF16)
    rows_f = lambda k: pltpu.VMEM((count, k), F32)
    scratch += [
        rows_bf(D), rows_bf(D), pltpu.VMEM((4, count, 128), F32), rows_bf(D), rows_bf(D),
        rows_f(D), rows_f(D), rows_f(128), rows_f(128),
        rows_bf(D), rows_bf(D), rows_bf(3 * D),
        pltpu.VMEM((len(PAIRS), count // FRAMES, 128), F32),
        rows_bf(D), rows_f(D), rows_bf(FF), rows_bf(FF),
        rows_f(D), rows_bf(D), rows_bf(3 * D),
    ]
    scratch += [
        pltpu.VMEM((8, 512), F32), pltpu.VMEM((8, 1024), F32), pltpu.VMEM((8, 2048), F32), pltpu.VMEM((1, 3 * D), F32),
        pltpu.VMEM((count // FRAMES, 128), F32), pltpu.VMEM((D, 128), BF16), pltpu.VMEM((128, D), BF16),
        pltpu.VMEM((8, 512), F32), pltpu.VMEM((8, 1024), F32), pltpu.VMEM((8, 2048), F32),
        pltpu.VMEM((2, 2, 8, 8, 128), F32),
    ]
    scratch += [pltpu.SemaphoreType.DMA((5, 19))] * 2 + [pltpu.SemaphoreType.DMA((5, 17))] * 2
    scratch += [pltpu.SemaphoreType.DMA((4,))]
    out_shape = [jax.ShapeDtypeStruct(tokens.shape, BF16)] * 2
    out_shape += [jax.ShapeDtypeStruct((1, n), F32) for n in SMALL]
    out_shape += [jax.ShapeDtypeStruct(s.shape, F32) for s in shards]

    def body(*refs):
        layer_kernel(split, count, *refs)

    return pl.pallas_call(
        body,
        name="layer",
        out_shape=out_shape,
        in_specs=[any_spec, any_spec] + [vmem] * 13,
        out_specs=[any_spec, any_spec] + [vmem] * 12,
        scratch_shapes=scratch,
        compiler_params=pltpu.CompilerParams(
            collective_id=0, has_side_effects=True, vmem_limit_bytes=63 << 20
        ),
        cost_estimate=pl.CostEstimate(
            flops=2 * 3 * count * (3 * D * D + D * D + 2 * D * FF), bytes_accessed=1 << 23, transcendentals=count * FF
        ),
    )(tokens, cotangent, frames, *small, *shards)


def local(split, tokens, frames, g1, b1, wqkv, bqv, wo, bo, g2, b2, w1, b1f, w2, b2f, cotangent):
    spot = lax.axis_index("fsdp") // split

    def block(values):
        if split == 1:
            return values
        n = values.shape[0]
        every = lax.all_gather(values, "fsdp", axis=0, tiled=True)
        return lax.dynamic_slice(every, (spot * split * n,), (split * n,))

    def owned(values):
        if split == 1:
            return values
        n = values.shape[0]
        spread = lax.dynamic_update_slice(jnp.zeros((8 * n,), F32), values, (spot * n,))
        return lax.psum_scatter(spread, "fsdp", scatter_dimension=0, tiled=True)

    small = [block(v).reshape(1, -1) for v in (g1, b1, bqv, bo, g2, b2, b1f, b2f)]
    shards = [block(v).reshape(-1, 128) for v in (wqkv, wo, w1, w2)]
    outs = call_layer(split, tokens, frames.reshape(1, -1), small, shards, cotangent)
    mixed, tokens_grad = outs[:2]
    dg1, db1, dbqv, dbo, dg2, db2, db1f, db2f = [owned(v.reshape(-1)) for v in outs[2:10]]
    dwqkv, dwo, dw1, dw2 = [owned(v.reshape(-1)) for v in outs[10:]]
    return (mixed, tokens_grad, dg1, db1, dwqkv, dbqv, dwo, dbo, dg2, db2, dw1, db1f, dw2, db2f)


def solution(mesh):
    split = mesh.shape["fsdp"] // 8
    flat, rows = P(("dp", "fsdp")), P(("dp", "fsdp"), None)

    def body(*args):
        return local(split, *args)

    return jax.shard_map(
        body,
        mesh=mesh,
        in_specs=(rows,) + (flat,) * 13 + (rows,),
        out_specs=(rows, rows) + (flat,) * 12,
        check_vma=False,
    )
```

```python
import math

import jax
import jax.numpy as jnp
from jax import lax
from jax.experimental import pallas as pl
from jax.experimental.pallas import tpu as pltpu
from jax.sharding import PartitionSpec as P

D = 512
HEADS = 8
HEAD_DIM = 64
FF = 2048
FRAMES = 5
EPSILON = 1e-05
PAIRS = [(t, u) for t in range(FRAMES) for u in range(t + 1)]

F32 = jnp.float32
BF16 = jnp.bfloat16
MESH = pl.DeviceIdType.MESH

SM, QA, QB, OUT, UP, DOWN = range(6)
ROWS = (8, 16, 16, 16, 16, 64)
COLS = (128, 3 * D // 2, 3 * D // 2, D, FF, D)
KEPT = (F32, BF16, BF16, BF16, BF16, BF16)
DIRECT = (SM, QA, QB)
HALF = D // 2
GROUP = HEADS // 2
QKV_ARG, OUT_ARG, UP_ARG, DOWN_ARG = range(4)
ARG = (None, QKV_ARG, QKV_ARG, OUT_ARG, UP_ARG, DOWN_ARG)
PACKED = (192, 64, 256, 256)
PACK = (0, 192, 256, 512)
PACK_SMALL, PACK_ALL = 768, 776
SMALL = (16, 16, 32, 16, 16, 16, 64, 16)
GAIN1, BIAS1, QVB, OUTB, GAIN2, BIAS2, UPB, DOWNB = range(8)

TILE = 192
CHUNK = 64


def dot(left, right):
    return lax.dot_general(left, right, (((1,), (0,)), ((), ())), preferred_element_type=F32)


def dot_nt(left, right):
    return lax.dot_general(left, right, (((1,), (1,)), ((), ())), preferred_element_type=F32)


def dot_tn(left, right):
    return lax.dot_general(left, right, (((0,), (0,)), ((), ())), preferred_element_type=F32)


def iota(shape, dim):
    return lax.broadcasted_iota(jnp.int32, shape, dim)


def fold(values):
    rows, cols = values.shape
    return jnp.sum(values.reshape(rows // 8, 8, cols), axis=0)


def split_two(values):
    high = values.astype(BF16)
    return high, (values - high.astype(F32)).astype(BF16)


def layer_kernel(split, count, *refs):
    refs = list(refs)

    def take(n):
        head = refs[:n]
        del refs[:n]
        return head

    tok_hbm, cot_hbm, frames_ref = take(3)
    small_in = take(8)
    shard_hbm = take(4)
    mixed_hbm, tgrad_hbm, grads_hbm = take(3)
    shard_in = take(4)
    (grads,) = take(1)
    whole = take(6)
    acc = take(6)
    sib_out, sib_in = take(6), take(6)
    two_out, two_in = take(6), take(6)
    one_out, one_in = take(6), take(6)
    zed_out, zed_in = take(6), take(6)
    (tokb, cotb, stage, xt, dm, xh1, xh2, rs1, rs2, a1, a2, qkv, prob, ctx, x1, act, slope, wide, dao, dpre, turned) = take(21)
    (vec16, vecqv, vecup, biasq, living, pick, pick_t, gs16, gsqv, gsup, sums) = take(11)
    (gsend, grecv, rsend, rrecv, io_sem) = take(5)

    seqs = count // FRAMES
    dp = lax.axis_index("dp")
    fs = lax.axis_index("fsdp")
    x, c = dp // 2, dp % 2
    group, rest = fs // split, fs % split
    z, y = group // 2, group % 2

    def device(x_, c_, z_, y_):
        return (x_ * 2 + c_, (z_ * 2 + y_) * split + rest)

    first = x + c * (y - x)
    second = y + c * (x - y)

    def to_xy(f_, s_):
        return f_ + c * (s_ - f_), s_ + c * (f_ - s_)

    def peer(f_, s_):
        x_, y_ = to_xy(f_, s_)
        return device(x_, c, z, y_)

    sibling = device(x, 1 - c, z, y)
    first_dev = peer(1 - first, second)
    second_dev = peer(first, 1 - second)
    across_dev = peer(1 - first, 1 - second)
    zeds = (z + 1 - 2 * (z % 2), (z + 2) % 4, 3 - z)
    zed_dev = [device(x, c, zk, y) for zk in zeds]

    tok_copy = pltpu.make_async_copy(tok_hbm, tokb, io_sem.at[0])
    cot_copy = pltpu.make_async_copy(cot_hbm, cotb, io_sem.at[1])
    shard_copy = [pltpu.make_async_copy(shard_hbm[k], shard_in[k], io_sem.at[4 + k]) for k in range(4)]
    for copy in shard_copy:
        copy.start()
    tok_copy.start()
    cot_copy.start()
    barrier = pltpu.get_barrier_semaphore()
    for dev in [sibling, first_dev, second_dev, across_dev] + zed_dev:
        pl.semaphore_signal(barrier, inc=1, device_id=dev, device_id_type=MESH)

    def shard(w, f_, s_, z_):
        x_, y_ = to_xy(f_, s_)
        return whole[w].at[x_, c, z_, y_]

    def line(w, f_, s_):
        x_, y_ = to_xy(f_, s_)
        return whole[w].at[x_, c, :, y_]

    def gcopy(w, sent, got, ref, dev):
        return pltpu.make_async_remote_copy(
            src_ref=ref, dst_ref=ref, send_sem=gsend.at[w, sent], recv_sem=grecv.at[w, got], device_id=dev, device_id_type=MESH
        )

    def cols_of(w):
        if w in (QA, QB):
            return [(4 * p + 2 * (w - QA) + b, 2 * p + b) for p in range(3) for b in range(2)]
        return [(k, k) for k in range(COLS[w] // 128)]

    def own_shard(w):
        if w == SM:
            whole[w][x, c, z, y] = jnp.zeros((8, 128), F32)
            for p, n in enumerate(SMALL):
                whole[w][x, c, z, y, p : p + 1, 0:n] = small_in[p][...].astype(BF16).astype(F32)
        else:
            if w != QB:
                shard_copy[ARG[w]].wait()
            step = PACKED[ARG[w]] // ROWS[w]
            for k, to in cols_of(w):
                part = shard_in[ARG[w]][pl.ds(k, ROWS[w], stride=step), :]
                whole[w][x, c, z, y, :, to * 128 : (to + 1) * 128] = part.astype(BF16)

    def hand_on(w, ref, spot):
        if w in DIRECT:
            gcopy(w, 1, 3, ref, first_dev).start()
            gcopy(w, 2, 7, ref, second_dev).start()
            gcopy(w, 3, 8, ref, across_dev).start()
        else:
            gcopy(w, 1, 3 + spot, ref, first_dev).start()
            gcopy(w, 2, 7, ref, second_dev).start()

    def to_sibling(w, f_, s_):
        gcopy(w, 4, 9, line(w, f_, s_), sibling).start()

    def g_start(w):
        ref = shard(w, first, second, z)
        for k in range(3):
            gcopy(w, 0, k, ref, zed_dev[k]).start()
        hand_on(w, ref, z)

    def g_z(w):
        for k in range(3):
            ref = shard(w, first, second, zeds[k])
            gcopy(w, 0, k, ref, zed_dev[k]).wait_recv()
            hand_on(w, ref, zeds[k])
        to_sibling(w, first, second)

    def g_f(w):
        for k in range(4):
            ref = shard(w, 1 - first, second, k)
            gcopy(w, 1, 3 + k, ref, first_dev).wait_recv()
            gcopy(w, 2, 8, ref, second_dev).start()
        to_sibling(w, 1 - first, second)

    def g_s(w):
        if w in DIRECT:
            gcopy(w, 1, 3, line(w, 1 - first, second), first_dev).wait_recv()
            to_sibling(w, 1 - first, second)
        gcopy(w, 2, 7, line(w, first, 1 - second), second_dev).wait_recv()
        to_sibling(w, first, 1 - second)
        gcopy(w, 2, 8, line(w, 1 - first, 1 - second), second_dev).wait_recv()
        to_sibling(w, 1 - first, 1 - second)

    def g_sib(w):
        ref = whole[w].at[:, 1 - c]
        gcopy(w, 4, 9, ref, sibling).wait_recv()

    def g_end(w):
        gcopy(w, 0, 0, zed_out[w], sibling).wait_send()
        four = line(w, first, second)
        gcopy(w, 1, 3, four, sibling).wait_send()
        if w in DIRECT:
            gcopy(w, 2, 7, four, sibling).wait_send()
            gcopy(w, 3, 8, four, sibling).wait_send()
        else:
            gcopy(w, 2, 7, two_out[w], sibling).wait_send()
        gcopy(w, 4, 9, sib_out[w], sibling).wait_send()

    def loop(n, body, start=0):
        def step(i, carry):
            body(i)
            return carry

        lax.fori_loop(start, n, step, 0)

    def place(f_, s_, z_):
        x_, y_ = to_xy(f_, s_)
        return x_ * 8 + z_ * 2 + y_

    def rcopy(w, sent, got, src, dst, dev):
        return pltpu.make_async_remote_copy(
            src_ref=src, dst_ref=dst, send_sem=rsend.at[w, sent], recv_sem=rrecv.at[w, got], device_id=dev, device_id_type=MESH
        )

    def sib_copy(w, at, n):
        return rcopy(w, 0, 0, sib_out[w].at[pl.ds(at, n)], sib_in[w].at[pl.ds(at, n)], sibling)

    def two_copy(w, k, got):
        return rcopy(w, 1, got, two_out[w].at[k], two_in[w].at[k], second_dev)

    def one_copy(w, k):
        return rcopy(w, 2, 6 + k, one_out[w].at[k], one_in[w].at[k], first_dev)

    def zed_copy(w, k):
        return rcopy(w, 3, 10, zed_out[w].at[k], zed_in[w].at[k], zed_dev[k])

    def r_1(w):
        sib_copy(w, 0, 16).wait_recv()

        def step(k, got):
            j = place(k // 4, 1 - second, k % 4)
            two_out[w][k] = (acc[w][j] + sib_in[w][j].astype(F32)).astype(KEPT[w])
            two_copy(w, k, got).start()

        loop(4, lambda i: step(4 * (1 - first) + i, 1 + i))
        loop(4, lambda i: step(4 * first + i, 5))

    def r_2(w):
        def step(i):
            k = (z + 1 + i) % 4
            j = place(1 - first, second, k)
            slot = (1 - first) * 4 + k
            two_copy(w, slot, 1 + k).wait_recv()
            total = acc[w][j] + sib_in[w][j].astype(F32) + two_in[w][slot].astype(F32)
            one_out[w][k] = total.astype(KEPT[w])
            one_copy(w, k).start()

        loop(4, step)

    def r_3(w):
        line_in = two_in[w].at[pl.ds(4 * first, 4)]
        rcopy(w, 1, 5, line_in, line_in, second_dev).wait_recv()
        for k in range(3):
            j = place(first, second, zeds[k])
            slot = first * 4 + zeds[k]
            one_copy(w, zeds[k]).wait_recv()
            total = acc[w][j] + sib_in[w][j].astype(F32) + two_in[w][slot].astype(F32) + one_in[w][zeds[k]].astype(F32)
            zed_out[w][k] = total.astype(KEPT[w])
            zed_copy(w, k).start()

    def grad_copy(at, rows, k):
        return pltpu.make_async_copy(grads.at[pl.ds(at, rows)], grads_hbm.at[pl.ds(at, rows)], io_sem.at[8 + k])

    def arg_copy(k):
        return grad_copy(PACK[k], PACKED[k], k)

    small_copy = grad_copy(PACK_SMALL, 8, 4)

    def r_4(w):
        j = place(first, second, z)
        slot = first * 4 + z
        one_copy(w, z).wait_recv()
        total = acc[w][j] + sib_in[w][j].astype(F32) + two_in[w][slot].astype(F32) + one_in[w][z].astype(F32)
        rcopy(w, 3, 10, zed_in[w], zed_in[w], sibling).wait_recv()
        for k in range(3):
            total = total + zed_in[w][k].astype(F32)
        if w == SM:
            grads[PACK_SMALL:PACK_ALL, :] = total
            small_copy.start()
        else:
            step = PACKED[ARG[w]] // ROWS[w]
            for k, at in cols_of(w):
                grads[pl.ds(PACK[ARG[w]] + k, ROWS[w], stride=step), :] = total[:, at * 128 : (at + 1) * 128]

    def r_end(w):
        sib_copy(w, 0, 16).wait_send()
        rcopy(w, 1, 5, two_out[w], two_in[w], sibling).wait_send()
        rcopy(w, 2, 6, one_out[w], one_in[w], sibling).wait_send()
        rcopy(w, 3, 10, zed_out[w], zed_in[w], sibling).wait_send()

    tiles = count // TILE
    per_frame = seqs // TILE

    def tile_rows(i):
        return pl.ds(pl.multiple_of(i * TILE, TILE), TILE)

    def strided(i):
        return pl.ds(i // per_frame + FRAMES * TILE * (i % per_frame), TILE, stride=FRAMES)

    def widen(src):
        def body(i):
            for h in range(4):
                stage[h, tile_rows(i), :] = src[tile_rows(i), h * 128 : (h + 1) * 128].astype(F32)

        loop(tiles, body)

    def narrow(dst):
        def body(i):
            for h in range(4):
                dst[tile_rows(i), h * 128 : (h + 1) * 128] = stage[h, tile_rows(i), :].astype(BF16)

        loop(tiles, body)

    def center(values):
        mean = jnp.mean(values, axis=-1, keepdims=True)
        centered = values - mean
        root = lax.rsqrt(jnp.mean(centered * centered, axis=-1, keepdims=True) + EPSILON)
        return centered * root, root

    def constants():
        lane, row = iota((HALF, 128), 1), iota((HALF, 128), 0)
        pick[...] = jnp.where((row // HEAD_DIM == lane % GROUP) & (lane < 2 * GROUP), 1.0, 0.0).astype(BF16)
        lane, row = iota((128, HALF), 1), iota((128, HALF), 0)
        pick_t[...] = jnp.where((lane // HEAD_DIM == row % GROUP) & (row < 2 * GROUP), 1.0, 0.0).astype(BF16)
        same = iota((seqs, seqs), 0) == iota((seqs, seqs), 1)
        wide_frames = jnp.broadcast_to(frames_ref[...].astype(F32), (seqs, seqs))
        spread = jnp.where(same, wide_frames, 0.0).astype(BF16)
        living[...] = dot(spread, jnp.ones((seqs, 128), BF16))
        gs16[...] = jnp.zeros_like(gs16)
        gsqv[...] = jnp.zeros_like(gsqv)
        gsup[...] = jnp.zeros_like(gsup)

    def first_norm():
        widen(tokb)

        def body(i):
            values = jnp.concatenate([stage[h, strided(i), :] for h in range(4)], axis=1)
            xt[tile_rows(i), :] = values.astype(BF16)
            hat, root = center(values)
            xh1[tile_rows(i), :] = hat
            rs1[tile_rows(i), :] = jnp.broadcast_to(root, (TILE, 128))

        loop(tiles, body)

    def cotangent_in():
        widen(cotb)

        def body(i):
            values = jnp.concatenate([stage[h, strided(i), :] for h in range(4)], axis=1)
            dm[tile_rows(i), :] = values.astype(BF16)
            gs16[DOWNB : DOWNB + 1, :] += jnp.sum(fold(values), axis=0, keepdims=True)

        loop(tiles, body)

    def small_vectors():
        raw = whole[SM][...].reshape(256, 128).astype(BF16)
        for n, dst in ((16, vec16), (32, vecqv), (64, vecup)):
            width = 32 * n
            for at in range(0, width, 512):
                near = iota((128, 512), 0) == (iota((128, 512), 1) + at) % n
                spread = dot(raw, jnp.where(near, 1.0, 0.0).astype(BF16))
                mine = iota((256, 512), 0) // 8 == (iota((256, 512), 1) + at) // n
                dst[:, at : at + 512] = jnp.sum(jnp.where(mine, spread, 0.0).reshape(32, 8, 512), axis=0)
        biasq[...] = jnp.zeros_like(biasq)
        for h in range(2):
            for part in range(2):
                at = 3 * HALF * h + 2 * HALF * part
                biasq[:, at : at + HALF] = vecqv[QVB : QVB + 1, part * D + h * HALF : part * D + (h + 1) * HALF]

    def small_grads():
        for n, src in ((16, gs16), (32, gsqv), (64, gsup)):
            width = 32 * n
            for at in range(0, width, 512):
                mine = iota((256, 512), 0) // 8 == (iota((256, 512), 1) + at) // n
                values = jnp.broadcast_to(src[:, at : at + 512][None], (32, 8, 512)).reshape(256, 512)
                high, low = split_two(jnp.where(mine, values, 0.0))
                near = jnp.where(iota((128, 512), 0) == (iota((128, 512), 1) + at) % n, 1.0, 0.0).astype(BF16)
                part = dot_nt(high, near) + dot_nt(low, near)
                total = part if n == 16 and at == 0 else total + part
        sums[...] = total.reshape(2, 2, 8, 8, 128)
        for h in range(2):
            acc[SM][8 * h : 8 * h + 8] = sums[h, c]
            sib_out[SM][8 * h : 8 * h + 8] = sums[h, 1 - c]
            sib_copy(SM, 8 * h, 8).start()

    def first_affine():
        gain, bias = vec16[GAIN1 : GAIN1 + 1, :], vec16[BIAS1 : BIAS1 + 1, :]

        def body(i):
            a1[tile_rows(i), :] = (xh1[tile_rows(i), :] * gain + bias).astype(BF16)

        loop(tiles, body)

    def cols(n, width):
        return pl.ds(pl.multiple_of(n * width, width), width)

    def matrix_cols(w, n, width):
        part = whole[w][:, :, :, :, :, cols(n, width)]
        return part.reshape(32 * ROWS[w], width)

    def matrix(w):
        return whole[w][...].reshape(32 * ROWS[w], COLS[w])

    def project_in(h):
        def body(n):
            at = cols(n + 3 * h, HALF)
            r = dot(a1[...], matrix_cols(QA + h, n, HALF)) + biasq[:, at]
            qkv[:, at] = r.astype(BF16)

        loop(3, body)

    def frame_rows(t, i):
        return pl.ds(pl.multiple_of(t * seqs + i * CHUNK, CHUNK), CHUNK)

    def heads_of(h, i, part):
        at = (3 * h + part) * HALF
        return [qkv[frame_rows(t, i), at : at + HALF].astype(F32) for t in range(FRAMES)]

    def spread_heads(parts):
        lanes = iota((CHUNK, 128), 1)
        mixed_parts = []
        for part in parts:
            high, low = split_two(part)
            mixed_parts.append(jnp.where(lanes < GROUP, high.astype(F32), low.astype(F32)).astype(BF16))
        return dot(jnp.concatenate(mixed_parts, axis=0), pick_t[...])

    def rows_of(values, k):
        return values[k * CHUNK : (k + 1) * CHUNK]

    def attention(h, i):
        q, k_, v = heads_of(h, i, 0), heads_of(h, i, 1), heads_of(h, i, 2)
        halves = [split_two(q[t] * k_[u]) for t, u in PAIRS]
        high = jnp.concatenate([h for h, _ in halves], axis=0)
        low = jnp.concatenate([l for _, l in halves], axis=0)
        scores = (dot(high, pick[...]) + dot(low, pick[...])) * (1.0 / math.sqrt(HEAD_DIM))
        live = living[pl.ds(pl.multiple_of(i * CHUNK, CHUNK), CHUNK), :]
        weights = []
        for t in range(FRAMES):
            row = [rows_of(scores, PAIRS.index((t, u))) for u in range(t + 1)]
            row = [jnp.where(u < live, part, -1e30) for u, part in enumerate(row)]
            top = row[0]
            for part in row[1:]:
                top = jnp.maximum(top, part)
            row = [jnp.exp(part - top) for part in row]
            total = row[0]
            for part in row[1:]:
                total = total + part
            weights += [part / total for part in row]
        for k, part in enumerate(weights):
            prob[h, k, pl.ds(pl.multiple_of(i * CHUNK, CHUNK), CHUNK), :] = part
        spread = spread_heads(weights)
        for t in range(FRAMES):
            total = rows_of(spread, PAIRS.index((t, 0))) * v[0]
            for u in range(1, t + 1):
                total = total + rows_of(spread, PAIRS.index((t, u))) * v[u]
            ctx[frame_rows(t, i), h * HALF : (h + 1) * HALF] = total.astype(BF16)

    def attention_back(h, i):
        v = heads_of(h, i, 2)
        g = [wide[frame_rows(t, i), h * HALF : (h + 1) * HALF] for t in range(FRAMES)]
        base = 3 * HALF * h
        products = jnp.concatenate([(g[t] * v[u]).astype(BF16) for t, u in PAIRS], axis=0)
        slopes = dot(products, pick[...])
        weights = [prob[h, k, pl.ds(pl.multiple_of(i * CHUNK, CHUNK), CHUNK), :] for k in range(len(PAIRS))]
        scaled = []
        for t in range(FRAMES):
            ks = [PAIRS.index((t, u)) for u in range(t + 1)]
            mean = weights[ks[0]] * rows_of(slopes, ks[0])
            for k in ks[1:]:
                mean = mean + weights[k] * rows_of(slopes, k)
            scaled += [weights[k] * (rows_of(slopes, k) - mean) * (1.0 / math.sqrt(HEAD_DIM)) for k in ks]
        spread_p = spread_heads(weights)
        for u in range(FRAMES):
            total = None
            for t in range(u, FRAMES):
                part = rows_of(spread_p, PAIRS.index((t, u))) * g[t]
                total = part if total is None else total + part
            low = total.astype(BF16)
            dpre[frame_rows(u, i), base + 2 * HALF : base + 3 * HALF] = low
            gsqv[QVB : QVB + 1, D + h * HALF : D + (h + 1) * HALF] += jnp.sum(fold(low.astype(F32)), axis=0, keepdims=True)
        q, k_ = heads_of(h, i, 0), heads_of(h, i, 1)
        spread_s = spread_heads(scaled)
        for t in range(FRAMES):
            total = None
            for u in range(t + 1):
                part = rows_of(spread_s, PAIRS.index((t, u))) * k_[u]
                total = part if total is None else total + part
            low = total.astype(BF16)
            dpre[frame_rows(t, i), base : base + HALF] = low
            gsqv[QVB : QVB + 1, h * HALF : (h + 1) * HALF] += jnp.sum(fold(low.astype(F32)), axis=0, keepdims=True)
        for u in range(FRAMES):
            total = None
            for t in range(u, FRAMES):
                part = rows_of(spread_s, PAIRS.index((t, u))) * q[t]
                total = part if total is None else total + part
            dpre[frame_rows(u, i), base + HALF : base + 2 * HALF] = total.astype(BF16)

    def project_out():
        bias = vec16[OUTB : OUTB + 1, :]
        for n in range(2):
            at = slice(n * 256, (n + 1) * 256)
            r = dot(ctx[...], whole[OUT][:, :, :, :, :, at].reshape(D, 256))
            x1[:, at] = xt[:, at].astype(F32) + r + bias[:, at]

    def second_norm(start, stop):
        gain, bias = vec16[GAIN2 : GAIN2 + 1, :], vec16[BIAS2 : BIAS2 + 1, :]

        def body(i):
            hat, root = center(x1[tile_rows(i), :])
            xh2[tile_rows(i), :] = hat
            rs2[tile_rows(i), :] = jnp.broadcast_to(root, (TILE, 128))
            a2[tile_rows(i), :] = (hat * gain + bias).astype(BF16)

        loop(stop, body, start)

    def feed_up(start, stop):
        k0 = math.sqrt(2.0 / math.pi)
        k1 = k0 * 0.044715

        def body(n):
            f = dot(a2[...], matrix_cols(UP, n, 256)) + vecup[UPB : UPB + 1, cols(n, 256)]
            square = f * f
            half = 0.5 + 0.5 * jnp.tanh(f * (k0 + k1 * square))
            act[:, cols(n, 256)] = (f * half).astype(BF16)
            grow = half + (f * (half - half * half)) * (2.0 * k0 + 6.0 * k1 * square)
            slope[:, cols(n, 256)] = grow.astype(BF16)

        loop(stop, body, start)

    def feed_down(n):
        bias = vec16[DOWNB : DOWNB + 1, :]
        at = slice(n * 256, (n + 1) * 256)
        r = dot(act[...], whole[DOWN][:, :, :, :, :, at].reshape(FF, 256))
        r = r + x1[:, at] + bias[:, at]
        for t in range(FRAMES):
            for h in range(2):
                stage[2 * n + h, pl.ds(t, seqs, stride=FRAMES), :] = r[t * seqs : (t + 1) * seqs, h * 128 : (h + 1) * 128]

    def turn(left, core):
        parts = [left[:, pl.ds(pl.multiple_of(h * 256 + core * 128, 128), 128)] for h in range(2)]
        turned[...] = jnp.transpose(jnp.concatenate(parts, axis=1))

    def grad_theirs(w, left, right, base, width):
        turn(left, 1 - c)

        def body(n):
            r = dot(turned[...], right[:, cols(n + base, width)])
            sib_out[w][:, :, cols(n, width)] = r.reshape(16, ROWS[w], width).astype(BF16)

        loop(COLS[w] // width, body)
        sib_copy(w, 0, 16).start()

    def grad_ours(w, left, right, base, width):
        turn(left, c)

        def body(n):
            r = dot(turned[...], right[:, cols(n + base, width)])
            acc[w][:, :, cols(n, width)] = r.reshape(16, ROWS[w], width)

        loop(COLS[w] // width, body)

    def down_theirs(h):
        left = act[:, pl.ds(pl.multiple_of(h * 1024 + (1 - c) * 512, 512), 512)]
        r = dot_tn(left, dm[...])
        sib_out[DOWN][8 * h : 8 * h + 8] = r.reshape(8, 64, D).astype(BF16)
        sib_copy(DOWN, 8 * h, 8).start()

    def down_ours(h):
        left = act[:, pl.ds(pl.multiple_of(h * 1024 + c * 512, 512), 512)]
        acc[DOWN][8 * h : 8 * h + 8] = dot_tn(left, dm[...]).reshape(8, 64, D)

    def feed_back(start, stop):
        def body(n):
            part = whole[DOWN][n // 4, (n // 2) % 2, pl.ds(2 * (n % 2), 2)].reshape(256, D)
            low = (dot_nt(dm[...], part) * slope[:, cols(n, 256)].astype(F32)).astype(BF16)
            slope[:, cols(n, 256)] = low
            gsup[UPB : UPB + 1, cols(n, 256)] = jnp.sum(fold(low.astype(F32)), axis=0, keepdims=True)

        loop(stop, body, start)

    def back_to(left, w, h):
        wide[:, h * 256 : (h + 1) * 256] = dot_nt(left[...], whole[w][h].reshape(256, COLS[w]))

    def back_in(h):
        r = dot_nt(dpre[:, : 3 * HALF], whole[QA][h].reshape(256, 3 * HALF))
        r = r + dot_nt(dpre[:, 3 * HALF :], whole[QB][h].reshape(256, 3 * HALF))
        wide[:, h * 256 : (h + 1) * 256] = r

    def norm_back(grads, hat, root, gain, gain_at, bias_at):
        gs16[gain_at : gain_at + 1, :] += jnp.sum(fold(grads * hat), axis=0, keepdims=True)
        gs16[bias_at : bias_at + 1, :] += jnp.sum(fold(grads), axis=0, keepdims=True)
        scaled = grads * gain
        mean = jnp.mean(scaled, axis=-1, keepdims=True)
        along = jnp.mean(scaled * hat, axis=-1, keepdims=True)
        return (scaled - mean - hat * along) * root

    def second_back(start, stop):
        gain = vec16[GAIN2 : GAIN2 + 1, :]

        def body(i):
            at = tile_rows(i)
            part = norm_back(wide[at, :], xh2[at, :], rs2[at, 0:1], gain, GAIN2, BIAS2)
            total = dm[at, :].astype(F32) + part
            xh2[at, :] = total
            low = total.astype(BF16)
            dao[at, :] = low
            gs16[OUTB : OUTB + 1, :] += jnp.sum(fold(low.astype(F32)), axis=0, keepdims=True)

        loop(stop, body, start)

    def first_back():
        gain = vec16[GAIN1 : GAIN1 + 1, :]

        def body(i):
            at = tile_rows(i)
            part = norm_back(wide[at, :], xh1[at, :], rs1[at, 0:1], gain, GAIN1, BIAS1)
            stage_part = xh2[at, :] + part
            for h in range(4):
                stage[h, strided(i), :] = stage_part[:, h * 128 : (h + 1) * 128]

        loop(tiles, body)
        narrow(cotb)

    own_shard(SM)
    own_shard(QA)
    own_shard(QB)
    pl.semaphore_wait(barrier, 7)
    g_start(SM)
    g_start(QA)
    constants()
    tok_copy.wait()
    first_norm()
    own_shard(OUT)
    g_start(OUT)
    g_start(QB)
    own_shard(UP)
    g_start(UP)
    g_z(SM)
    g_z(QA)
    g_z(OUT)
    own_shard(DOWN)
    g_start(DOWN)
    g_s(SM)
    g_sib(SM)
    g_z(QB)
    g_s(QA)
    g_sib(QA)
    cot_copy.wait()
    cotangent_in()
    g_f(OUT)
    g_z(UP)
    g_s(QB)
    small_vectors()
    first_affine()
    project_in(0)
    loop(1, lambda i: attention(0, i), 0)
    g_sib(QB)
    g_f(UP)
    g_s(OUT)
    project_in(1)
    g_z(DOWN)
    loop(3, lambda i: attention(0, i), 1)
    loop(2, lambda i: attention(1, i), 0)
    g_sib(OUT)
    loop(3, lambda i: attention(1, i), 2)
    g_s(UP)
    project_out()
    second_norm(0, 5)
    g_f(DOWN)
    g_sib(UP)
    feed_up(0, 8)
    down_theirs(0)
    g_s(DOWN)
    down_theirs(1)
    down_ours(0)
    down_ours(1)
    g_sib(DOWN)
    feed_back(0, 4)
    r_1(DOWN)
    feed_back(4, 8)
    back_to(slope, UP, 0)
    grad_theirs(UP, a2, slope, 0, 512)
    grad_ours(UP, a2, slope, 0, 512)
    r_2(DOWN)
    back_to(slope, UP, 1)
    r_1(UP)
    second_back(0, 5)
    back_to(dao, OUT, 0)
    back_to(dao, OUT, 1)
    grad_ours(OUT, ctx, dao, 0, 512)
    loop(1, lambda i: attention_back(1, i), 0)
    grad_theirs(OUT, ctx, dao, 0, 512)
    loop(2, lambda i: attention_back(0, i), 0)
    r_3(DOWN)
    r_2(UP)
    loop(3, lambda i: attention_back(0, i), 2)
    r_1(OUT)
    grad_theirs(QA, a1, dpre, 0, HALF)
    loop(3, lambda i: attention_back(1, i), 1)
    grad_ours(QA, a1, dpre, 0, HALF)
    r_1(QA)
    grad_theirs(QB, a1, dpre, 3, HALF)
    r_3(UP)
    r_2(OUT)
    grad_ours(QB, a1, dpre, 3, HALF)
    back_in(0)
    r_1(QB)
    r_2(QA)
    back_in(1)
    first_back()
    tgrad_copy = pltpu.make_async_copy(cotb, tgrad_hbm, io_sem.at[3])
    tgrad_copy.start()
    small_grads()
    r_2(QB)
    r_3(QA)
    r_3(OUT)
    r_1(SM)
    r_3(QB)
    r_4(DOWN)
    arg_copy(DOWN_ARG).start()
    r_2(SM)
    r_3(SM)
    r_4(UP)
    arg_copy(UP_ARG).start()
    for w in (SM, QA, QB, OUT, UP, DOWN):
        g_end(w)
    r_4(QA)
    feed_down(0)
    feed_down(1)
    narrow(tokb)
    mixed_copy = pltpu.make_async_copy(tokb, mixed_hbm, io_sem.at[2])
    mixed_copy.start()
    r_4(OUT)
    arg_copy(OUT_ARG).start()
    r_4(SM)
    r_4(QB)
    arg_copy(QKV_ARG).start()
    for w in (SM, QA, QB, OUT, UP, DOWN):
        r_end(w)
    for k in range(4):
        arg_copy(k).wait()
    small_copy.wait()
    mixed_copy.wait()
    tgrad_copy.wait()


def call_layer(split, tokens, frames, small, shards, cotangent):
    count = tokens.shape[0]
    any_spec = pl.BlockSpec(memory_space=pl.ANY)
    vmem = pl.BlockSpec(memory_space=pltpu.VMEM)

    def kept(n, dtype=None):
        return [pltpu.VMEM((n, r, k), dtype or t) for r, k, t in zip(ROWS, COLS, KEPT)]

    scratch = [pltpu.VMEM((n, 128), F32) for n in PACKED] + [pltpu.VMEM((PACK_ALL, 128), F32)]
    scratch += [pltpu.VMEM((2, 2, 4, 2, r, k), t) for r, k, t in zip(ROWS, COLS, KEPT)]
    scratch += kept(16, F32)
    for n in (16, 8, 4, 3):
        scratch += kept(n) + kept(n)
    rows_bf = lambda k: pltpu.VMEM((count, k), BF16)
    rows_f = lambda k: pltpu.VMEM((count, k), F32)
    scratch += [
        rows_bf(D), rows_bf(D), pltpu.VMEM((4, count, 128), F32), rows_bf(D), rows_bf(D),
        rows_f(D), rows_f(D), rows_f(128), rows_f(128),
        rows_bf(D), rows_bf(D), rows_bf(3 * D),
        pltpu.VMEM((2, len(PAIRS), count // FRAMES, 128), F32),
        rows_bf(D), rows_f(D), rows_bf(FF), rows_bf(FF),
        rows_f(D), rows_bf(D), rows_bf(3 * D), pltpu.VMEM((HALF, count), BF16),
    ]
    scratch += [
        pltpu.VMEM((8, 512), F32), pltpu.VMEM((8, 1024), F32), pltpu.VMEM((8, 2048), F32), pltpu.VMEM((1, 3 * D), F32),
        pltpu.VMEM((count // FRAMES, 128), F32), pltpu.VMEM((HALF, 128), BF16), pltpu.VMEM((128, HALF), BF16),
        pltpu.VMEM((8, 512), F32), pltpu.VMEM((8, 1024), F32), pltpu.VMEM((8, 2048), F32),
        pltpu.VMEM((2, 2, 8, 8, 128), F32),
    ]
    scratch += [pltpu.SemaphoreType.DMA((6, n)) for n in (5, 10, 4, 11)]
    scratch += [pltpu.SemaphoreType.DMA((13,))]
    out_shape = [jax.ShapeDtypeStruct(tokens.shape, BF16)] * 2
    out_shape += [jax.ShapeDtypeStruct((PACK_ALL, 128), F32)]

    def body(*refs):
        layer_kernel(split, count, *refs)

    return pl.pallas_call(
        body,
        name="layer",
        out_shape=out_shape,
        in_specs=[any_spec, any_spec] + [vmem] * 9 + [any_spec] * 4,
        out_specs=[any_spec] * 3,
        scratch_shapes=scratch,
        compiler_params=pltpu.CompilerParams(
            collective_id=0, has_side_effects=True, vmem_limit_bytes=63 << 20
        ),
        cost_estimate=pl.CostEstimate(
            flops=2 * 3 * count * (3 * D * D + D * D + 2 * D * FF), bytes_accessed=1 << 23, transcendentals=count * FF
        ),
    )(tokens, cotangent, frames, *small, *shards)


def hand_out(mixed, tokens_grad, grads):
    any_spec = pl.BlockSpec(memory_space=pl.ANY)
    vmem = pl.BlockSpec(memory_space=pltpu.VMEM)

    def body(mixed_in, tgrad_in, grads_in, *refs):
        outs, (mixed_v, tgrad_v, grads_v, in_sem, out_sem) = refs[:14], refs[14:]
        smalls, big = outs[2:10], (outs[0], outs[1]) + tuple(outs[10:])
        reads = [
            pltpu.make_async_copy(src, dst, in_sem.at[k])
            for k, (src, dst) in enumerate(((mixed_in, mixed_v), (tgrad_in, tgrad_v), (grads_in, grads_v)))
        ]
        parts = [mixed_v, tgrad_v] + [grads_v.at[pl.ds(PACK[k], PACKED[k])] for k in range(4)]
        writes = [pltpu.make_async_copy(src, dst, out_sem.at[k]) for k, (src, dst) in enumerate(zip(parts, big))]
        for copy in reads:
            copy.start()
        for k in range(3):
            reads[k].wait()
            for copy in writes[2:] if k == 2 else writes[k : k + 1]:
                copy.start()
        for p, n in enumerate(SMALL):
            smalls[p][...] = grads_v[PACK_SMALL + p : PACK_SMALL + p + 1, 0:n]
        for copy in writes:
            copy.wait()

    row_shapes = [jax.ShapeDtypeStruct(mixed.shape, BF16)] * 2
    small_shapes = [jax.ShapeDtypeStruct((1, n), F32) for n in SMALL]
    shard_shapes = [jax.ShapeDtypeStruct((n, 128), F32) for n in PACKED]
    return pl.pallas_call(
        body,
        name="hand_out",
        out_shape=row_shapes + small_shapes + shard_shapes,
        in_specs=[any_spec] * 3,
        out_specs=[any_spec] * 2 + [vmem] * 8 + [any_spec] * 4,
        scratch_shapes=[
            pltpu.VMEM(mixed.shape, BF16), pltpu.VMEM(mixed.shape, BF16), pltpu.VMEM(grads.shape, F32),
            pltpu.SemaphoreType.DMA((3,)), pltpu.SemaphoreType.DMA((6,)),
        ],
    )(mixed, tokens_grad, grads)


def local(split, tokens, frames, g1, b1, wqkv, bqv, wo, bo, g2, b2, w1, b1f, w2, b2f, cotangent):
    spot = lax.axis_index("fsdp") // split

    def block(values):
        if split == 1:
            return values
        n = values.shape[0]
        every = lax.all_gather(values, "fsdp", axis=0, tiled=True)
        return lax.dynamic_slice(every, (spot * split * n,), (split * n,))

    def owned(values):
        if split == 1:
            return values
        n = values.shape[0]
        spread = lax.dynamic_update_slice(jnp.zeros((8 * n,), F32), values, (spot * n,))
        return lax.psum_scatter(spread, "fsdp", scatter_dimension=0, tiled=True)

    small = [block(v).reshape(1, -1) for v in (g1, b1, bqv, bo, g2, b2, b1f, b2f)]
    shards = [block(v).reshape(-1, 128) for v in (wqkv, wo, w1, w2)]
    outs = hand_out(*call_layer(split, tokens, frames.reshape(1, -1), small, shards, cotangent))
    mixed, tokens_grad = outs[:2]
    dg1, db1, dbqv, dbo, dg2, db2, db1f, db2f = [owned(v.reshape(-1)) for v in outs[2:10]]
    dwqkv, dwo, dw1, dw2 = [owned(v.reshape(-1)) for v in outs[10:]]
    return (mixed, tokens_grad, dg1, db1, dwqkv, dbqv, dwo, dbo, dg2, db2, dw1, db1f, dw2, db2f)


def solution(mesh):
    split = mesh.shape["fsdp"] // 8
    flat, rows = P(("dp", "fsdp")), P(("dp", "fsdp"), None)

    def body(*args):
        return local(split, *args)

    return jax.shard_map(
        body,
        mesh=mesh,
        in_specs=(rows,) + (flat,) * 13 + (rows,),
        out_specs=(rows, rows) + (flat,) * 12,
        check_vma=False,
    )
```

```python
import math

import jax
import jax.numpy as jnp
from jax import lax
from jax.experimental import pallas as pl
from jax.experimental.pallas import tpu as pltpu
from jax.sharding import PartitionSpec as P

D = 512
HEADS = 8
HEAD_DIM = 64
FF = 2048
FRAMES = 5
EPSILON = 1e-05
PAIRS = [(t, u) for t in range(FRAMES) for u in range(t + 1)]

F32 = jnp.float32
BF16 = jnp.bfloat16
MESH = pl.DeviceIdType.MESH

SM, QA, QB, OUT, UP, DOWN = range(6)
ROWS = (8, 16, 16, 16, 16, 64)
COLS = (128, 3 * D // 2, 3 * D // 2, D, FF, D)
KEPT = (F32, BF16, BF16, BF16, BF16, BF16)
DIRECT = (SM, QA, QB,)
HALF = D // 2
WIDE = FF // 2
GROUP = HEADS // 2
QKV_ARG, OUT_ARG, UP_ARG, DOWN_ARG = range(4)
ARG = (None, QKV_ARG, QKV_ARG, OUT_ARG, UP_ARG, DOWN_ARG)
PACKED = (192, 64, 256, 256)
PACK = (0, 192, 256, 512)
PACK_SMALL, PACK_ALL = 768, 776
SMALL = (16, 16, 32, 16, 16, 16, 64, 16)
GAIN1, BIAS1, QVB, OUTB, GAIN2, BIAS2, UPB, DOWNB = range(8)

TILE = 192
CHUNK = 64


def dot(left, right):
    return lax.dot_general(left, right, (((1,), (0,)), ((), ())), preferred_element_type=F32)


def dot_nt(left, right):
    return lax.dot_general(left, right, (((1,), (1,)), ((), ())), preferred_element_type=F32)


def dot_tn(left, right):
    return lax.dot_general(left, right, (((0,), (0,)), ((), ())), preferred_element_type=F32)


def iota(shape, dim):
    return lax.broadcasted_iota(jnp.int32, shape, dim)


def fold(values):
    rows, cols = values.shape
    return jnp.sum(values.reshape(rows // 8, 8, cols), axis=0)


def split_two(values):
    high = values.astype(BF16)
    return high, (values - high.astype(F32)).astype(BF16)


def layer_kernel(split, count, *refs):
    refs = list(refs)

    def take(n):
        head = refs[:n]
        del refs[:n]
        return head

    tok_hbm, cot_hbm, frames_hbm = take(3)
    small_hbm = take(8)
    shard_hbm = take(4)
    mixed_hbm, tgrad_hbm, grads_hbm = take(3)
    shard_in = take(4)
    small_in = take(8)
    (frames_in,) = take(1)
    (grads,) = take(1)
    whole = take(6)
    acc = take(6)
    sib_out, sib_in = take(6), take(6)
    two_out, two_in = take(6), take(6)
    one_out, one_in = take(6), take(6)
    zed_out, zed_in = take(6), take(6)
    (tokb, cotb, stage, xt, dm, xh1, xh2, rs1, rs2, a1, a2, qkv, prob, ctx, x1, act, slope, wide, dpre, turned) = take(20)
    (vec16, vecqv, vecup, biasq, living, pick, pick_t, gs16, gsqv, gsup, sums) = take(11)
    (gsend, grecv, rsend, rrecv, io_sem, small_sem) = take(6)

    dao = cotb

    seqs = count // FRAMES
    dp = lax.axis_index("dp")
    fs = lax.axis_index("fsdp")
    x, c = dp // 2, dp % 2
    group, rest = fs // split, fs % split
    z, y = group // 2, group % 2

    def device(x_, c_, z_, y_):
        return (x_ * 2 + c_, (z_ * 2 + y_) * split + rest)

    first = x + c * (y - x)
    second = y + c * (x - y)

    def to_xy(f_, s_):
        return f_ + c * (s_ - f_), s_ + c * (f_ - s_)

    def peer(f_, s_):
        x_, y_ = to_xy(f_, s_)
        return device(x_, c, z, y_)

    sibling = device(x, 1 - c, z, y)
    first_dev = peer(1 - first, second)
    second_dev = peer(first, 1 - second)
    across_dev = peer(1 - first, 1 - second)
    zeds = (z + 1 - 2 * (z % 2), (z + 2) % 4, 3 - z)
    zed_dev = [device(x, c, zk, y) for zk in zeds]

    barrier = pltpu.get_barrier_semaphore()
    for dev in [sibling, first_dev, second_dev, across_dev] + zed_dev:
        pl.semaphore_signal(barrier, inc=1, device_id=dev, device_id_type=MESH)
    small_copy_in = [pltpu.make_async_copy(small_hbm[p], small_in[p], small_sem.at[p]) for p in range(8)]
    shard_copy = [pltpu.make_async_copy(shard_hbm[k], shard_in[k], io_sem.at[4 + k]) for k in range(4)]
    frames_copy = pltpu.make_async_copy(frames_hbm, frames_in, small_sem.at[8])
    tok_copy = pltpu.make_async_copy(tok_hbm, tokb, io_sem.at[0])
    cot_copy = pltpu.make_async_copy(cot_hbm, cotb, io_sem.at[1])
    for copy in small_copy_in + shard_copy + [tok_copy, frames_copy, cot_copy]:
        copy.start()

    def shard(w, f_, s_, z_):
        x_, y_ = to_xy(f_, s_)
        return whole[w].at[x_, c, z_, y_]

    def line(w, f_, s_):
        x_, y_ = to_xy(f_, s_)
        return whole[w].at[x_, c, :, y_]

    def gcopy(w, sent, got, ref, dev):
        return pltpu.make_async_remote_copy(
            src_ref=ref, dst_ref=ref, send_sem=gsend.at[w, sent], recv_sem=grecv.at[w, got], device_id=dev, device_id_type=MESH
        )

    def cols_of(w):
        if w in (QA, QB):
            return [(4 * p + 2 * (w - QA) + b, 2 * p + b) for p in range(3) for b in range(2)]
        return [(k, k) for k in range(COLS[w] // 128)]

    def own_shard(w):
        if w == SM:
            whole[w][x, c, z, y] = jnp.zeros((8, 128), F32)
            for p, n in enumerate(SMALL):
                small_copy_in[p].wait()
                whole[w][x, c, z, y, p : p + 1, 0:n] = small_in[p][...].astype(BF16).astype(F32)
        else:
            if w != QB:
                shard_copy[ARG[w]].wait()
            step = PACKED[ARG[w]] // ROWS[w]
            for k, to in cols_of(w):
                part = shard_in[ARG[w]][pl.ds(k, ROWS[w], stride=step), :]
                whole[w][x, c, z, y, :, to * 128 : (to + 1) * 128] = part.astype(BF16)

    def hand_on(w, ref, spot):
        if w in DIRECT:
            gcopy(w, 1, 3, ref, first_dev).start()
            gcopy(w, 2, 7, ref, second_dev).start()
            gcopy(w, 3, 8, ref, across_dev).start()
        else:
            gcopy(w, 1, 3 + spot, ref, first_dev).start()
            gcopy(w, 2, 7, ref, second_dev).start()

    def to_sibling(w, f_, s_):
        gcopy(w, 4, 9, line(w, f_, s_), sibling).start()

    def g_start(w):
        ref = shard(w, first, second, z)
        for k in range(3):
            gcopy(w, 0, k, ref, zed_dev[k]).start()
        hand_on(w, ref, z)

    def g_z(w):
        for k in range(3):
            ref = shard(w, first, second, zeds[k])
            gcopy(w, 0, k, ref, zed_dev[k]).wait_recv()
            hand_on(w, ref, zeds[k])
        to_sibling(w, first, second)

    def g_f(w):
        for k in range(4):
            ref = shard(w, 1 - first, second, k)
            gcopy(w, 1, 3 + k, ref, first_dev).wait_recv()
            gcopy(w, 2, 8, ref, second_dev).start()
        to_sibling(w, 1 - first, second)

    def g_s(w):
        if w in DIRECT:
            gcopy(w, 1, 3, line(w, 1 - first, second), first_dev).wait_recv()
            to_sibling(w, 1 - first, second)
        gcopy(w, 2, 7, line(w, first, 1 - second), second_dev).wait_recv()
        to_sibling(w, first, 1 - second)
        gcopy(w, 2, 8, line(w, 1 - first, 1 - second), second_dev).wait_recv()
        to_sibling(w, 1 - first, 1 - second)

    def g_sib(w):
        ref = whole[w].at[:, 1 - c]
        gcopy(w, 4, 9, ref, sibling).wait_recv()

    def g_end(w):
        gcopy(w, 0, 0, zed_out[w], sibling).wait_send()
        four = line(w, first, second)
        gcopy(w, 1, 3, four, sibling).wait_send()
        if w in DIRECT:
            gcopy(w, 2, 7, four, sibling).wait_send()
            gcopy(w, 3, 8, four, sibling).wait_send()
        else:
            gcopy(w, 2, 7, two_out[w], sibling).wait_send()
        gcopy(w, 4, 9, sib_out[w], sibling).wait_send()

    def loop(n, body, start=0):
        def step(i, carry):
            body(i)
            return carry

        lax.fori_loop(start, n, step, 0)

    def place(f_, s_, z_):
        x_, y_ = to_xy(f_, s_)
        return x_ * 8 + z_ * 2 + y_

    def rcopy(w, sent, got, src, dst, dev):
        return pltpu.make_async_remote_copy(
            src_ref=src, dst_ref=dst, send_sem=rsend.at[w, sent], recv_sem=rrecv.at[w, got], device_id=dev, device_id_type=MESH
        )

    def sib_copy(w, at, n):
        return rcopy(w, 0, 0, sib_out[w].at[pl.ds(at, n)], sib_in[w].at[pl.ds(at, n)], sibling)

    def two_copy(w, k, got):
        return rcopy(w, 1, got, two_out[w].at[k], two_in[w].at[k], second_dev)

    def one_copy(w, k):
        return rcopy(w, 2, 6 + k, one_out[w].at[k], one_in[w].at[k], first_dev)

    def zed_copy(w, k):
        return rcopy(w, 3, 10, zed_out[w].at[k], zed_in[w].at[k], zed_dev[k])

    def r_1(w):
        sib_copy(w, 0, 16).wait_recv()

        def step(k, got):
            j = place(k // 4, 1 - second, k % 4)
            two_out[w][k] = (acc[w][j] + sib_in[w][j].astype(F32)).astype(KEPT[w])
            two_copy(w, k, got).start()

        loop(4, lambda i: step(4 * (1 - first) + i, 1 + i))
        loop(4, lambda i: step(4 * first + i, 5))

    def r_2(w):
        def step(i):
            k = (z + 1 + i) % 4
            j = place(1 - first, second, k)
            slot = (1 - first) * 4 + k
            two_copy(w, slot, 1 + k).wait_recv()
            total = acc[w][j] + sib_in[w][j].astype(F32) + two_in[w][slot].astype(F32)
            one_out[w][k] = total.astype(KEPT[w])
            one_copy(w, k).start()

        loop(4, step)

    def r_3(w):
        line_in = two_in[w].at[pl.ds(4 * first, 4)]
        rcopy(w, 1, 5, line_in, line_in, second_dev).wait_recv()
        for k in range(3):
            j = place(first, second, zeds[k])
            slot = first * 4 + zeds[k]
            one_copy(w, zeds[k]).wait_recv()
            total = acc[w][j] + sib_in[w][j].astype(F32) + two_in[w][slot].astype(F32) + one_in[w][zeds[k]].astype(F32)
            zed_out[w][k] = total.astype(KEPT[w])
            zed_copy(w, k).start()

    def grad_copy(at, rows, k):
        return pltpu.make_async_copy(grads.at[pl.ds(at, rows)], grads_hbm.at[pl.ds(at, rows)], io_sem.at[8 + k])

    def arg_copy(k):
        return grad_copy(PACK[k], PACKED[k], k)

    small_copy = grad_copy(PACK_SMALL, 8, 4)

    def r_4(w):
        j = place(first, second, z)
        slot = first * 4 + z
        one_copy(w, z).wait_recv()
        total = acc[w][j] + sib_in[w][j].astype(F32) + two_in[w][slot].astype(F32) + one_in[w][z].astype(F32)
        rcopy(w, 3, 10, zed_in[w], zed_in[w], sibling).wait_recv()
        for k in range(3):
            total = total + zed_in[w][k].astype(F32)
        if w == SM:
            grads[PACK_SMALL:PACK_ALL, :] = total
            small_copy.start()
        else:
            step = PACKED[ARG[w]] // ROWS[w]
            for k, at in cols_of(w):
                grads[pl.ds(PACK[ARG[w]] + k, ROWS[w], stride=step), :] = total[:, at * 128 : (at + 1) * 128]

    def r_end(w):
        sib_copy(w, 0, 16).wait_send()
        rcopy(w, 1, 5, two_out[w], two_in[w], sibling).wait_send()
        rcopy(w, 2, 6, one_out[w], one_in[w], sibling).wait_send()
        rcopy(w, 3, 10, zed_out[w], zed_in[w], sibling).wait_send()

    tiles = count // TILE
    per_frame = seqs // TILE

    def tile_rows(i):
        return pl.ds(pl.multiple_of(i * TILE, TILE), TILE)

    def strided(i):
        return pl.ds(i // per_frame + FRAMES * TILE * (i % per_frame), TILE, stride=FRAMES)

    def widen(src):
        def body(i):
            for h in range(4):
                stage[h, tile_rows(i), :] = src[tile_rows(i), h * 128 : (h + 1) * 128].astype(F32)

        loop(tiles, body)

    def narrow(dst):
        def body(i):
            for h in range(4):
                dst[tile_rows(i), h * 128 : (h + 1) * 128] = stage[h, tile_rows(i), :].astype(BF16)

        loop(tiles, body)

    def center(values):
        mean = jnp.mean(values, axis=-1, keepdims=True)
        centered = values - mean
        root = lax.rsqrt(jnp.mean(centered * centered, axis=-1, keepdims=True) + EPSILON)
        return centered * root, root

    def constants():
        lane, row = iota((HALF, 128), 1), iota((HALF, 128), 0)
        pick[...] = jnp.where((row // HEAD_DIM == lane % GROUP) & (lane < 2 * GROUP), 1.0, 0.0).astype(BF16)
        lane, row = iota((128, HALF), 1), iota((128, HALF), 0)
        pick_t[...] = jnp.where((lane // HEAD_DIM == row % GROUP) & (row < 2 * GROUP), 1.0, 0.0).astype(BF16)
        frames_copy.wait()
        same = iota((seqs, seqs), 0) == iota((seqs, seqs), 1)
        wide_frames = jnp.broadcast_to(frames_in[...].astype(F32), (seqs, seqs))
        spread = jnp.where(same, wide_frames, 0.0).astype(BF16)
        living[...] = dot(spread, jnp.ones((seqs, 128), BF16))
        gs16[...] = jnp.zeros_like(gs16)
        gsqv[...] = jnp.zeros_like(gsqv)
        gsup[...] = jnp.zeros_like(gsup)

    def first_norm():
        widen(tokb)

        def body(i):
            values = jnp.concatenate([stage[h, strided(i), :] for h in range(4)], axis=1)
            xt[tile_rows(i), :] = values.astype(BF16)
            hat, root = center(values)
            xh1[tile_rows(i), :] = hat
            rs1[tile_rows(i), :] = jnp.broadcast_to(root, (TILE, 128))

        loop(tiles, body)

    def cotangent_in():
        widen(cotb)

        def body(i):
            values = jnp.concatenate([stage[h, strided(i), :] for h in range(4)], axis=1)
            dm[tile_rows(i), :] = values.astype(BF16)
            gs16[DOWNB : DOWNB + 1, :] += jnp.sum(fold(values), axis=0, keepdims=True)

        loop(tiles, body)

    def small_vectors():
        raw = whole[SM][...].reshape(256, 128).astype(BF16)
        for n, dst in ((16, vec16), (32, vecqv), (64, vecup)):
            width = 32 * n
            for at in range(0, width, 512):
                near = iota((128, 512), 0) == (iota((128, 512), 1) + at) % n
                spread = dot(raw, jnp.where(near, 1.0, 0.0).astype(BF16))
                mine = iota((256, 512), 0) // 8 == (iota((256, 512), 1) + at) // n
                dst[:, at : at + 512] = jnp.sum(jnp.where(mine, spread, 0.0).reshape(32, 8, 512), axis=0)
        biasq[...] = jnp.zeros_like(biasq)
        for h in range(2):
            for part in range(2):
                at = 3 * HALF * h + 2 * HALF * part
                biasq[:, at : at + HALF] = vecqv[QVB : QVB + 1, part * D + h * HALF : part * D + (h + 1) * HALF]

    def small_grads():
        for n, src in ((16, gs16), (32, gsqv), (64, gsup)):
            width = 32 * n
            for at in range(0, width, 512):
                mine = iota((256, 512), 0) // 8 == (iota((256, 512), 1) + at) // n
                values = jnp.broadcast_to(src[:, at : at + 512][None], (32, 8, 512)).reshape(256, 512)
                high, low = split_two(jnp.where(mine, values, 0.0))
                near = jnp.where(iota((128, 512), 0) == (iota((128, 512), 1) + at) % n, 1.0, 0.0).astype(BF16)
                part = dot_nt(high, near) + dot_nt(low, near)
                total = part if n == 16 and at == 0 else total + part
        sums[...] = total.reshape(2, 2, 8, 8, 128)
        for h in range(2):
            acc[SM][8 * h : 8 * h + 8] = sums[h, c]
            sib_out[SM][8 * h : 8 * h + 8] = sums[h, 1 - c]
            sib_copy(SM, 8 * h, 8).start()

    def first_affine():
        gain, bias = vec16[GAIN1 : GAIN1 + 1, :], vec16[BIAS1 : BIAS1 + 1, :]

        def body(i):
            a1[tile_rows(i), :] = (xh1[tile_rows(i), :] * gain + bias).astype(BF16)

        loop(tiles, body)

    def cols(n, width):
        return pl.ds(pl.multiple_of(n * width, width), width)

    def matrix_cols(w, n, width):
        return whole[w][:, :, :, :, :, cols(n, width)].reshape(32 * ROWS[w], width)

    def matrix(w):
        return whole[w][...].reshape(32 * ROWS[w], COLS[w])

    def project_in(h):
        at = slice(3 * HALF * h, 3 * HALF * (h + 1))
        r = dot(a1[...], matrix(QA + h)) + biasq[:, at]
        qkv[:, at] = r.astype(BF16)

    def frame_rows(t, i):
        return pl.ds(pl.multiple_of(t * seqs + i * CHUNK, CHUNK), CHUNK)

    def heads_of(h, i, part):
        at = (3 * h + part) * HALF
        return [qkv[frame_rows(t, i), at : at + HALF].astype(F32) for t in range(FRAMES)]

    def spread_heads(parts):
        lanes = iota((CHUNK, 128), 1)
        mixed_parts = []
        for part in parts:
            high, low = split_two(part)
            mixed_parts.append(jnp.where(lanes < GROUP, high.astype(F32), low.astype(F32)).astype(BF16))
        return dot(jnp.concatenate(mixed_parts, axis=0), pick_t[...])

    def rows_of(values, k):
        return values[k * CHUNK : (k + 1) * CHUNK]

    def attention(h, i):
        q, k_, v = heads_of(h, i, 0), heads_of(h, i, 1), heads_of(h, i, 2)
        halves = [split_two(q[t] * k_[u]) for t, u in PAIRS]
        high = jnp.concatenate([h for h, _ in halves], axis=0)
        low = jnp.concatenate([l for _, l in halves], axis=0)
        scores = (dot(high, pick[...]) + dot(low, pick[...])) * (1.0 / math.sqrt(HEAD_DIM))
        live = living[pl.ds(pl.multiple_of(i * CHUNK, CHUNK), CHUNK), :]
        weights = []
        for t in range(FRAMES):
            row = [rows_of(scores, PAIRS.index((t, u))) for u in range(t + 1)]
            row = [jnp.where(u < live, part, -1e30) for u, part in enumerate(row)]
            top = row[0]
            for part in row[1:]:
                top = jnp.maximum(top, part)
            row = [jnp.exp(part - top) for part in row]
            total = row[0]
            for part in row[1:]:
                total = total + part
            weights += [part / total for part in row]
        for k, part in enumerate(weights):
            prob[h, k, pl.ds(pl.multiple_of(i * CHUNK, CHUNK), CHUNK), :] = part
        spread = spread_heads(weights)
        for t in range(FRAMES):
            total = rows_of(spread, PAIRS.index((t, 0))) * v[0]
            for u in range(1, t + 1):
                total = total + rows_of(spread, PAIRS.index((t, u))) * v[u]
            ctx[frame_rows(t, i), h * HALF : (h + 1) * HALF] = total.astype(BF16)

    def attention_back(h, i):
        v = heads_of(h, i, 2)
        g = [wide[frame_rows(t, i), h * HALF : (h + 1) * HALF] for t in range(FRAMES)]
        base = 3 * HALF * h
        products = jnp.concatenate([(g[t] * v[u]).astype(BF16) for t, u in PAIRS], axis=0)
        slopes = dot(products, pick[...])
        weights = [prob[h, k, pl.ds(pl.multiple_of(i * CHUNK, CHUNK), CHUNK), :] for k in range(len(PAIRS))]
        scaled = []
        for t in range(FRAMES):
            ks = [PAIRS.index((t, u)) for u in range(t + 1)]
            mean = weights[ks[0]] * rows_of(slopes, ks[0])
            for k in ks[1:]:
                mean = mean + weights[k] * rows_of(slopes, k)
            scaled += [weights[k] * (rows_of(slopes, k) - mean) * (1.0 / math.sqrt(HEAD_DIM)) for k in ks]
        spread_p = spread_heads(weights)
        for u in range(FRAMES):
            total = None
            for t in range(u, FRAMES):
                part = rows_of(spread_p, PAIRS.index((t, u))) * g[t]
                total = part if total is None else total + part
            low = total.astype(BF16)
            dpre[frame_rows(u, i), base + 2 * HALF : base + 3 * HALF] = low
            gsqv[QVB : QVB + 1, D + h * HALF : D + (h + 1) * HALF] += jnp.sum(fold(low.astype(F32)), axis=0, keepdims=True)
        q, k_ = heads_of(h, i, 0), heads_of(h, i, 1)
        spread_s = spread_heads(scaled)
        for t in range(FRAMES):
            total = None
            for u in range(t + 1):
                part = rows_of(spread_s, PAIRS.index((t, u))) * k_[u]
                total = part if total is None else total + part
            low = total.astype(BF16)
            dpre[frame_rows(t, i), base : base + HALF] = low
            gsqv[QVB : QVB + 1, h * HALF : (h + 1) * HALF] += jnp.sum(fold(low.astype(F32)), axis=0, keepdims=True)
        for u in range(FRAMES):
            total = None
            for t in range(u, FRAMES):
                part = rows_of(spread_s, PAIRS.index((t, u))) * q[t]
                total = part if total is None else total + part
            dpre[frame_rows(u, i), base + HALF : base + 2 * HALF] = total.astype(BF16)

    def project_out():
        bias = vec16[OUTB : OUTB + 1, :]
        for n in range(2):
            at = slice(n * 256, (n + 1) * 256)
            r = dot(ctx[...], whole[OUT][:, :, :, :, :, at].reshape(D, 256))
            x1[:, at] = xt[:, at].astype(F32) + r + bias[:, at]

    def second_norm(start, stop):
        gain, bias = vec16[GAIN2 : GAIN2 + 1, :], vec16[BIAS2 : BIAS2 + 1, :]

        def body(i):
            hat, root = center(x1[tile_rows(i), :])
            xh2[tile_rows(i), :] = hat
            rs2[tile_rows(i), :] = jnp.broadcast_to(root, (TILE, 128))
            a2[tile_rows(i), :] = (hat * gain + bias).astype(BF16)

        loop(stop, body, start)

    def feed_up(start, stop):
        k0 = math.sqrt(2.0 / math.pi)
        k1 = k0 * 0.044715

        def body(n):
            f = dot(a2[...], matrix_cols(UP, n, WIDE)) + vecup[UPB : UPB + 1, cols(n, WIDE)]
            square = f * f
            half = 0.5 + 0.5 * jnp.tanh(f * (k0 + k1 * square))
            act[:, cols(n, WIDE)] = (f * half).astype(BF16)
            grow = half + (f * (half - half * half)) * (2.0 * k0 + 6.0 * k1 * square)
            slope[:, cols(n, WIDE)] = grow.astype(BF16)

        loop(stop, body, start)

    def feed_down(n):
        bias = vec16[DOWNB : DOWNB + 1, :]
        at = slice(n * 256, (n + 1) * 256)
        r = dot(act[...], whole[DOWN][:, :, :, :, :, at].reshape(FF, 256))
        r = r + x1[:, at] + bias[:, at]
        for t in range(FRAMES):
            for h in range(2):
                stage[2 * n + h, pl.ds(t, seqs, stride=FRAMES), :] = r[t * seqs : (t + 1) * seqs, h * 128 : (h + 1) * 128]

    def turn(left):
        parts = [left[:, pl.ds(pl.multiple_of(h * 256 + core * 128, 128), 128)] for core in (1 - c, c) for h in range(2)]
        turned[...] = jnp.transpose(jnp.concatenate(parts, axis=1))

    def weight_grad(w, right, base, n, width):
        at = slice(n * width, (n + 1) * width)
        r = dot(turned[...], right[:, base + n * width : base + (n + 1) * width])
        sib_out[w][:, :, at] = r[:HALF].reshape(16, ROWS[w], width).astype(BF16)
        rcopy(w, 0, 0, sib_out[w].at[:, :, at], sib_in[w].at[:, :, at], sibling).start()
        acc[w][:, :, at] = r[HALF:].reshape(16, ROWS[w], width)

    def down_theirs(h):
        left = act[:, pl.ds(pl.multiple_of(h * 1024 + (1 - c) * 512, 512), 512)]
        r = dot_tn(left, dm[...])
        sib_out[DOWN][8 * h : 8 * h + 8] = r.reshape(8, 64, D).astype(BF16)
        sib_copy(DOWN, 8 * h, 8).start()

    def down_ours(h):
        left = act[:, pl.ds(pl.multiple_of(h * 1024 + c * 512, 512), 512)]
        acc[DOWN][8 * h : 8 * h + 8] = dot_tn(left, dm[...]).reshape(8, 64, D)

    def feed_back(start, stop):
        def body(n):
            part = whole[DOWN][n].reshape(WIDE, D)
            low = (dot_nt(dm[...], part) * slope[:, cols(n, WIDE)].astype(F32)).astype(BF16)
            slope[:, cols(n, WIDE)] = low
            gsup[UPB : UPB + 1, cols(n, WIDE)] = jnp.sum(fold(low.astype(F32)), axis=0, keepdims=True)

        loop(stop, body, start)

    def back_to(left, w, h):
        wide[:, h * 256 : (h + 1) * 256] = dot_nt(left[...], whole[w][h].reshape(256, COLS[w]))

    def back_in(h):
        r = dot_nt(dpre[:, : 3 * HALF], whole[QA][h].reshape(256, 3 * HALF))
        r = r + dot_nt(dpre[:, 3 * HALF :], whole[QB][h].reshape(256, 3 * HALF))
        wide[:, h * 256 : (h + 1) * 256] = r

    def norm_back(grads, hat, root, gain, gain_at, bias_at):
        gs16[gain_at : gain_at + 1, :] += jnp.sum(fold(grads * hat), axis=0, keepdims=True)
        gs16[bias_at : bias_at + 1, :] += jnp.sum(fold(grads), axis=0, keepdims=True)
        scaled = grads * gain
        mean = jnp.mean(scaled, axis=-1, keepdims=True)
        along = jnp.mean(scaled * hat, axis=-1, keepdims=True)
        return (scaled - mean - hat * along) * root

    def second_back(start, stop):
        gain = vec16[GAIN2 : GAIN2 + 1, :]

        def body(i):
            at = tile_rows(i)
            part = norm_back(wide[at, :], xh2[at, :], rs2[at, 0:1], gain, GAIN2, BIAS2)
            total = dm[at, :].astype(F32) + part
            xh2[at, :] = total
            low = total.astype(BF16)
            dao[at, :] = low
            gs16[OUTB : OUTB + 1, :] += jnp.sum(fold(low.astype(F32)), axis=0, keepdims=True)

        loop(stop, body, start)

    def first_back():
        gain = vec16[GAIN1 : GAIN1 + 1, :]

        def body(i):
            at = tile_rows(i)
            part = norm_back(wide[at, :], xh1[at, :], rs1[at, 0:1], gain, GAIN1, BIAS1)
            stage_part = xh2[at, :] + part
            for h in range(4):
                stage[h, strided(i), :] = stage_part[:, h * 128 : (h + 1) * 128]

        loop(tiles, body)
        narrow(cotb)

    own_shard(QA)
    own_shard(QB)
    own_shard(SM)
    own_shard(OUT)
    own_shard(UP)
    own_shard(DOWN)
    pl.semaphore_wait(barrier, 7)
    g_start(SM)
    g_start(OUT)
    g_start(QB)
    g_start(UP)
    tok_copy.wait()
    first_norm()
    g_start(QA)
    g_start(DOWN)
    g_z(SM)
    g_z(OUT)
    g_z(QB)
    g_s(SM)
    g_sib(SM)
    g_f(OUT)
    small_vectors()
    constants()
    g_z(UP)
    g_s(QB)
    cot_copy.wait()
    cotangent_in()
    g_z(QA)
    first_affine()
    g_sib(QB)
    g_s(OUT)
    project_in(1)
    loop(1, lambda i: attention(1, i), 0)
    g_f(UP)
    loop(2, lambda i: attention(1, i), 1)
    g_z(DOWN)
    loop(3, lambda i: attention(1, i), 2)
    g_s(QA)
    g_sib(OUT)
    g_sib(QA)
    project_in(0)
    loop(3, lambda i: attention(0, i), 0)
    g_s(UP)
    project_out()
    second_norm(0, 2)
    g_f(DOWN)
    second_norm(2, 5)
    g_sib(UP)
    feed_up(0, 2)
    down_ours(0)
    g_s(DOWN)
    down_theirs(0)
    down_theirs(1)
    down_ours(1)
    g_sib(DOWN)
    feed_back(0, 2)
    r_1(DOWN)
    turn(a2)
    weight_grad(UP, slope, 0, 0, WIDE)
    turn(a2)
    weight_grad(UP, slope, 0, 1, WIDE)
    back_to(slope, UP, 0)
    back_to(slope, UP, 1)
    r_2(DOWN)
    second_back(0, 5)
    r_1(UP)
    back_to(dao, OUT, 0)
    back_to(dao, OUT, 1)
    loop(2, lambda i: attention_back(0, i), 0)
    r_3(DOWN)
    turn(ctx)
    weight_grad(OUT, dao, 0, 0, D)
    loop(3, lambda i: attention_back(0, i), 2)
    turn(a1)
    weight_grad(QA, dpre, 0, 0, 3 * HALF)
    loop(1, lambda i: attention_back(1, i), 0)
    r_2(UP)
    loop(3, lambda i: attention_back(1, i), 1)
    r_1(QA)
    r_1(OUT)
    back_in(0)
    back_in(1)
    turn(a1)
    weight_grad(QB, dpre, 3 * HALF, 0, 3 * HALF)
    r_3(UP)
    r_2(QA)
    first_back()
    tgrad_copy = pltpu.make_async_copy(cotb, tgrad_hbm, io_sem.at[3])
    tgrad_copy.start()
    r_1(QB)
    small_grads()
    r_3(QA)
    r_2(OUT)
    r_2(QB)
    r_1(SM)
    feed_down(0)
    r_3(OUT)
    r_3(QB)
    r_2(SM)
    r_3(SM)
    for w in (SM, QA, QB, OUT, UP, DOWN):
        g_end(w)
    r_4(QA)
    r_4(UP)
    arg_copy(UP_ARG).start()
    feed_down(1)
    narrow(tokb)
    mixed_copy = pltpu.make_async_copy(tokb, mixed_hbm, io_sem.at[2])
    mixed_copy.start()
    r_4(DOWN)
    arg_copy(DOWN_ARG).start()
    r_4(OUT)
    arg_copy(OUT_ARG).start()
    r_4(QB)
    arg_copy(QKV_ARG).start()
    r_4(SM)
    for w in (SM, QA, QB, OUT, UP, DOWN):
        r_end(w)
    for k in range(4):
        arg_copy(k).wait()
    small_copy.wait()
    mixed_copy.wait()
    tgrad_copy.wait()


def call_layer(split, tokens, frames, small, shards, cotangent):
    count = tokens.shape[0]
    any_spec = pl.BlockSpec(memory_space=pl.ANY)

    def kept(n, dtype=None):
        return [pltpu.VMEM((n, r, k), dtype or t) for r, k, t in zip(ROWS, COLS, KEPT)]

    scratch = [pltpu.VMEM((n, 128), F32) for n in PACKED]
    scratch += [pltpu.VMEM((1, n), F32) for n in SMALL] + [pltpu.VMEM((1, count // FRAMES), jnp.int32)]
    scratch += [pltpu.VMEM((PACK_ALL, 128), F32)]
    scratch += [pltpu.VMEM((2, 2, 4, 2, r, k), t) for r, k, t in zip(ROWS, COLS, KEPT)]
    scratch += kept(16, F32)
    for n in (16, 8, 4, 3):
        scratch += kept(n) + kept(n)
    rows_bf = lambda k: pltpu.VMEM((count, k), BF16)
    rows_f = lambda k: pltpu.VMEM((count, k), F32)
    scratch += [
        rows_bf(D), rows_bf(D), pltpu.VMEM((4, count, 128), F32), rows_bf(D), rows_bf(D),
        rows_f(D), rows_f(D), rows_f(128), rows_f(128),
        rows_bf(D), rows_bf(D), rows_bf(3 * D),
        pltpu.VMEM((2, len(PAIRS), count // FRAMES, 128), F32),
        rows_bf(D), rows_f(D), rows_bf(FF), rows_bf(FF),
        rows_f(D), rows_bf(3 * D), pltpu.VMEM((D, count), BF16),
    ]
    scratch += [
        pltpu.VMEM((8, 512), F32), pltpu.VMEM((8, 1024), F32), pltpu.VMEM((8, 2048), F32), pltpu.VMEM((1, 3 * D), F32),
        pltpu.VMEM((count // FRAMES, 128), F32), pltpu.VMEM((HALF, 128), BF16), pltpu.VMEM((128, HALF), BF16),
        pltpu.VMEM((8, 512), F32), pltpu.VMEM((8, 1024), F32), pltpu.VMEM((8, 2048), F32),
        pltpu.VMEM((2, 2, 8, 8, 128), F32),
    ]
    scratch += [pltpu.SemaphoreType.DMA((6, n)) for n in (5, 10, 4, 11)]
    scratch += [pltpu.SemaphoreType.DMA((13,)), pltpu.SemaphoreType.DMA((9,))]
    out_shape = [jax.ShapeDtypeStruct(tokens.shape, BF16)] * 2
    out_shape += [jax.ShapeDtypeStruct((PACK_ALL, 128), F32)]

    def body(*refs):
        layer_kernel(split, count, *refs)

    return pl.pallas_call(
        body,
        name="layer",
        out_shape=out_shape,
        in_specs=[any_spec] * 15,
        out_specs=[any_spec] * 3,
        scratch_shapes=scratch,
        compiler_params=pltpu.CompilerParams(
            collective_id=0, has_side_effects=True, vmem_limit_bytes=63 << 20
        ),
        cost_estimate=pl.CostEstimate(
            flops=2 * 3 * count * (3 * D * D + D * D + 2 * D * FF), bytes_accessed=1 << 23, transcendentals=count * FF
        ),
    )(tokens, cotangent, frames, *small, *shards)


def hand_out(mixed, tokens_grad, grads):
    any_spec = pl.BlockSpec(memory_space=pl.ANY)
    vmem = pl.BlockSpec(memory_space=pltpu.VMEM)

    def body(mixed_in, tgrad_in, grads_in, *refs):
        outs, (mixed_v, tgrad_v, grads_v, in_sem, out_sem) = refs[:14], refs[14:]
        smalls, big = outs[2:10], (outs[0], outs[1]) + tuple(outs[10:])
        reads = [
            pltpu.make_async_copy(src, dst, in_sem.at[k])
            for k, (src, dst) in enumerate(((mixed_in, mixed_v), (tgrad_in, tgrad_v), (grads_in, grads_v)))
        ]
        parts = [mixed_v, tgrad_v] + [grads_v.at[pl.ds(PACK[k], PACKED[k])] for k in range(4)]
        writes = [pltpu.make_async_copy(src, dst, out_sem.at[k]) for k, (src, dst) in enumerate(zip(parts, big))]
        for copy in reads:
            copy.start()
        for k in range(3):
            reads[k].wait()
            for copy in writes[2:] if k == 2 else writes[k : k + 1]:
                copy.start()
        for p, n in enumerate(SMALL):
            smalls[p][...] = grads_v[PACK_SMALL + p : PACK_SMALL + p + 1, 0:n]
        for copy in writes:
            copy.wait()

    row_shapes = [jax.ShapeDtypeStruct(mixed.shape, BF16)] * 2
    small_shapes = [jax.ShapeDtypeStruct((1, n), F32) for n in SMALL]
    shard_shapes = [jax.ShapeDtypeStruct((n, 128), F32) for n in PACKED]
    return pl.pallas_call(
        body,
        name="hand_out",
        out_shape=row_shapes + small_shapes + shard_shapes,
        in_specs=[any_spec] * 3,
        out_specs=[any_spec] * 2 + [vmem] * 8 + [any_spec] * 4,
        scratch_shapes=[
            pltpu.VMEM(mixed.shape, BF16), pltpu.VMEM(mixed.shape, BF16), pltpu.VMEM(grads.shape, F32),
            pltpu.SemaphoreType.DMA((3,)), pltpu.SemaphoreType.DMA((6,)),
        ],
    )(mixed, tokens_grad, grads)


def local(split, tokens, frames, g1, b1, wqkv, bqv, wo, bo, g2, b2, w1, b1f, w2, b2f, cotangent):
    spot = lax.axis_index("fsdp") // split

    def block(values):
        if split == 1:
            return values
        n = values.shape[0]
        every = lax.all_gather(values, "fsdp", axis=0, tiled=True)
        return lax.dynamic_slice(every, (spot * split * n,), (split * n,))

    def owned(values):
        if split == 1:
            return values
        n = values.shape[0]
        spread = lax.dynamic_update_slice(jnp.zeros((8 * n,), F32), values, (spot * n,))
        return lax.psum_scatter(spread, "fsdp", scatter_dimension=0, tiled=True)

    small = [block(v).reshape(1, -1) for v in (g1, b1, bqv, bo, g2, b2, b1f, b2f)]
    shards = [block(v).reshape(-1, 128) for v in (wqkv, wo, w1, w2)]
    outs = hand_out(*call_layer(split, tokens, frames.reshape(1, -1), small, shards, cotangent))
    mixed, tokens_grad = outs[:2]
    dg1, db1, dbqv, dbo, dg2, db2, db1f, db2f = [owned(v.reshape(-1)) for v in outs[2:10]]
    dwqkv, dwo, dw1, dw2 = [owned(v.reshape(-1)) for v in outs[10:]]
    return (mixed, tokens_grad, dg1, db1, dwqkv, dbqv, dwo, dbo, dg2, db2, dw1, db1f, dw2, db2f)


def solution(mesh):
    split = mesh.shape["fsdp"] // 8
    flat, rows = P(("dp", "fsdp")), P(("dp", "fsdp"), None)

    def body(*args):
        return local(split, *args)

    return jax.shard_map(
        body,
        mesh=mesh,
        in_specs=(rows,) + (flat,) * 13 + (rows,),
        out_specs=(rows, rows) + (flat,) * 12,
        check_vma=False,
    )
```

```python
import math

import jax
import jax.numpy as jnp
from jax import lax
from jax.experimental import pallas as pl
from jax.experimental.pallas import tpu as pltpu
from jax.sharding import PartitionSpec as P

D = 512
HEADS = 8
HEAD_DIM = 64
FF = 2048
FRAMES = 5
EPSILON = 1e-05
PAIRS = [(t, u) for t in range(FRAMES) for u in range(t + 1)]

F32 = jnp.float32
BF16 = jnp.bfloat16
MESH = pl.DeviceIdType.MESH

SM, QA, QB, OUT, UP, DOWN = range(6)
ROWS = (8, 16, 16, 16, 16, 64)
COLS = (128, 3 * D // 2, 3 * D // 2, D, FF, D)
KEPT = (F32, BF16, BF16, BF16, BF16, BF16)
DIRECT = (SM, QA, QB,)
HALF = D // 2
WIDE = FF // 2
GROUP = HEADS // 2
QKV_ARG, OUT_ARG, UP_ARG, DOWN_ARG = range(4)
ARG = (None, QKV_ARG, QKV_ARG, OUT_ARG, UP_ARG, DOWN_ARG)
PACKED = (192, 64, 256, 256)
PACK = (0, 192, 256, 512)
PACK_SMALL, PACK_ALL = 768, 776
SMALL = (16, 16, 32, 16, 16, 16, 64, 16)
GAIN1, BIAS1, QVB, OUTB, GAIN2, BIAS2, UPB, DOWNB = range(8)

TILE = 192
CHUNK = 64


def dot(left, right):
    return lax.dot_general(left, right, (((1,), (0,)), ((), ())), preferred_element_type=F32)


def dot_nt(left, right):
    return lax.dot_general(left, right, (((1,), (1,)), ((), ())), preferred_element_type=F32)


def dot_tn(left, right):
    return lax.dot_general(left, right, (((0,), (0,)), ((), ())), preferred_element_type=F32)


def iota(shape, dim):
    return lax.broadcasted_iota(jnp.int32, shape, dim)


def fold(values):
    rows, cols = values.shape
    return jnp.sum(values.reshape(rows // 8, 8, cols), axis=0)


def split_two(values):
    high = values.astype(BF16)
    return high, (values - high.astype(F32)).astype(BF16)


def layer_kernel(split, count, *refs):
    refs = list(refs)

    def take(n):
        head = refs[:n]
        del refs[:n]
        return head

    tok_hbm, cot_hbm, frames_hbm = take(3)
    small_hbm = take(8)
    shard_hbm = take(4)
    mixed_hbm, tgrad_hbm, grads_hbm = take(3)
    shard_in = take(4)
    small_in = take(8)
    (frames_in,) = take(1)
    (grads,) = take(1)
    whole = take(6)
    acc = take(6)
    sib_out, sib_in = take(6), take(6)
    two_out, two_in = take(6), take(6)
    one_out, one_in = take(6), take(6)
    zed_out, zed_in = take(6), take(6)
    (tokb, cotb, stage, xt, dm, xh1, xh2, rs1, rs2, a1, a2, qkv, prob, ctx, x1, act, slope, wide, dpre, turned) = take(20)
    (vec16, vecqv, vecup, biasq, living, pick, pick_t, gs16, gsqv, gsup, sums) = take(11)
    (gsend, grecv, rsend, rrecv, io_sem, small_sem) = take(6)

    dao = cotb

    seqs = count // FRAMES
    dp = lax.axis_index("dp")
    fs = lax.axis_index("fsdp")
    x, c = dp // 2, dp % 2
    group, rest = fs // split, fs % split
    z, y = group // 2, group % 2

    plane = (c + x + y) % 2

    def core_at(x_, y_):
        return (plane + x_ + y_) % 2

    def device(x_, c_, z_, y_):
        return (x_ * 2 + c_, (z_ * 2 + y_) * split + rest)

    first = x + plane * (y - x)
    second = y + plane * (x - y)

    def to_xy(f_, s_):
        return f_ + plane * (s_ - f_), s_ + plane * (f_ - s_)

    def peer(f_, s_):
        x_, y_ = to_xy(f_, s_)
        return device(x_, core_at(x_, y_), z, y_)

    sibling = device(x, 1 - c, z, y)
    first_dev = peer(1 - first, second)
    second_dev = peer(first, 1 - second)
    across_dev = peer(1 - first, 1 - second)
    zeds = (z + 1 - 2 * (z % 2), (z + 2) % 4, 3 - z)
    zed_dev = [device(x, c, zk, y) for zk in zeds]

    barrier = pltpu.get_barrier_semaphore()
    for dev in [sibling, first_dev, second_dev, across_dev] + zed_dev:
        pl.semaphore_signal(barrier, inc=1, device_id=dev, device_id_type=MESH)
    small_copy_in = [pltpu.make_async_copy(small_hbm[p], small_in[p], small_sem.at[p]) for p in range(8)]
    shard_copy = [pltpu.make_async_copy(shard_hbm[k], shard_in[k], io_sem.at[4 + k]) for k in range(4)]
    frames_copy = pltpu.make_async_copy(frames_hbm, frames_in, small_sem.at[8])
    tok_copy = pltpu.make_async_copy(tok_hbm, tokb, io_sem.at[0])
    cot_copy = pltpu.make_async_copy(cot_hbm, cotb, io_sem.at[1])
    for copy in small_copy_in + shard_copy + [tok_copy, frames_copy, cot_copy]:
        copy.start()

    def shard(w, f_, s_, z_):
        x_, y_ = to_xy(f_, s_)
        return whole[w].at[x_, core_at(x_, y_), z_, y_]

    def line(w, f_, s_):
        x_, y_ = to_xy(f_, s_)
        return whole[w].at[x_, core_at(x_, y_), :, y_]

    def gcopy(w, sent, got, ref, dev):
        return pltpu.make_async_remote_copy(
            src_ref=ref, dst_ref=ref, send_sem=gsend.at[w, sent], recv_sem=grecv.at[w, got], device_id=dev, device_id_type=MESH
        )

    def cols_of(w):
        if w in (QA, QB):
            return [(4 * p + 2 * (w - QA) + b, 2 * p + b) for p in range(3) for b in range(2)]
        return [(k, k) for k in range(COLS[w] // 128)]

    def own_shard(w):
        if w == SM:
            whole[w][x, c, z, y] = jnp.zeros((8, 128), F32)
            for p, n in enumerate(SMALL):
                small_copy_in[p].wait()
                whole[w][x, c, z, y, p : p + 1, 0:n] = small_in[p][...].astype(BF16).astype(F32)
        else:
            if w != QB:
                shard_copy[ARG[w]].wait()
            step = PACKED[ARG[w]] // ROWS[w]
            for k, to in cols_of(w):
                part = shard_in[ARG[w]][pl.ds(k, ROWS[w], stride=step), :]
                whole[w][x, c, z, y, :, to * 128 : (to + 1) * 128] = part.astype(BF16)

    def hand_on(w, ref, spot):
        if w in DIRECT:
            gcopy(w, 1, 3, ref, first_dev).start()
            gcopy(w, 2, 7, ref, second_dev).start()
            gcopy(w, 3, 8, ref, across_dev).start()
        else:
            gcopy(w, 1, 3 + spot, ref, first_dev).start()
            gcopy(w, 2, 7, ref, second_dev).start()

    def to_sibling(w, f_, s_):
        gcopy(w, 4, 9, line(w, f_, s_), sibling).start()

    def g_start(w):
        ref = shard(w, first, second, z)
        for k in range(3):
            gcopy(w, 0, k, ref, zed_dev[k]).start()
        hand_on(w, ref, z)

    def g_z(w):
        for k in range(3):
            ref = shard(w, first, second, zeds[k])
            gcopy(w, 0, k, ref, zed_dev[k]).wait_recv()
            hand_on(w, ref, zeds[k])
        to_sibling(w, first, second)

    def g_f(w):
        for k in range(4):
            ref = shard(w, 1 - first, second, k)
            gcopy(w, 1, 3 + k, ref, first_dev).wait_recv()
            gcopy(w, 2, 8, ref, second_dev).start()
        to_sibling(w, 1 - first, second)

    def g_s(w):
        if w in DIRECT:
            gcopy(w, 1, 3, line(w, 1 - first, second), first_dev).wait_recv()
            to_sibling(w, 1 - first, second)
        gcopy(w, 2, 7, line(w, first, 1 - second), second_dev).wait_recv()
        to_sibling(w, first, 1 - second)
        gcopy(w, 2, 8, line(w, 1 - first, 1 - second), second_dev).wait_recv()
        to_sibling(w, 1 - first, 1 - second)

    def g_sib(w):
        ref = whole[w].at[:, 1 - c]
        gcopy(w, 4, 9, ref, sibling).wait_recv()

    def g_end(w):
        gcopy(w, 0, 0, zed_out[w], sibling).wait_send()
        four = line(w, first, second)
        gcopy(w, 1, 3, four, sibling).wait_send()
        if w in DIRECT:
            gcopy(w, 2, 7, four, sibling).wait_send()
            gcopy(w, 3, 8, four, sibling).wait_send()
        else:
            gcopy(w, 2, 7, two_out[w], sibling).wait_send()
        gcopy(w, 4, 9, sib_out[w], sibling).wait_send()

    def loop(n, body, start=0):
        def step(i, carry):
            body(i)
            return carry

        lax.fori_loop(start, n, step, 0)

    def place(f_, s_, z_):
        x_, y_ = to_xy(f_, s_)
        return x_ * 8 + z_ * 2 + y_

    def rcopy(w, sent, got, src, dst, dev):
        return pltpu.make_async_remote_copy(
            src_ref=src, dst_ref=dst, send_sem=rsend.at[w, sent], recv_sem=rrecv.at[w, got], device_id=dev, device_id_type=MESH
        )

    def sib_copy(w, at, n):
        return rcopy(w, 0, 0, sib_out[w].at[pl.ds(at, n)], sib_in[w].at[pl.ds(at, n)], sibling)

    def two_copy(w, k, got):
        return rcopy(w, 1, got, two_out[w].at[k], two_in[w].at[k], second_dev)

    def one_copy(w, k):
        return rcopy(w, 2, 6 + k, one_out[w].at[k], one_in[w].at[k], first_dev)

    def zed_copy(w, k):
        return rcopy(w, 3, 10, zed_out[w].at[k], zed_in[w].at[k], zed_dev[k])

    def chip_sum(w, j):
        return acc[w][j] + sib_in[w][j].astype(F32)

    def r_1(w):
        sib_copy(w, 0, 16).wait_recv()
        if w == SM:
            for k in range(4):
                one_out[w][k] = chip_sum(w, place(1 - first, second, k))
                rcopy(w, 2, 6, one_out[w].at[k], one_in[w].at[k], first_dev).start()
                two_out[w][k] = chip_sum(w, place(first, 1 - second, k))
                two_copy(w, k, 5).start()
                two_out[w][4 + k] = chip_sum(w, place(1 - first, 1 - second, k))
                rcopy(w, 1, 1, two_out[w].at[4 + k], two_in[w].at[4 + k], across_dev).start()
            return

        def step(k, got):
            j = place(k // 4, 1 - second, k % 4)
            two_out[w][k] = chip_sum(w, j).astype(KEPT[w])
            two_copy(w, k, got).start()

        loop(4, lambda i: step(4 * (1 - first) + i, 1 + i))
        loop(4, lambda i: step(4 * first + i, 5))

    def r_2(w):
        def step(i):
            k = (z + 1 + i) % 4
            j = place(1 - first, second, k)
            slot = (1 - first) * 4 + k
            two_copy(w, slot, 1 + k).wait_recv()
            total = chip_sum(w, j) + two_in[w][slot].astype(F32)
            one_out[w][k] = total.astype(KEPT[w])
            one_copy(w, k).start()

        loop(4, step)

    def line_sum(w, k):
        j = place(first, second, k)
        total = chip_sum(w, j) + one_in[w][k].astype(F32)
        if w == SM:
            return total + two_in[w][k] + two_in[w][4 + k]
        return total + two_in[w][4 * first + k].astype(F32)

    def r_3(w):
        if w == SM:
            rcopy(w, 2, 6, one_in[w], one_in[w], first_dev).wait_recv()
            for got, at in ((5, 0), (1, 4)):
                part = two_in[w].at[pl.ds(at, 4)]
                rcopy(w, 1, got, part, part, second_dev).wait_recv()
        else:
            line_in = two_in[w].at[pl.ds(4 * first, 4)]
            rcopy(w, 1, 5, line_in, line_in, second_dev).wait_recv()
        for k in range(3):
            if w != SM:
                one_copy(w, zeds[k]).wait_recv()
            zed_out[w][k] = line_sum(w, zeds[k]).astype(KEPT[w])
            zed_copy(w, k).start()

    def grad_copy(at, rows, k):
        return pltpu.make_async_copy(grads.at[pl.ds(at, rows)], grads_hbm.at[pl.ds(at, rows)], io_sem.at[8 + k])

    def arg_copy(k):
        return grad_copy(PACK[k], PACKED[k], k)

    small_copy = grad_copy(PACK_SMALL, 8, 4)

    def r_4(w):
        if w != SM:
            one_copy(w, z).wait_recv()
        total = line_sum(w, z)
        rcopy(w, 3, 10, zed_in[w], zed_in[w], sibling).wait_recv()
        for k in range(3):
            total = total + zed_in[w][k].astype(F32)
        if w == SM:
            grads[PACK_SMALL:PACK_ALL, :] = total
            small_copy.start()
        else:
            step = PACKED[ARG[w]] // ROWS[w]
            for k, at in cols_of(w):
                grads[pl.ds(PACK[ARG[w]] + k, ROWS[w], stride=step), :] = total[:, at * 128 : (at + 1) * 128]

    def r_end(w):
        sib_copy(w, 0, 16).wait_send()
        rcopy(w, 1, 5, two_out[w], two_in[w], sibling).wait_send()
        rcopy(w, 2, 6, one_out[w], one_in[w], sibling).wait_send()
        rcopy(w, 3, 10, zed_out[w], zed_in[w], sibling).wait_send()

    tiles = count // TILE
    per_frame = seqs // TILE

    def tile_rows(i):
        return pl.ds(pl.multiple_of(i * TILE, TILE), TILE)

    def strided(i):
        return pl.ds(i // per_frame + FRAMES * TILE * (i % per_frame), TILE, stride=FRAMES)

    def widen(src):
        def body(i):
            for h in range(4):
                stage[h, tile_rows(i), :] = src[tile_rows(i), h * 128 : (h + 1) * 128].astype(F32)

        loop(tiles, body)

    def narrow(dst):
        def body(i):
            for h in range(4):
                dst[tile_rows(i), h * 128 : (h + 1) * 128] = stage[h, tile_rows(i), :].astype(BF16)

        loop(tiles, body)

    def center(values):
        mean = jnp.mean(values, axis=-1, keepdims=True)
        centered = values - mean
        root = lax.rsqrt(jnp.mean(centered * centered, axis=-1, keepdims=True) + EPSILON)
        return centered * root, root

    def constants():
        lane, row = iota((HALF, 128), 1), iota((HALF, 128), 0)
        pick[...] = jnp.where((row // HEAD_DIM == lane % GROUP) & (lane < 2 * GROUP), 1.0, 0.0).astype(BF16)
        lane, row = iota((128, HALF), 1), iota((128, HALF), 0)
        pick_t[...] = jnp.where((lane // HEAD_DIM == row % GROUP) & (row < 2 * GROUP), 1.0, 0.0).astype(BF16)
        frames_copy.wait()
        same = iota((seqs, seqs), 0) == iota((seqs, seqs), 1)
        wide_frames = jnp.broadcast_to(frames_in[...].astype(F32), (seqs, seqs))
        spread = jnp.where(same, wide_frames, 0.0).astype(BF16)
        living[...] = dot(spread, jnp.ones((seqs, 128), BF16))
        gs16[...] = jnp.zeros_like(gs16)
        gsqv[...] = jnp.zeros_like(gsqv)
        gsup[...] = jnp.zeros_like(gsup)

    def first_norm():
        widen(tokb)

        def body(i):
            values = jnp.concatenate([stage[h, strided(i), :] for h in range(4)], axis=1)
            xt[tile_rows(i), :] = values.astype(BF16)
            hat, root = center(values)
            xh1[tile_rows(i), :] = hat
            rs1[tile_rows(i), :] = jnp.broadcast_to(root, (TILE, 128))

        loop(tiles, body)

    def cotangent_in():
        widen(cotb)

        def body(i):
            values = jnp.concatenate([stage[h, strided(i), :] for h in range(4)], axis=1)
            dm[tile_rows(i), :] = values.astype(BF16)
            gs16[DOWNB : DOWNB + 1, :] += jnp.sum(fold(values), axis=0, keepdims=True)

        loop(tiles, body)

    def small_vectors():
        raw = whole[SM][...].reshape(256, 128).astype(BF16)
        for n, dst in ((16, vec16), (32, vecqv), (64, vecup)):
            width = 32 * n
            for at in range(0, width, 512):
                near = iota((128, 512), 0) == (iota((128, 512), 1) + at) % n
                spread = dot(raw, jnp.where(near, 1.0, 0.0).astype(BF16))
                mine = iota((256, 512), 0) // 8 == (iota((256, 512), 1) + at) // n
                dst[:, at : at + 512] = jnp.sum(jnp.where(mine, spread, 0.0).reshape(32, 8, 512), axis=0)
        biasq[...] = jnp.zeros_like(biasq)
        for h in range(2):
            for part in range(2):
                at = 3 * HALF * h + 2 * HALF * part
                biasq[:, at : at + HALF] = vecqv[QVB : QVB + 1, part * D + h * HALF : part * D + (h + 1) * HALF]

    def small_grads():
        for n, src in ((16, gs16), (32, gsqv), (64, gsup)):
            width = 32 * n
            for at in range(0, width, 512):
                mine = iota((256, 512), 0) // 8 == (iota((256, 512), 1) + at) // n
                values = jnp.broadcast_to(src[:, at : at + 512][None], (32, 8, 512)).reshape(256, 512)
                high, low = split_two(jnp.where(mine, values, 0.0))
                near = jnp.where(iota((128, 512), 0) == (iota((128, 512), 1) + at) % n, 1.0, 0.0).astype(BF16)
                part = dot_nt(high, near) + dot_nt(low, near)
                total = part if n == 16 and at == 0 else total + part
        sums[...] = total.reshape(2, 2, 4, 2, 8, 128)
        for h in range(2):
            for q in range(2):
                for own in range(2):
                    part = sums[h, core_at(h, q) if own else 1 - core_at(h, q), :, q]
                    for k in range(4):
                        (acc if own else sib_out)[SM][8 * h + 2 * k + q] = part[k]
            sib_copy(SM, 8 * h, 8).start()

    def first_affine():
        gain, bias = vec16[GAIN1 : GAIN1 + 1, :], vec16[BIAS1 : BIAS1 + 1, :]

        def body(i):
            a1[tile_rows(i), :] = (xh1[tile_rows(i), :] * gain + bias).astype(BF16)

        loop(tiles, body)

    def cols(n, width):
        return pl.ds(pl.multiple_of(n * width, width), width)

    def matrix_cols(w, n, width):
        return whole[w][:, :, :, :, :, cols(n, width)].reshape(32 * ROWS[w], width)

    def matrix(w):
        return whole[w][...].reshape(32 * ROWS[w], COLS[w])

    def project_in(h):
        at = slice(3 * HALF * h, 3 * HALF * (h + 1))
        r = dot(a1[...], matrix(QA + h)) + biasq[:, at]
        qkv[:, at] = r.astype(BF16)

    def frame_rows(t, i):
        return pl.ds(pl.multiple_of(t * seqs + i * CHUNK, CHUNK), CHUNK)

    def heads_of(h, i, part):
        at = (3 * h + part) * HALF
        return [qkv[frame_rows(t, i), at : at + HALF].astype(F32) for t in range(FRAMES)]

    def spread_heads(parts):
        lanes = iota((CHUNK, 128), 1)
        mixed_parts = []
        for part in parts:
            high, low = split_two(part)
            mixed_parts.append(jnp.where(lanes < GROUP, high.astype(F32), low.astype(F32)).astype(BF16))
        return dot(jnp.concatenate(mixed_parts, axis=0), pick_t[...])

    def rows_of(values, k):
        return values[k * CHUNK : (k + 1) * CHUNK]

    def attention(h, i):
        q, k_, v = heads_of(h, i, 0), heads_of(h, i, 1), heads_of(h, i, 2)
        halves = [split_two(q[t] * k_[u]) for t, u in PAIRS]
        high = jnp.concatenate([h for h, _ in halves], axis=0)
        low = jnp.concatenate([l for _, l in halves], axis=0)
        scores = (dot(high, pick[...]) + dot(low, pick[...])) * (1.0 / math.sqrt(HEAD_DIM))
        live = living[pl.ds(pl.multiple_of(i * CHUNK, CHUNK), CHUNK), :]
        weights = []
        for t in range(FRAMES):
            row = [rows_of(scores, PAIRS.index((t, u))) for u in range(t + 1)]
            row = [jnp.where(u < live, part, -1e30) for u, part in enumerate(row)]
            top = row[0]
            for part in row[1:]:
                top = jnp.maximum(top, part)
            row = [jnp.exp(part - top) for part in row]
            total = row[0]
            for part in row[1:]:
                total = total + part
            weights += [part / total for part in row]
        for k, part in enumerate(weights):
            prob[h, k, pl.ds(pl.multiple_of(i * CHUNK, CHUNK), CHUNK), :] = part
        spread = spread_heads(weights)
        for t in range(FRAMES):
            total = rows_of(spread, PAIRS.index((t, 0))) * v[0]
            for u in range(1, t + 1):
                total = total + rows_of(spread, PAIRS.index((t, u))) * v[u]
            ctx[frame_rows(t, i), h * HALF : (h + 1) * HALF] = total.astype(BF16)

    def attention_back(h, i):
        v = heads_of(h, i, 2)
        g = [wide[frame_rows(t, i), h * HALF : (h + 1) * HALF] for t in range(FRAMES)]
        base = 3 * HALF * h
        products = jnp.concatenate([(g[t] * v[u]).astype(BF16) for t, u in PAIRS], axis=0)
        slopes = dot(products, pick[...])
        weights = [prob[h, k, pl.ds(pl.multiple_of(i * CHUNK, CHUNK), CHUNK), :] for k in range(len(PAIRS))]
        scaled = []
        for t in range(FRAMES):
            ks = [PAIRS.index((t, u)) for u in range(t + 1)]
            mean = weights[ks[0]] * rows_of(slopes, ks[0])
            for k in ks[1:]:
                mean = mean + weights[k] * rows_of(slopes, k)
            scaled += [weights[k] * (rows_of(slopes, k) - mean) * (1.0 / math.sqrt(HEAD_DIM)) for k in ks]
        spread_p = spread_heads(weights)
        for u in range(FRAMES):
            total = None
            for t in range(u, FRAMES):
                part = rows_of(spread_p, PAIRS.index((t, u))) * g[t]
                total = part if total is None else total + part
            low = total.astype(BF16)
            dpre[frame_rows(u, i), base + 2 * HALF : base + 3 * HALF] = low
            gsqv[QVB : QVB + 1, D + h * HALF : D + (h + 1) * HALF] += jnp.sum(fold(low.astype(F32)), axis=0, keepdims=True)
        q, k_ = heads_of(h, i, 0), heads_of(h, i, 1)
        spread_s = spread_heads(scaled)
        for t in range(FRAMES):
            total = None
            for u in range(t + 1):
                part = rows_of(spread_s, PAIRS.index((t, u))) * k_[u]
                total = part if total is None else total + part
            low = total.astype(BF16)
            dpre[frame_rows(t, i), base : base + HALF] = low
            gsqv[QVB : QVB + 1, h * HALF : (h + 1) * HALF] += jnp.sum(fold(low.astype(F32)), axis=0, keepdims=True)
        for u in range(FRAMES):
            total = None
            for t in range(u, FRAMES):
                part = rows_of(spread_s, PAIRS.index((t, u))) * q[t]
                total = part if total is None else total + part
            dpre[frame_rows(u, i), base + HALF : base + 2 * HALF] = total.astype(BF16)

    def project_out():
        bias = vec16[OUTB : OUTB + 1, :]
        for n in range(2):
            at = slice(n * 256, (n + 1) * 256)
            r = dot(ctx[...], whole[OUT][:, :, :, :, :, at].reshape(D, 256))
            x1[:, at] = xt[:, at].astype(F32) + r + bias[:, at]

    def second_norm(start, stop):
        gain, bias = vec16[GAIN2 : GAIN2 + 1, :], vec16[BIAS2 : BIAS2 + 1, :]

        def body(i):
            hat, root = center(x1[tile_rows(i), :])
            xh2[tile_rows(i), :] = hat
            rs2[tile_rows(i), :] = jnp.broadcast_to(root, (TILE, 128))
            a2[tile_rows(i), :] = (hat * gain + bias).astype(BF16)

        loop(stop, body, start)

    def feed_up(start, stop):
        k0 = math.sqrt(2.0 / math.pi)
        k1 = k0 * 0.044715

        def body(n):
            f = dot(a2[...], matrix_cols(UP, n, WIDE)) + vecup[UPB : UPB + 1, cols(n, WIDE)]
            square = f * f
            half = 0.5 + 0.5 * jnp.tanh(f * (k0 + k1 * square))
            act[:, cols(n, WIDE)] = (f * half).astype(BF16)
            grow = half + (f * (half - half * half)) * (2.0 * k0 + 6.0 * k1 * square)
            slope[:, cols(n, WIDE)] = grow.astype(BF16)

        loop(stop, body, start)

    def feed_down(n):
        bias = vec16[DOWNB : DOWNB + 1, :]
        at = slice(n * 256, (n + 1) * 256)
        r = dot(act[...], whole[DOWN][:, :, :, :, :, at].reshape(FF, 256))
        r = r + x1[:, at] + bias[:, at]
        for t in range(FRAMES):
            for h in range(2):
                stage[2 * n + h, pl.ds(t, seqs, stride=FRAMES), :] = r[t * seqs : (t + 1) * seqs, h * 128 : (h + 1) * 128]

    def turn(left):
        for h in range(2):
            for k in range(2):
                at = h * 256 + k * 128
                part = jnp.transpose(left[:, at : at + 128]).reshape(4, 2, 16, count)
                for q in range(2):
                    turned[(k + core_at(h, q) + 1) % 2, h, :, q] = part[:, q]

    def weight_grad(w, right, base, n, width):
        at = slice(n * width, (n + 1) * width)
        r = dot(turned[...].reshape(D, count), right[:, base + n * width : base + (n + 1) * width])
        sib_out[w][:, :, at] = r[:HALF].reshape(16, ROWS[w], width).astype(BF16)
        rcopy(w, 0, 0, sib_out[w].at[:, :, at], sib_in[w].at[:, :, at], sibling).start()
        acc[w][:, :, at] = r[HALF:].reshape(16, ROWS[w], width)

    def act_of(h, own):
        core = core_at(h, 0) if own else 1 - core_at(h, 0)
        even = act[:, pl.ds(pl.multiple_of(h * 1024 + core * 512, 512), 512)]
        odd = act[:, pl.ds(pl.multiple_of(h * 1024 + (1 - core) * 512, 512), 512)]
        return jnp.where(iota((count, 512), 1) % 128 < 64, even, odd)

    def down_theirs(h):
        r = dot_tn(act_of(h, False), dm[...])
        sib_out[DOWN][8 * h : 8 * h + 8] = r.reshape(8, 64, D).astype(BF16)
        sib_copy(DOWN, 8 * h, 8).start()

    def down_ours(h):
        acc[DOWN][8 * h : 8 * h + 8] = dot_tn(act_of(h, True), dm[...]).reshape(8, 64, D)

    def feed_back(start, stop):
        def body(n):
            part = whole[DOWN][n].reshape(WIDE, D)
            low = (dot_nt(dm[...], part) * slope[:, cols(n, WIDE)].astype(F32)).astype(BF16)
            slope[:, cols(n, WIDE)] = low
            gsup[UPB : UPB + 1, cols(n, WIDE)] = jnp.sum(fold(low.astype(F32)), axis=0, keepdims=True)

        loop(stop, body, start)

    def back_to(left, w, h):
        wide[:, h * 256 : (h + 1) * 256] = dot_nt(left[...], whole[w][h].reshape(256, COLS[w]))

    def back_in(h):
        r = dot_nt(dpre[:, : 3 * HALF], whole[QA][h].reshape(256, 3 * HALF))
        r = r + dot_nt(dpre[:, 3 * HALF :], whole[QB][h].reshape(256, 3 * HALF))
        wide[:, h * 256 : (h + 1) * 256] = r

    def norm_back(grads, hat, root, gain, gain_at, bias_at):
        gs16[gain_at : gain_at + 1, :] += jnp.sum(fold(grads * hat), axis=0, keepdims=True)
        gs16[bias_at : bias_at + 1, :] += jnp.sum(fold(grads), axis=0, keepdims=True)
        scaled = grads * gain
        mean = jnp.mean(scaled, axis=-1, keepdims=True)
        along = jnp.mean(scaled * hat, axis=-1, keepdims=True)
        return (scaled - mean - hat * along) * root

    def second_back(start, stop):
        gain = vec16[GAIN2 : GAIN2 + 1, :]

        def body(i):
            at = tile_rows(i)
            part = norm_back(wide[at, :], xh2[at, :], rs2[at, 0:1], gain, GAIN2, BIAS2)
            total = dm[at, :].astype(F32) + part
            xh2[at, :] = total
            low = total.astype(BF16)
            dao[at, :] = low
            gs16[OUTB : OUTB + 1, :] += jnp.sum(fold(low.astype(F32)), axis=0, keepdims=True)

        loop(stop, body, start)

    def first_back():
        gain = vec16[GAIN1 : GAIN1 + 1, :]

        def body(i):
            at = tile_rows(i)
            part = norm_back(wide[at, :], xh1[at, :], rs1[at, 0:1], gain, GAIN1, BIAS1)
            stage_part = xh2[at, :] + part
            for h in range(4):
                stage[h, strided(i), :] = stage_part[:, h * 128 : (h + 1) * 128]

        loop(tiles, body)
        narrow(cotb)

    own_shard(QA)
    own_shard(QB)
    own_shard(SM)
    own_shard(OUT)
    own_shard(UP)
    own_shard(DOWN)
    pl.semaphore_wait(barrier, 7)
    g_start(SM)
    g_start(OUT)
    g_start(QB)
    g_start(UP)
    tok_copy.wait()
    first_norm()
    g_start(QA)
    constants()
    g_start(DOWN)
    g_z(OUT)
    g_z(QB)
    g_z(SM)
    g_z(UP)
    g_s(QB)
    g_s(SM)
    cot_copy.wait()
    cotangent_in()
    g_z(QA)
    g_sib(SM)
    small_vectors()
    g_sib(QB)
    g_f(OUT)
    first_affine()
    g_f(UP)
    project_in(1)
    loop(2, lambda i: attention(1, i), 0)
    g_s(QA)
    g_z(DOWN)
    loop(3, lambda i: attention(1, i), 2)
    g_s(OUT)
    g_sib(QA)
    project_in(0)
    loop(3, lambda i: attention(0, i), 0)
    g_s(UP)
    g_sib(OUT)
    project_out()
    second_norm(0, 5)
    g_f(DOWN)
    g_sib(UP)
    feed_up(0, 1)
    down_ours(0)
    down_theirs(0)
    feed_up(1, 2)
    g_s(DOWN)
    down_theirs(1)
    down_ours(1)
    g_sib(DOWN)
    feed_back(0, 1)
    r_1(DOWN)
    feed_back(1, 2)
    turn(a2)
    weight_grad(UP, slope, 0, 0, WIDE)
    turn(a2)
    weight_grad(UP, slope, 0, 1, WIDE)
    r_2(DOWN)
    back_to(slope, UP, 0)
    back_to(slope, UP, 1)
    second_back(0, 2)
    r_1(UP)
    second_back(2, 5)
    back_to(dao, OUT, 0)
    back_to(dao, OUT, 1)
    loop(3, lambda i: attention_back(0, i), 0)
    turn(a1)
    weight_grad(QA, dpre, 0, 0, 3 * HALF)
    r_3(DOWN)
    r_2(UP)
    loop(3, lambda i: attention_back(1, i), 0)
    r_1(QA)
    turn(ctx)
    weight_grad(OUT, dao, 0, 0, D)
    turn(a1)
    weight_grad(QB, dpre, 3 * HALF, 0, 3 * HALF)
    r_3(UP)
    r_1(OUT)
    back_in(0)
    back_in(1)
    r_2(QA)
    r_1(QB)
    first_back()
    tgrad_copy = pltpu.make_async_copy(cotb, tgrad_hbm, io_sem.at[3])
    tgrad_copy.start()
    r_2(OUT)
    small_grads()
    r_3(QA)
    r_2(QB)
    r_1(SM)
    r_3(OUT)
    r_3(QB)
    r_3(SM)
    r_4(DOWN)
    arg_copy(DOWN_ARG).start()
    feed_down(0)
    for w in (SM, QA, QB, OUT, UP, DOWN):
        g_end(w)
    r_4(QA)
    r_4(UP)
    arg_copy(UP_ARG).start()
    r_4(OUT)
    arg_copy(OUT_ARG).start()
    feed_down(1)
    narrow(tokb)
    mixed_copy = pltpu.make_async_copy(tokb, mixed_hbm, io_sem.at[2])
    mixed_copy.start()
    r_4(QB)
    arg_copy(QKV_ARG).start()
    r_4(SM)
    for w in (SM, QA, QB, OUT, UP, DOWN):
        r_end(w)
    for k in range(4):
        arg_copy(k).wait()
    small_copy.wait()
    mixed_copy.wait()
    tgrad_copy.wait()


def call_layer(split, tokens, frames, small, shards, cotangent):
    count = tokens.shape[0]
    any_spec = pl.BlockSpec(memory_space=pl.ANY)

    def kept(n, dtype=None):
        return [pltpu.VMEM((n, r, k), dtype or t) for r, k, t in zip(ROWS, COLS, KEPT)]

    scratch = [pltpu.VMEM((n, 128), F32) for n in PACKED]
    scratch += [pltpu.VMEM((1, n), F32) for n in SMALL] + [pltpu.VMEM((1, count // FRAMES), jnp.int32)]
    scratch += [pltpu.VMEM((PACK_ALL, 128), F32)]
    scratch += [pltpu.VMEM((2, 2, 4, 2, r, k), t) for r, k, t in zip(ROWS, COLS, KEPT)]
    scratch += kept(16, F32)
    for n in (16, 8, 4, 3):
        scratch += kept(n) + kept(n)
    rows_bf = lambda k: pltpu.VMEM((count, k), BF16)
    rows_f = lambda k: pltpu.VMEM((count, k), F32)
    scratch += [
        rows_bf(D), rows_bf(D), pltpu.VMEM((4, count, 128), F32), rows_bf(D), rows_bf(D),
        rows_f(D), rows_f(D), rows_f(128), rows_f(128),
        rows_bf(D), rows_bf(D), rows_bf(3 * D),
        pltpu.VMEM((2, len(PAIRS), count // FRAMES, 128), F32),
        rows_bf(D), rows_f(D), rows_bf(FF), rows_bf(FF),
        rows_f(D), rows_bf(3 * D), pltpu.VMEM((2, 2, 4, 2, 16, count), BF16),
    ]
    scratch += [
        pltpu.VMEM((8, 512), F32), pltpu.VMEM((8, 1024), F32), pltpu.VMEM((8, 2048), F32), pltpu.VMEM((1, 3 * D), F32),
        pltpu.VMEM((count // FRAMES, 128), F32), pltpu.VMEM((HALF, 128), BF16), pltpu.VMEM((128, HALF), BF16),
        pltpu.VMEM((8, 512), F32), pltpu.VMEM((8, 1024), F32), pltpu.VMEM((8, 2048), F32),
        pltpu.VMEM((2, 2, 4, 2, 8, 128), F32),
    ]
    scratch += [pltpu.SemaphoreType.DMA((6, n)) for n in (5, 10, 4, 11)]
    scratch += [pltpu.SemaphoreType.DMA((13,)), pltpu.SemaphoreType.DMA((9,))]
    out_shape = [jax.ShapeDtypeStruct(tokens.shape, BF16)] * 2
    out_shape += [jax.ShapeDtypeStruct((PACK_ALL, 128), F32)]

    def body(*refs):
        layer_kernel(split, count, *refs)

    return pl.pallas_call(
        body,
        name="layer",
        out_shape=out_shape,
        in_specs=[any_spec] * 15,
        out_specs=[any_spec] * 3,
        scratch_shapes=scratch,
        compiler_params=pltpu.CompilerParams(
            collective_id=0, has_side_effects=True, vmem_limit_bytes=63 << 20
        ),
        cost_estimate=pl.CostEstimate(
            flops=2 * 3 * count * (3 * D * D + D * D + 2 * D * FF), bytes_accessed=1 << 23, transcendentals=count * FF
        ),
    )(tokens, cotangent, frames, *small, *shards)


def hand_out(mixed, tokens_grad, grads):
    any_spec = pl.BlockSpec(memory_space=pl.ANY)

    def body(mixed_in, tgrad_in, grads_in, *refs):
        outs, smalls, (mixed_v, tgrad_v, grads_v, in_sem, out_sem) = refs[:14], refs[14:22], refs[22:]
        big = (outs[0], outs[1]) + tuple(outs[10:])
        reads = [
            pltpu.make_async_copy(src, dst, in_sem.at[k])
            for k, (src, dst) in enumerate(((mixed_in, mixed_v), (tgrad_in, tgrad_v), (grads_in, grads_v)))
        ]
        parts = [mixed_v, tgrad_v] + [grads_v.at[pl.ds(PACK[k], PACKED[k])] for k in range(4)]
        writes = [pltpu.make_async_copy(src, dst, out_sem.at[k]) for k, (src, dst) in enumerate(zip(parts, big))]
        for k in (2, 0, 1):
            reads[k].start()
        reads[2].wait()
        for copy in writes[2:]:
            copy.start()
        for p, n in enumerate(SMALL):
            smalls[p][...] = grads_v[PACK_SMALL + p : PACK_SMALL + p + 1, 0:n]
            writes.append(pltpu.make_async_copy(smalls[p], outs[2 + p], out_sem.at[6 + p]))
            writes[-1].start()
        for k in range(2):
            reads[k].wait()
            writes[k].start()
        for copy in writes:
            copy.wait()

    row_shapes = [jax.ShapeDtypeStruct(mixed.shape, BF16)] * 2
    small_shapes = [jax.ShapeDtypeStruct((1, n), F32) for n in SMALL]
    shard_shapes = [jax.ShapeDtypeStruct((n, 128), F32) for n in PACKED]
    return pl.pallas_call(
        body,
        name="hand_out",
        out_shape=row_shapes + small_shapes + shard_shapes,
        in_specs=[any_spec] * 3,
        out_specs=[any_spec] * 14,
        scratch_shapes=[pltpu.VMEM((1, n), F32) for n in SMALL]
        + [
            pltpu.VMEM(mixed.shape, BF16), pltpu.VMEM(mixed.shape, BF16), pltpu.VMEM(grads.shape, F32),
            pltpu.SemaphoreType.DMA((3,)), pltpu.SemaphoreType.DMA((14,)),
        ],
    )(mixed, tokens_grad, grads)


def local(split, tokens, frames, g1, b1, wqkv, bqv, wo, bo, g2, b2, w1, b1f, w2, b2f, cotangent):
    spot = lax.axis_index("fsdp") // split

    def block(values):
        if split == 1:
            return values
        n = values.shape[0]
        every = lax.all_gather(values, "fsdp", axis=0, tiled=True)
        return lax.dynamic_slice(every, (spot * split * n,), (split * n,))

    def owned(values):
        if split == 1:
            return values
        n = values.shape[0]
        spread = lax.dynamic_update_slice(jnp.zeros((8 * n,), F32), values, (spot * n,))
        return lax.psum_scatter(spread, "fsdp", scatter_dimension=0, tiled=True)

    small = [block(v).reshape(1, -1) for v in (g1, b1, bqv, bo, g2, b2, b1f, b2f)]
    shards = [block(v).reshape(-1, 128) for v in (wqkv, wo, w1, w2)]
    outs = hand_out(*call_layer(split, tokens, frames.reshape(1, -1), small, shards, cotangent))
    mixed, tokens_grad = outs[:2]
    dg1, db1, dbqv, dbo, dg2, db2, db1f, db2f = [owned(v.reshape(-1)) for v in outs[2:10]]
    dwqkv, dwo, dw1, dw2 = [owned(v.reshape(-1)) for v in outs[10:]]
    return (mixed, tokens_grad, dg1, db1, dwqkv, dbqv, dwo, dbo, dg2, db2, dw1, db1f, dw2, db2f)


def solution(mesh):
    split = mesh.shape["fsdp"] // 8
    flat, rows = P(("dp", "fsdp")), P(("dp", "fsdp"), None)

    def body(*args):
        return local(split, *args)

    return jax.shard_map(
        body,
        mesh=mesh,
        in_specs=(rows,) + (flat,) * 13 + (rows,),
        out_specs=(rows, rows) + (flat,) * 12,
        check_vma=False,
    )
```

```python
import math

import jax
import jax.numpy as jnp
from jax import lax
from jax.experimental import pallas as pl
from jax.experimental.pallas import tpu as pltpu
from jax.sharding import PartitionSpec as P

D = 512
HEADS = 8
HEAD_DIM = 64
FF = 2048
FRAMES = 5
EPSILON = 1e-05
PAIRS = [(t, u) for t in range(FRAMES) for u in range(t + 1)]

F32 = jnp.float32
BF16 = jnp.bfloat16
MESH = pl.DeviceIdType.MESH

SM, QA, QB, OUT, UP, DOWN = range(6)
ROWS = (8, 16, 16, 16, 16, 64)
COLS = (128, 3 * D // 2, 3 * D // 2, D, FF, D)
KEPT = (F32, BF16, BF16, BF16, BF16, BF16)
DIRECT = (SM, QA, QB,)
LARGE = (UP, DOWN)
HALF = D // 2
WIDE = FF // 2
GROUP = HEADS // 2
QKV_ARG, OUT_ARG, UP_ARG, DOWN_ARG = range(4)
ARG = (None, QKV_ARG, QKV_ARG, OUT_ARG, UP_ARG, DOWN_ARG)
PACKED = (192, 64, 256, 256)
PACK = (0, 192, 256, 512)
PACK_SMALL, PACK_ALL = 768, 776
SMALL = (16, 16, 32, 16, 16, 16, 64, 16)
GAIN1, BIAS1, QVB, OUTB, GAIN2, BIAS2, UPB, DOWNB = range(8)

TILE = 192
CHUNK = 64


def dot(left, right):
    return lax.dot_general(left, right, (((1,), (0,)), ((), ())), preferred_element_type=F32)


def dot_nt(left, right):
    return lax.dot_general(left, right, (((1,), (1,)), ((), ())), preferred_element_type=F32)


def dot_tn(left, right):
    return lax.dot_general(left, right, (((0,), (0,)), ((), ())), preferred_element_type=F32)


def iota(shape, dim):
    return lax.broadcasted_iota(jnp.int32, shape, dim)


def fold(values):
    rows, cols = values.shape
    return jnp.sum(values.reshape(rows // 8, 8, cols), axis=0)


def split_two(values):
    high = values.astype(BF16)
    return high, (values - high.astype(F32)).astype(BF16)


def layer_kernel(split, count, *refs):
    refs = list(refs)

    def take(n):
        head = refs[:n]
        del refs[:n]
        return head

    tok_hbm, cot_hbm, frames_hbm = take(3)
    small_hbm = take(8)
    shard_hbm = take(4)
    mixed_hbm, tgrad_hbm, grads_hbm = take(3)
    shard_in = take(4)
    small_in = take(8)
    (frames_in,) = take(1)
    (grads,) = take(1)
    whole = take(6)
    acc = take(6)
    sib_out, sib_in = take(6), take(6)
    two_out, two_in = take(6), take(6)
    one_out, one_in = take(6), take(6)
    zed_out, zed_in = take(6), take(6)
    (tokb, cotb, stage, xt, dm, xh1, xh2, rs1, rs2, a1, a2, qkv, prob, ctx, x1, act, slope, wide, dpre, turned) = take(20)
    (vec16, vecqv, vecup, biasq, living, pick, pick_t, gs16, gsqv, gsup, sums) = take(11)
    (gsend, grecv, grecv_large, rsend, rrecv, rrecv_large, io_sem, small_sem) = take(8)

    dao = cotb

    seqs = count // FRAMES
    dp = lax.axis_index("dp")
    fs = lax.axis_index("fsdp")
    x, c = dp // 2, dp % 2
    group, rest = fs // split, fs % split
    z, y = group // 2, group % 2

    plane = (c + x + y) % 2

    def core_at(x_, y_):
        return (plane + x_ + y_) % 2

    def device(x_, c_, z_, y_):
        return (x_ * 2 + c_, (z_ * 2 + y_) * split + rest)

    first = x + plane * (y - x)
    second = y + plane * (x - y)

    def to_xy(f_, s_):
        return f_ + plane * (s_ - f_), s_ + plane * (f_ - s_)

    def peer(f_, s_):
        x_, y_ = to_xy(f_, s_)
        return device(x_, core_at(x_, y_), z, y_)

    sibling = device(x, 1 - c, z, y)
    first_dev = peer(1 - first, second)
    second_dev = peer(first, 1 - second)
    across_dev = peer(1 - first, 1 - second)
    zeds = (z + 1 - 2 * (z % 2), (z + 2) % 4, 3 - z)
    zed_dev = [device(x, c, zk, y) for zk in zeds]

    barrier = pltpu.get_barrier_semaphore()
    for dev in [sibling, first_dev, second_dev, across_dev] + zed_dev:
        pl.semaphore_signal(barrier, inc=1, device_id=dev, device_id_type=MESH)
    small_copy_in = [pltpu.make_async_copy(small_hbm[p], small_in[p], small_sem.at[p]) for p in range(8)]
    shard_copy = [pltpu.make_async_copy(shard_hbm[k], shard_in[k], io_sem.at[4 + k]) for k in range(4)]
    frames_copy = pltpu.make_async_copy(frames_hbm, frames_in, small_sem.at[8])
    tok_copy = pltpu.make_async_copy(tok_hbm, tokb, io_sem.at[0])
    cot_copy = pltpu.make_async_copy(cot_hbm, cotb, io_sem.at[1])
    for copy in small_copy_in + shard_copy + [tok_copy, frames_copy, cot_copy]:
        copy.start()

    def shard(w, f_, s_, z_):
        x_, y_ = to_xy(f_, s_)
        return whole[w].at[x_, core_at(x_, y_), z_, y_]

    def line(w, f_, s_):
        x_, y_ = to_xy(f_, s_)
        return whole[w].at[x_, core_at(x_, y_), :, y_]

    def gcopy(w, sent, got, ref, dev):
        sent_sem = gsend.at[w, sent]
        got_sem = grecv_large.at[w - UP, got] if w in LARGE else grecv.at[w, got]
        return pltpu.make_async_remote_copy(
            src_ref=ref, dst_ref=ref, send_sem=sent_sem, recv_sem=got_sem, device_id=dev, device_id_type=MESH
        )

    def cols_of(w):
        if w in (QA, QB):
            return [(4 * p + 2 * (w - QA) + b, 2 * p + b) for p in range(3) for b in range(2)]
        return [(k, k) for k in range(COLS[w] // 128)]

    def own_shard(w):
        if w == SM:
            whole[w][x, c, z, y] = jnp.zeros((8, 128), F32)
            for p, n in enumerate(SMALL):
                small_copy_in[p].wait()
                whole[w][x, c, z, y, p : p + 1, 0:n] = small_in[p][...].astype(BF16).astype(F32)
        else:
            if w != QB:
                shard_copy[ARG[w]].wait()
            step = PACKED[ARG[w]] // ROWS[w]
            for k, to in cols_of(w):
                part = shard_in[ARG[w]][pl.ds(k, ROWS[w], stride=step), :]
                whole[w][x, c, z, y, :, to * 128 : (to + 1) * 128] = part.astype(BF16)

    def got_first(w, spot):
        return 6 + spot if w in LARGE else 3

    def got_sibling(w):
        return 10 if w in LARGE else 6

    def hand_on(w, ref, spot):
        gcopy(w, 0, got_first(w, spot), ref, first_dev).start()
        gcopy(w, 0, 4, ref, second_dev).start()
        if w in DIRECT:
            gcopy(w, 0, 5, ref, across_dev).start()

    def to_sibling(w, f_, s_):
        gcopy(w, 1, got_sibling(w), line(w, f_, s_), sibling).start()

    def g_start(w):
        ref = shard(w, first, second, z)
        for k in range(3):
            gcopy(w, 0, k, ref, zed_dev[k]).start()
        hand_on(w, ref, z)

    def g_z(w):
        for k in range(3):
            ref = shard(w, first, second, zeds[k])
            gcopy(w, 0, k, ref, zed_dev[k]).wait_recv()
            hand_on(w, ref, zeds[k])
        to_sibling(w, first, second)

    def g_f(w):
        if w not in LARGE:
            gcopy(w, 0, 3, line(w, 1 - first, second), first_dev).wait_recv()
        for k in range(4):
            ref = shard(w, 1 - first, second, k)
            if w in LARGE:
                gcopy(w, 0, 6 + k, ref, first_dev).wait_recv()
            gcopy(w, 0, 5, ref, second_dev).start()
        to_sibling(w, 1 - first, second)

    def g_s(w):
        if w in DIRECT:
            gcopy(w, 0, 3, line(w, 1 - first, second), first_dev).wait_recv()
            to_sibling(w, 1 - first, second)
        gcopy(w, 0, 4, line(w, first, 1 - second), second_dev).wait_recv()
        to_sibling(w, first, 1 - second)
        gcopy(w, 0, 5, line(w, 1 - first, 1 - second), second_dev).wait_recv()
        to_sibling(w, 1 - first, 1 - second)

    def g_sib(w):
        gcopy(w, 1, got_sibling(w), whole[w].at[:, 1 - c], sibling).wait_recv()

    def g_end(w):
        gcopy(w, 0, 0, sib_out[w].at[pl.ds(0, 15)], sibling).wait_send()
        gcopy(w, 1, 0, sib_out[w], sibling).wait_send()

    def loop(n, body, start=0):
        def step(i, carry):
            body(i)
            return carry

        lax.fori_loop(start, n, step, 0)

    def place(f_, s_, z_):
        x_, y_ = to_xy(f_, s_)
        return x_ * 8 + z_ * 2 + y_

    def rcopy(w, sent, got, src, dst, dev):
        sent_sem = rsend.at[w, sent]
        got_sem = rrecv_large.at[w - UP, got] if w in LARGE else rrecv.at[w, got]
        return pltpu.make_async_remote_copy(
            src_ref=src, dst_ref=dst, send_sem=sent_sem, recv_sem=got_sem, device_id=dev, device_id_type=MESH
        )

    def sib_copy(w, at, n):
        return rcopy(w, 1, 0, sib_out[w].at[pl.ds(at, n)], sib_in[w].at[pl.ds(at, n)], sibling)

    def two_copy(w, k, got):
        return rcopy(w, 0, got, two_out[w].at[k], two_in[w].at[k], second_dev)

    def one_copy(w, k):
        return rcopy(w, 0, 9 + k if w in LARGE else 3, one_out[w].at[k], one_in[w].at[k], first_dev)

    def zed_copy(w, k):
        return rcopy(w, 0, 4, zed_out[w].at[k], zed_in[w].at[k], zed_dev[k])

    def four_of(w, at):
        return two_in[w].at[pl.ds(at, 4)]

    def chip_sum(w, j):
        return acc[w][j] + sib_in[w][j].astype(F32)

    def r_1(w):
        sib_copy(w, 0, 16).wait_recv()
        if w == SM:
            for k in range(4):
                one_out[w][k] = chip_sum(w, place(1 - first, second, k))
                one_copy(w, k).start()
                two_out[w][k] = chip_sum(w, place(first, 1 - second, k))
                two_copy(w, k, 2).start()
                two_out[w][4 + k] = chip_sum(w, place(1 - first, 1 - second, k))
                rcopy(w, 0, 1, two_out[w].at[4 + k], two_in[w].at[4 + k], across_dev).start()
            return

        def step(k, got):
            j = place(k // 4, 1 - second, k % 4)
            two_out[w][k] = chip_sum(w, j).astype(KEPT[w])
            two_copy(w, k, got).start()

        loop(4, lambda i: step(4 * (1 - first) + i, 5 + i if w in LARGE else 1))
        loop(4, lambda i: step(4 * first + i, 2))

    def r_2(w):
        if w not in LARGE:
            part = four_of(w, 4 * (1 - first))
            rcopy(w, 0, 1, part, part, second_dev).wait_recv()

        def step(i):
            k = (z + 1 + i) % 4
            j = place(1 - first, second, k)
            slot = (1 - first) * 4 + k
            if w in LARGE:
                two_copy(w, slot, 5 + k).wait_recv()
            total = chip_sum(w, j) + two_in[w][slot].astype(F32)
            one_out[w][k] = total.astype(KEPT[w])
            one_copy(w, k).start()

        loop(4, step)

    def line_sum(w, k):
        j = place(first, second, k)
        total = chip_sum(w, j) + one_in[w][k].astype(F32)
        if w == SM:
            return total + two_in[w][k] + two_in[w][4 + k]
        return total + two_in[w][4 * first + k].astype(F32)

    def r_3(w):
        if w == SM:
            waits = ((2, 0), (1, 4))
        else:
            waits = ((2, 4 * first),)
        for got, at in waits:
            part = four_of(w, at)
            rcopy(w, 0, got, part, part, second_dev).wait_recv()
        if w not in LARGE:
            rcopy(w, 0, 3, one_in[w], one_in[w], first_dev).wait_recv()
        for k in range(3):
            if w in LARGE:
                one_copy(w, zeds[k]).wait_recv()
            zed_out[w][k] = line_sum(w, zeds[k]).astype(KEPT[w])
            zed_copy(w, k).start()

    def grad_copy(at, rows, k):
        return pltpu.make_async_copy(grads.at[pl.ds(at, rows)], grads_hbm.at[pl.ds(at, rows)], io_sem.at[8 + k])

    def arg_copy(k):
        return grad_copy(PACK[k], PACKED[k], k)

    small_copy = grad_copy(PACK_SMALL, 8, 4)

    def r_4(w):
        if w in LARGE:
            one_copy(w, z).wait_recv()
        total = line_sum(w, z)
        rcopy(w, 0, 4, zed_in[w], zed_in[w], sibling).wait_recv()
        for k in range(3):
            total = total + zed_in[w][k].astype(F32)
        if w == SM:
            grads[PACK_SMALL:PACK_ALL, :] = total
            small_copy.start()
        else:
            step = PACKED[ARG[w]] // ROWS[w]
            for k, at in cols_of(w):
                grads[pl.ds(PACK[ARG[w]] + k, ROWS[w], stride=step), :] = total[:, at * 128 : (at + 1) * 128]

    def r_end(w):
        sib_copy(w, 0, 16).wait_send()
        rcopy(w, 0, 0, sib_out[w].at[pl.ds(0, 15)], sib_in[w].at[pl.ds(0, 15)], sibling).wait_send()

    tiles = count // TILE
    per_frame = seqs // TILE

    def tile_rows(i):
        return pl.ds(pl.multiple_of(i * TILE, TILE), TILE)

    def strided(i):
        return pl.ds(i // per_frame + FRAMES * TILE * (i % per_frame), TILE, stride=FRAMES)

    def widen(src):
        def body(i):
            for h in range(4):
                stage[h, tile_rows(i), :] = src[tile_rows(i), h * 128 : (h + 1) * 128].astype(F32)

        loop(tiles, body)

    def narrow(dst):
        def body(i):
            for h in range(4):
                dst[tile_rows(i), h * 128 : (h + 1) * 128] = stage[h, tile_rows(i), :].astype(BF16)

        loop(tiles, body)

    def center(values):
        mean = jnp.mean(values, axis=-1, keepdims=True)
        centered = values - mean
        root = lax.rsqrt(jnp.mean(centered * centered, axis=-1, keepdims=True) + EPSILON)
        return centered * root, root

    def constants():
        lane, row = iota((HALF, 128), 1), iota((HALF, 128), 0)
        pick[...] = jnp.where((row // HEAD_DIM == lane % GROUP) & (lane < 2 * GROUP), 1.0, 0.0).astype(BF16)
        lane, row = iota((128, HALF), 1), iota((128, HALF), 0)
        pick_t[...] = jnp.where((lane // HEAD_DIM == row % GROUP) & (row < 2 * GROUP), 1.0, 0.0).astype(BF16)
        frames_copy.wait()
        same = iota((seqs, seqs), 0) == iota((seqs, seqs), 1)
        wide_frames = jnp.broadcast_to(frames_in[...].astype(F32), (seqs, seqs))
        spread = jnp.where(same, wide_frames, 0.0).astype(BF16)
        living[...] = dot(spread, jnp.ones((seqs, 128), BF16))
        gs16[...] = jnp.zeros_like(gs16)
        gsqv[...] = jnp.zeros_like(gsqv)
        gsup[...] = jnp.zeros_like(gsup)

    def first_norm():
        widen(tokb)

        def body(i):
            values = jnp.concatenate([stage[h, strided(i), :] for h in range(4)], axis=1)
            xt[tile_rows(i), :] = values.astype(BF16)
            hat, root = center(values)
            xh1[tile_rows(i), :] = hat
            rs1[tile_rows(i), :] = jnp.broadcast_to(root, (TILE, 128))

        loop(tiles, body)

    def cotangent_in():
        widen(cotb)

        def body(i):
            values = jnp.concatenate([stage[h, strided(i), :] for h in range(4)], axis=1)
            dm[tile_rows(i), :] = values.astype(BF16)
            gs16[DOWNB : DOWNB + 1, :] += jnp.sum(fold(values), axis=0, keepdims=True)

        loop(tiles, body)

    def small_vectors():
        raw = whole[SM][...].reshape(256, 128).astype(BF16)
        for n, dst in ((16, vec16), (32, vecqv), (64, vecup)):
            width = 32 * n
            for at in range(0, width, 512):
                near = iota((128, 512), 0) == (iota((128, 512), 1) + at) % n
                spread = dot(raw, jnp.where(near, 1.0, 0.0).astype(BF16))
                mine = iota((256, 512), 0) // 8 == (iota((256, 512), 1) + at) // n
                dst[:, at : at + 512] = jnp.sum(jnp.where(mine, spread, 0.0).reshape(32, 8, 512), axis=0)
        biasq[...] = jnp.zeros_like(biasq)
        for h in range(2):
            for part in range(2):
                at = 3 * HALF * h + 2 * HALF * part
                biasq[:, at : at + HALF] = vecqv[QVB : QVB + 1, part * D + h * HALF : part * D + (h + 1) * HALF]

    def small_grads():
        for n, src in ((16, gs16), (32, gsqv), (64, gsup)):
            width = 32 * n
            for at in range(0, width, 512):
                mine = iota((256, 512), 0) // 8 == (iota((256, 512), 1) + at) // n
                values = jnp.broadcast_to(src[:, at : at + 512][None], (32, 8, 512)).reshape(256, 512)
                high, low = split_two(jnp.where(mine, values, 0.0))
                near = jnp.where(iota((128, 512), 0) == (iota((128, 512), 1) + at) % n, 1.0, 0.0).astype(BF16)
                part = dot_nt(high, near) + dot_nt(low, near)
                total = part if n == 16 and at == 0 else total + part
        sums[...] = total.reshape(2, 2, 4, 2, 8, 128)
        for h in range(2):
            for q in range(2):
                for own in range(2):
                    part = sums[h, core_at(h, q) if own else 1 - core_at(h, q), :, q]
                    for k in range(4):
                        (acc if own else sib_out)[SM][8 * h + 2 * k + q] = part[k]
            sib_copy(SM, 8 * h, 8).start()

    def first_affine():
        gain, bias = vec16[GAIN1 : GAIN1 + 1, :], vec16[BIAS1 : BIAS1 + 1, :]

        def body(i):
            a1[tile_rows(i), :] = (xh1[tile_rows(i), :] * gain + bias).astype(BF16)

        loop(tiles, body)

    def cols(n, width):
        return pl.ds(pl.multiple_of(n * width, width), width)

    def matrix_cols(w, n, width):
        return whole[w][:, :, :, :, :, cols(n, width)].reshape(32 * ROWS[w], width)

    def matrix(w):
        return whole[w][...].reshape(32 * ROWS[w], COLS[w])

    def project_in(h):
        at = slice(3 * HALF * h, 3 * HALF * (h + 1))
        r = dot(a1[...], matrix(QA + h)) + biasq[:, at]
        qkv[:, at] = r.astype(BF16)

    def frame_rows(t, i):
        return pl.ds(pl.multiple_of(t * seqs + i * CHUNK, CHUNK), CHUNK)

    def heads_of(h, i, part):
        at = (3 * h + part) * HALF
        return [qkv[frame_rows(t, i), at : at + HALF].astype(F32) for t in range(FRAMES)]

    def spread_heads(parts):
        lanes = iota((CHUNK, 128), 1)
        mixed_parts = []
        for part in parts:
            high, low = split_two(part)
            mixed_parts.append(jnp.where(lanes < GROUP, high.astype(F32), low.astype(F32)).astype(BF16))
        return dot(jnp.concatenate(mixed_parts, axis=0), pick_t[...])

    def rows_of(values, k):
        return values[k * CHUNK : (k + 1) * CHUNK]

    def attention(h, i):
        q, k_, v = heads_of(h, i, 0), heads_of(h, i, 1), heads_of(h, i, 2)
        halves = [split_two(q[t] * k_[u]) for t, u in PAIRS]
        high = jnp.concatenate([h for h, _ in halves], axis=0)
        low = jnp.concatenate([l for _, l in halves], axis=0)
        scores = (dot(high, pick[...]) + dot(low, pick[...])) * (1.0 / math.sqrt(HEAD_DIM))
        live = living[pl.ds(pl.multiple_of(i * CHUNK, CHUNK), CHUNK), :]
        weights = []
        for t in range(FRAMES):
            row = [rows_of(scores, PAIRS.index((t, u))) for u in range(t + 1)]
            row = [jnp.where(u < live, part, -1e30) for u, part in enumerate(row)]
            top = row[0]
            for part in row[1:]:
                top = jnp.maximum(top, part)
            row = [jnp.exp(part - top) for part in row]
            total = row[0]
            for part in row[1:]:
                total = total + part
            weights += [part / total for part in row]
        for k, part in enumerate(weights):
            prob[h, k, pl.ds(pl.multiple_of(i * CHUNK, CHUNK), CHUNK), :] = part
        spread = spread_heads(weights)
        for t in range(FRAMES):
            total = rows_of(spread, PAIRS.index((t, 0))) * v[0]
            for u in range(1, t + 1):
                total = total + rows_of(spread, PAIRS.index((t, u))) * v[u]
            ctx[frame_rows(t, i), h * HALF : (h + 1) * HALF] = total.astype(BF16)

    def attention_back(h, i):
        v = heads_of(h, i, 2)
        g = [wide[frame_rows(t, i), h * HALF : (h + 1) * HALF] for t in range(FRAMES)]
        base = 3 * HALF * h
        products = jnp.concatenate([(g[t] * v[u]).astype(BF16) for t, u in PAIRS], axis=0)
        slopes = dot(products, pick[...])
        weights = [prob[h, k, pl.ds(pl.multiple_of(i * CHUNK, CHUNK), CHUNK), :] for k in range(len(PAIRS))]
        scaled = []
        for t in range(FRAMES):
            ks = [PAIRS.index((t, u)) for u in range(t + 1)]
            mean = weights[ks[0]] * rows_of(slopes, ks[0])
            for k in ks[1:]:
                mean = mean + weights[k] * rows_of(slopes, k)
            scaled += [weights[k] * (rows_of(slopes, k) - mean) * (1.0 / math.sqrt(HEAD_DIM)) for k in ks]
        spread_p = spread_heads(weights)
        for u in range(FRAMES):
            total = None
            for t in range(u, FRAMES):
                part = rows_of(spread_p, PAIRS.index((t, u))) * g[t]
                total = part if total is None else total + part
            low = total.astype(BF16)
            dpre[frame_rows(u, i), base + 2 * HALF : base + 3 * HALF] = low
            gsqv[QVB : QVB + 1, D + h * HALF : D + (h + 1) * HALF] += jnp.sum(fold(low.astype(F32)), axis=0, keepdims=True)
        q, k_ = heads_of(h, i, 0), heads_of(h, i, 1)
        spread_s = spread_heads(scaled)
        for t in range(FRAMES):
            total = None
            for u in range(t + 1):
                part = rows_of(spread_s, PAIRS.index((t, u))) * k_[u]
                total = part if total is None else total + part
            low = total.astype(BF16)
            dpre[frame_rows(t, i), base : base + HALF] = low
            gsqv[QVB : QVB + 1, h * HALF : (h + 1) * HALF] += jnp.sum(fold(low.astype(F32)), axis=0, keepdims=True)
        for u in range(FRAMES):
            total = None
            for t in range(u, FRAMES):
                part = rows_of(spread_s, PAIRS.index((t, u))) * q[t]
                total = part if total is None else total + part
            dpre[frame_rows(u, i), base + HALF : base + 2 * HALF] = total.astype(BF16)

    def project_out():
        bias = vec16[OUTB : OUTB + 1, :]
        for n in range(2):
            at = slice(n * 256, (n + 1) * 256)
            r = dot(ctx[...], whole[OUT][:, :, :, :, :, at].reshape(D, 256))
            x1[:, at] = xt[:, at].astype(F32) + r + bias[:, at]

    def second_norm(start, stop):
        gain, bias = vec16[GAIN2 : GAIN2 + 1, :], vec16[BIAS2 : BIAS2 + 1, :]

        def body(i):
            hat, root = center(x1[tile_rows(i), :])
            xh2[tile_rows(i), :] = hat
            rs2[tile_rows(i), :] = jnp.broadcast_to(root, (TILE, 128))
            a2[tile_rows(i), :] = (hat * gain + bias).astype(BF16)

        loop(stop, body, start)

    def feed_up(start, stop):
        k0 = math.sqrt(2.0 / math.pi)
        k1 = k0 * 0.044715

        def body(n):
            f = dot(a2[...], matrix_cols(UP, n, WIDE)) + vecup[UPB : UPB + 1, cols(n, WIDE)]
            square = f * f
            half = 0.5 + 0.5 * jnp.tanh(f * (k0 + k1 * square))
            act[:, cols(n, WIDE)] = (f * half).astype(BF16)
            grow = half + (f * (half - half * half)) * (2.0 * k0 + 6.0 * k1 * square)
            slope[:, cols(n, WIDE)] = grow.astype(BF16)

        loop(stop, body, start)

    def feed_down(n):
        bias = vec16[DOWNB : DOWNB + 1, :]
        at = slice(n * 256, (n + 1) * 256)
        r = dot(act[...], whole[DOWN][:, :, :, :, :, at].reshape(FF, 256))
        r = r + x1[:, at] + bias[:, at]
        for t in range(FRAMES):
            for h in range(2):
                stage[2 * n + h, pl.ds(t, seqs, stride=FRAMES), :] = r[t * seqs : (t + 1) * seqs, h * 128 : (h + 1) * 128]

    def turn(left):
        for h in range(2):
            for k in range(2):
                at = h * 256 + k * 128
                part = jnp.transpose(left[:, at : at + 128]).reshape(4, 2, 16, count)
                for q in range(2):
                    turned[(k + core_at(h, q) + 1) % 2, h, :, q] = part[:, q]

    def weight_grad(w, right, base, n, width):
        at = slice(n * width, (n + 1) * width)
        r = dot(turned[...].reshape(D, count), right[:, base + n * width : base + (n + 1) * width])
        sib_out[w][:, :, at] = r[:HALF].reshape(16, ROWS[w], width).astype(BF16)
        rcopy(w, 1, 0, sib_out[w].at[:, :, at], sib_in[w].at[:, :, at], sibling).start()
        acc[w][:, :, at] = r[HALF:].reshape(16, ROWS[w], width)

    def act_of(h, own):
        core = core_at(h, 0) if own else 1 - core_at(h, 0)
        even = act[:, pl.ds(pl.multiple_of(h * 1024 + core * 512, 512), 512)]
        odd = act[:, pl.ds(pl.multiple_of(h * 1024 + (1 - core) * 512, 512), 512)]
        return jnp.where(iota((count, 512), 1) % 128 < 64, even, odd)

    def down_theirs(h):
        r = dot_tn(act_of(h, False), dm[...])
        sib_out[DOWN][8 * h : 8 * h + 8] = r.reshape(8, 64, D).astype(BF16)
        sib_copy(DOWN, 8 * h, 8).start()

    def down_ours(h):
        acc[DOWN][8 * h : 8 * h + 8] = dot_tn(act_of(h, True), dm[...]).reshape(8, 64, D)

    def feed_back(start, stop):
        def body(n):
            part = whole[DOWN][n].reshape(WIDE, D)
            low = (dot_nt(dm[...], part) * slope[:, cols(n, WIDE)].astype(F32)).astype(BF16)
            slope[:, cols(n, WIDE)] = low
            gsup[UPB : UPB + 1, cols(n, WIDE)] = jnp.sum(fold(low.astype(F32)), axis=0, keepdims=True)

        loop(stop, body, start)

    def back_to(left, w, h):
        wide[:, h * 256 : (h + 1) * 256] = dot_nt(left[...], whole[w][h].reshape(256, COLS[w]))

    def back_in(h):
        r = dot_nt(dpre[:, : 3 * HALF], whole[QA][h].reshape(256, 3 * HALF))
        r = r + dot_nt(dpre[:, 3 * HALF :], whole[QB][h].reshape(256, 3 * HALF))
        wide[:, h * 256 : (h + 1) * 256] = r

    def norm_back(grads, hat, root, gain, gain_at, bias_at):
        gs16[gain_at : gain_at + 1, :] += jnp.sum(fold(grads * hat), axis=0, keepdims=True)
        gs16[bias_at : bias_at + 1, :] += jnp.sum(fold(grads), axis=0, keepdims=True)
        scaled = grads * gain
        mean = jnp.mean(scaled, axis=-1, keepdims=True)
        along = jnp.mean(scaled * hat, axis=-1, keepdims=True)
        return (scaled - mean - hat * along) * root

    def second_back(start, stop):
        gain = vec16[GAIN2 : GAIN2 + 1, :]

        def body(i):
            at = tile_rows(i)
            part = norm_back(wide[at, :], xh2[at, :], rs2[at, 0:1], gain, GAIN2, BIAS2)
            total = dm[at, :].astype(F32) + part
            xh2[at, :] = total
            low = total.astype(BF16)
            dao[at, :] = low
            gs16[OUTB : OUTB + 1, :] += jnp.sum(fold(low.astype(F32)), axis=0, keepdims=True)

        loop(stop, body, start)

    def first_back():
        gain = vec16[GAIN1 : GAIN1 + 1, :]

        def body(i):
            at = tile_rows(i)
            part = norm_back(wide[at, :], xh1[at, :], rs1[at, 0:1], gain, GAIN1, BIAS1)
            stage_part = xh2[at, :] + part
            for h in range(4):
                stage[h, strided(i), :] = stage_part[:, h * 128 : (h + 1) * 128]

        loop(tiles, body)
        narrow(cotb)

    own_shard(QA)
    own_shard(QB)
    own_shard(SM)
    own_shard(OUT)
    own_shard(UP)
    own_shard(DOWN)
    pl.semaphore_wait(barrier, 7)
    g_start(SM)
    g_start(OUT)
    g_start(QB)
    g_start(UP)
    tok_copy.wait()
    first_norm()
    g_start(QA)
    constants()
    g_start(DOWN)
    g_z(OUT)
    g_z(QB)
    g_z(SM)
    g_z(UP)
    g_s(QB)
    g_s(SM)
    cot_copy.wait()
    cotangent_in()
    g_z(QA)
    g_sib(SM)
    small_vectors()
    g_sib(QB)
    g_f(OUT)
    first_affine()
    g_f(UP)
    project_in(1)
    loop(2, lambda i: attention(1, i), 0)
    g_s(QA)
    g_z(DOWN)
    loop(3, lambda i: attention(1, i), 2)
    g_s(OUT)
    g_sib(QA)
    project_in(0)
    loop(3, lambda i: attention(0, i), 0)
    g_s(UP)
    g_sib(OUT)
    project_out()
    second_norm(0, 5)
    g_f(DOWN)
    g_sib(UP)
    feed_up(0, 1)
    down_ours(0)
    down_theirs(0)
    feed_up(1, 2)
    g_s(DOWN)
    down_theirs(1)
    down_ours(1)
    g_sib(DOWN)
    feed_back(0, 1)
    r_1(DOWN)
    feed_back(1, 2)
    turn(a2)
    weight_grad(UP, slope, 0, 0, WIDE)
    turn(a2)
    weight_grad(UP, slope, 0, 1, WIDE)
    r_2(DOWN)
    back_to(slope, UP, 0)
    back_to(slope, UP, 1)
    second_back(0, 2)
    r_1(UP)
    second_back(2, 5)
    back_to(dao, OUT, 0)
    back_to(dao, OUT, 1)
    loop(3, lambda i: attention_back(0, i), 0)
    turn(a1)
    weight_grad(QA, dpre, 0, 0, 3 * HALF)
    r_3(DOWN)
    r_2(UP)
    loop(3, lambda i: attention_back(1, i), 0)
    r_1(QA)
    turn(ctx)
    weight_grad(OUT, dao, 0, 0, D)
    turn(a1)
    weight_grad(QB, dpre, 3 * HALF, 0, 3 * HALF)
    r_3(UP)
    r_1(OUT)
    back_in(0)
    back_in(1)
    r_2(QA)
    r_1(QB)
    first_back()
    tgrad_copy = pltpu.make_async_copy(cotb, tgrad_hbm, io_sem.at[3])
    tgrad_copy.start()
    r_2(OUT)
    small_grads()
    r_3(QA)
    r_2(QB)
    r_1(SM)
    r_3(OUT)
    r_3(QB)
    r_3(SM)
    r_4(DOWN)
    arg_copy(DOWN_ARG).start()
    feed_down(0)
    for w in (SM, QA, QB, OUT, UP, DOWN):
        g_end(w)
    r_4(QA)
    r_4(UP)
    arg_copy(UP_ARG).start()
    r_4(OUT)
    arg_copy(OUT_ARG).start()
    feed_down(1)
    narrow(tokb)
    mixed_copy = pltpu.make_async_copy(tokb, mixed_hbm, io_sem.at[2])
    mixed_copy.start()
    r_4(QB)
    arg_copy(QKV_ARG).start()
    for w in (SM, QA, QB, OUT, UP, DOWN):
        r_end(w)
    r_4(SM)
    for k in range(4):
        arg_copy(k).wait()
    small_copy.wait()
    mixed_copy.wait()
    tgrad_copy.wait()


def call_layer(split, tokens, frames, small, shards, cotangent):
    count = tokens.shape[0]
    any_spec = pl.BlockSpec(memory_space=pl.ANY)

    def kept(n, dtype=None):
        return [pltpu.VMEM((n, r, k), dtype or t) for r, k, t in zip(ROWS, COLS, KEPT)]

    scratch = [pltpu.VMEM((n, 128), F32) for n in PACKED]
    scratch += [pltpu.VMEM((1, n), F32) for n in SMALL] + [pltpu.VMEM((1, count // FRAMES), jnp.int32)]
    scratch += [pltpu.VMEM((PACK_ALL, 128), F32)]
    scratch += [pltpu.VMEM((2, 2, 4, 2, r, k), t) for r, k, t in zip(ROWS, COLS, KEPT)]
    scratch += kept(16, F32)
    for n in (16, 8, 4, 3):
        scratch += kept(n) + kept(n)
    rows_bf = lambda k: pltpu.VMEM((count, k), BF16)
    rows_f = lambda k: pltpu.VMEM((count, k), F32)
    scratch += [
        rows_bf(D), rows_bf(D), pltpu.VMEM((4, count, 128), F32), rows_bf(D), rows_bf(D),
        rows_f(D), rows_f(D), rows_f(128), rows_f(128),
        rows_bf(D), rows_bf(D), rows_bf(3 * D),
        pltpu.VMEM((2, len(PAIRS), count // FRAMES, 128), F32),
        rows_bf(D), rows_f(D), rows_bf(FF), rows_bf(FF),
        rows_f(D), rows_bf(3 * D), pltpu.VMEM((2, 2, 4, 2, 16, count), BF16),
    ]
    scratch += [
        pltpu.VMEM((8, 512), F32), pltpu.VMEM((8, 1024), F32), pltpu.VMEM((8, 2048), F32), pltpu.VMEM((1, 3 * D), F32),
        pltpu.VMEM((count // FRAMES, 128), F32), pltpu.VMEM((HALF, 128), BF16), pltpu.VMEM((128, HALF), BF16),
        pltpu.VMEM((8, 512), F32), pltpu.VMEM((8, 1024), F32), pltpu.VMEM((8, 2048), F32),
        pltpu.VMEM((2, 2, 4, 2, 8, 128), F32),
    ]
    scratch += [pltpu.SemaphoreType.DMA(shape) for shape in ((6, 2), (4, 7), (2, 11), (6, 2), (4, 5), (2, 13))]
    scratch += [pltpu.SemaphoreType.DMA((13,)), pltpu.SemaphoreType.DMA((9,))]
    out_shape = [jax.ShapeDtypeStruct(tokens.shape, BF16)] * 2
    out_shape += [jax.ShapeDtypeStruct((PACK_ALL, 128), F32)]

    def body(*refs):
        layer_kernel(split, count, *refs)

    return pl.pallas_call(
        body,
        name="layer",
        out_shape=out_shape,
        in_specs=[any_spec] * 15,
        out_specs=[any_spec] * 3,
        scratch_shapes=scratch,
        compiler_params=pltpu.CompilerParams(
            collective_id=0, has_side_effects=True, vmem_limit_bytes=63 << 20
        ),
        cost_estimate=pl.CostEstimate(
            flops=2 * 3 * count * (3 * D * D + D * D + 2 * D * FF), bytes_accessed=1 << 23, transcendentals=count * FF
        ),
    )(tokens, cotangent, frames, *small, *shards)


def hand_out(mixed, tokens_grad, grads):
    any_spec = pl.BlockSpec(memory_space=pl.ANY)

    def body(mixed_in, tgrad_in, grads_in, *refs):
        outs, smalls, (mixed_v, tgrad_v, grads_v, in_sem, out_sem) = refs[:14], refs[14:22], refs[22:]
        big = (outs[0], outs[1]) + tuple(outs[10:])
        reads = [
            pltpu.make_async_copy(src, dst, in_sem.at[k])
            for k, (src, dst) in enumerate(((mixed_in, mixed_v), (tgrad_in, tgrad_v), (grads_in, grads_v)))
        ]
        parts = [mixed_v, tgrad_v] + [grads_v.at[pl.ds(PACK[k], PACKED[k])] for k in range(4)]
        writes = [pltpu.make_async_copy(src, dst, out_sem.at[k]) for k, (src, dst) in enumerate(zip(parts, big))]
        for k in (2, 0, 1):
            reads[k].start()
        reads[2].wait()
        for copy in writes[2:]:
            copy.start()
        for p, n in enumerate(SMALL):
            smalls[p][...] = grads_v[PACK_SMALL + p : PACK_SMALL + p + 1, 0:n]
            writes.append(pltpu.make_async_copy(smalls[p], outs[2 + p], out_sem.at[6 + p]))
            writes[-1].start()
        for k in range(2):
            reads[k].wait()
            writes[k].start()
        for copy in writes:
            copy.wait()

    row_shapes = [jax.ShapeDtypeStruct(mixed.shape, BF16)] * 2
    small_shapes = [jax.ShapeDtypeStruct((1, n), F32) for n in SMALL]
    shard_shapes = [jax.ShapeDtypeStruct((n, 128), F32) for n in PACKED]
    return pl.pallas_call(
        body,
        name="hand_out",
        out_shape=row_shapes + small_shapes + shard_shapes,
        in_specs=[any_spec] * 3,
        out_specs=[any_spec] * 14,
        scratch_shapes=[pltpu.VMEM((1, n), F32) for n in SMALL]
        + [
            pltpu.VMEM(mixed.shape, BF16), pltpu.VMEM(mixed.shape, BF16), pltpu.VMEM(grads.shape, F32),
            pltpu.SemaphoreType.DMA((3,)), pltpu.SemaphoreType.DMA((14,)),
        ],
    )(mixed, tokens_grad, grads)


def local(split, tokens, frames, g1, b1, wqkv, bqv, wo, bo, g2, b2, w1, b1f, w2, b2f, cotangent):
    spot = lax.axis_index("fsdp") // split

    def block(values):
        if split == 1:
            return values
        n = values.shape[0]
        every = lax.all_gather(values, "fsdp", axis=0, tiled=True)
        return lax.dynamic_slice(every, (spot * split * n,), (split * n,))

    def owned(values):
        if split == 1:
            return values
        n = values.shape[0]
        spread = lax.dynamic_update_slice(jnp.zeros((8 * n,), F32), values, (spot * n,))
        return lax.psum_scatter(spread, "fsdp", scatter_dimension=0, tiled=True)

    small = [block(v).reshape(1, -1) for v in (g1, b1, bqv, bo, g2, b2, b1f, b2f)]
    shards = [block(v).reshape(-1, 128) for v in (wqkv, wo, w1, w2)]
    outs = hand_out(*call_layer(split, tokens, frames.reshape(1, -1), small, shards, cotangent))
    mixed, tokens_grad = outs[:2]
    dg1, db1, dbqv, dbo, dg2, db2, db1f, db2f = [owned(v.reshape(-1)) for v in outs[2:10]]
    dwqkv, dwo, dw1, dw2 = [owned(v.reshape(-1)) for v in outs[10:]]
    return (mixed, tokens_grad, dg1, db1, dwqkv, dbqv, dwo, dbo, dg2, db2, dw1, db1f, dw2, db2f)


def solution(mesh):
    split = mesh.shape["fsdp"] // 8
    flat, rows = P(("dp", "fsdp")), P(("dp", "fsdp"), None)

    def body(*args):
        return local(split, *args)

    return jax.shard_map(
        body,
        mesh=mesh,
        in_specs=(rows,) + (flat,) * 13 + (rows,),
        out_specs=(rows, rows) + (flat,) * 12,
        check_vma=False,
    )
```
